32 devices in a mesh: grp: 4 (over z), dp: 2 (over y), width: 4 (over x, core).
Axes of the slice: x: 2, y: 2, z: 4, core: 2. Of those that a mesh axis runs over, the one named last changes fastest.
Arguments:
- query_out: bfloat16 [512, 8192], P(None, ('grp', 'dp')), may hold values from -0.09375 to 0.09375
- query_in: bfloat16 [512, 14336], P(None, 'width'), may hold values from -0.046875 to 0.046875
- eigen_out: bfloat16 [8192, 8192], P(('grp', 'dp'), 'width'), may hold values from -0.0625 to 0.0625
- eigen_in: bfloat16 [14336, 14336], P('width', ('grp', 'dp')), may hold values from -0.046875 to 0.046875
- eigvals: float32 [8192, 14336], P('width', ('grp', 'dp')), may hold values from 0.001 to 5
- start: bfloat16 [14336, 256], P(('grp', 'dp')), may hold values from -6 to 6
- grads_out: bfloat16 [4096, 8192], P(('grp', 'dp'), 'width'), may hold values from -0.0625 to 0.0625
- gate_pre: bfloat16 [4096, 14336], P(('grp', 'dp'), 'width'), may hold values from -6 to 6
- up_pre: bfloat16 [4096, 14336], P(('grp', 'dp'), 'width'), may hold values from -0.046875 to 0.046875
Outputs:
- scores: float32 [16, 4096], P(None, ('grp', 'dp', 'width'))
- out_factor: bfloat16 [8192, 256], P('width')
- in_factor: bfloat16 [14336, 256], P('width')
The draws below stay inside these ranges and needn't reach their ends.
All inputs are finite; a program needn't handle non-finite values.
Results may differ from the reference program's by a relative error of at most 0.0095.
Values may be sent and summed in bfloat16 or wider, within the bound.
No kernel may reach another device: no remote copies, remote signals or barrier semaphores. Data moves between devices by JAX's collectives and lax.ppermute only.
A program may use at most 256 MiB of HBM per device.

```python
import jax
import jax.numpy as jnp
from jax import lax

D = 8192
FF = 14336
NQ = 16
QTOK = 32
RANK = 16
ITERS = 2
KQ = 512
TOKENS = 4096
N_GRP = 4
N_DP = 2


def draw_eigvals(key, part):
    block_count = N_GRP * N_DP
    width_block = FF // block_count
    chosen_block = jax.random.randint(jax.random.fold_in(key, 7), (), 0, block_count)
    uniform_draw = jax.random.uniform(jax.random.fold_in(key, 11), (D, FF), jnp.float32)
    base_values = 0.05 * 100.0 ** uniform_draw
    column_block = jnp.arange(FF) // width_block
    scale_factor = jnp.where(column_block == chosen_block, 0.02, 1.0).astype(jnp.float32)
    return base_values * scale_factor[None, :]


def spiked(entries, key, source, target, shards_of, factor):
    owner, partner = [(jnp.arange(entries.shape[position]) // (entries.shape[position] // shards_of)).reshape([-1 if axis == position else 1 for axis in range(entries.ndim)]) for position in (source, target)]
    chosen = jax.random.permutation(key, shards_of)[partner]
    strong = (owner == chosen) | (owner == (partner + shards_of // 2) % shards_of)
    return jnp.where(strong, factor * entries, entries)


def block_levels(own_key, shape, split, smallest, top_value):
    level, own = 1.0, jax.random.fold_in(own_key, 6)
    for position, shards_of in split:
        draws = jnp.exp(jax.random.uniform(jax.random.fold_in(own, position), (shards_of,), jnp.float32, smallest / len(split), top_value / len(split)))
        level = level * jnp.repeat(draws, shape[position] // shards_of).reshape([-1 if axis == position else 1 for axis in range(len(shape))])
    return level


def bell_draw(key, dims, spread, reach, pieces=(), kind=jnp.bfloat16):
    gain = block_levels(key, dims, pieces, -0.22, 0.18) if pieces else 1.0
    entries = jax.random.normal(key, dims, jnp.float32) * spread * gain
    return jnp.minimum(jnp.maximum(entries, -reach), reach).astype(kind)


def noise_with(stream_key, shape, deviation, bound, pieces, heavy, kind=jnp.bfloat16):
    array = deviation * jax.random.normal(stream_key, shape, jnp.float32)
    if pieces:
        array = array * block_levels(stream_key, shape, pieces, -0.22, 0.18)
    return jnp.clip(spiked(array, jax.random.fold_in(stream_key, 3), *heavy), -bound, bound).astype(kind)


def setup_inputs(seed: int = 0) -> dict:
    streams_of = jax.random.split(jax.random.key(seed), 10)
    query_out = noise_with(streams_of[0], (KQ, D), D ** -0.5, 0.09375, ((1, 8),), (1, 0, 8, 2.0))
    query_in = bell_draw(streams_of[1], (KQ, FF), FF ** -0.5, 0.046875, ((1, 4),))
    eigen_out = bell_draw(streams_of[2], (D, D), D ** -0.5, 0.0625, ((0, 8), (1, 4)))
    eigen_in = bell_draw(streams_of[3], (FF, FF), FF ** -0.5, 0.046875, ((0, 4), (1, 8)))
    eigvals = draw_eigvals(jax.random.fold_in(streams_of[9], 71), 0)
    start = bell_draw(streams_of[5], (FF, NQ * RANK), 1.0, 6.0, ((0, 8),))
    grads_out = bell_draw(streams_of[6], (TOKENS, D), D ** -0.5, 0.0625, ((0, 8), (1, 4)))
    gate_pre = bell_draw(streams_of[7], (TOKENS, FF), 1.0, 6.0, ((0, 8), (1, 4)))
    up_pre = bell_draw(streams_of[8], (TOKENS, FF), FF ** -0.5, 0.046875, ((0, 8), (1, 4)))
    return {"query_out": query_out, "query_in": query_in, "eigen_out": eigen_out, "eigen_in": eigen_in, "eigvals": eigvals, "start": start, "grads_out": grads_out, "gate_pre": gate_pre, "up_pre": up_pre}


damping = 0.01
ridge_scale = 1e-06

def reference(query_out, query_in, eigen_out, eigen_in, eigvals, start, grads_out, gate_pre, up_pre):
    rot_out = jnp.dot(query_out.astype(jnp.float32), eigen_out.astype(jnp.float32), preferred_element_type=jnp.float32).astype(jnp.bfloat16)
    rot_in = jnp.dot(query_in.astype(jnp.float32), eigen_in.astype(jnp.float32), preferred_element_type=jnp.float32).astype(jnp.bfloat16)
    rot_out = rot_out.reshape(NQ, QTOK, D)
    rot_in = rot_in.reshape(NQ, QTOK, FF)
    start_cols = start.reshape(FF, NQ, RANK).transpose(1, 0, 2)
    identity = jnp.eye(RANK, dtype=jnp.float32)

    def precondition(operands):
        out_rows, in_rows, basis_in = operands
        rotated = jnp.dot(out_rows.T.astype(jnp.float32), in_rows.astype(jnp.float32), preferred_element_type=jnp.float32)
        rotated = (rotated / (eigvals + damping)).astype(jnp.bfloat16)
        basis_out = None
        for iteration in range(ITERS):
            image_cols = jnp.dot(rotated.astype(jnp.float32), basis_in.astype(jnp.float32), preferred_element_type=jnp.float32)
            gram_mat = jnp.dot(image_cols.T, image_cols, precision=lax.Precision.HIGHEST) / D
            gram_mat = gram_mat + ridge_scale * (jnp.trace(gram_mat) / RANK) * identity
            lower_factor = jnp.linalg.cholesky(gram_mat)
            inverse = jax.scipy.linalg.solve_triangular(lower_factor, identity, lower=True)
            basis_out = jnp.dot(image_cols, inverse.T, precision=lax.Precision.HIGHEST).astype(jnp.bfloat16)
            basis_in = jnp.dot(rotated.T.astype(jnp.float32), basis_out.astype(jnp.float32), preferred_element_type=jnp.float32).astype(jnp.bfloat16)
        return (basis_out, basis_in)
    basis_out, basis_in = lax.map(precondition, (rot_out, rot_in, start_cols))
    out_cols = basis_out.transpose(1, 0, 2).reshape(D, NQ * RANK)
    in_cols = basis_in.transpose(1, 0, 2).reshape(FF, NQ * RANK)
    out_factor = jnp.dot(eigen_out.astype(jnp.float32), out_cols.astype(jnp.float32), preferred_element_type=jnp.float32).astype(jnp.bfloat16)
    in_factor = jnp.dot(eigen_in.astype(jnp.float32), in_cols.astype(jnp.float32), preferred_element_type=jnp.float32).astype(jnp.bfloat16)
    hidden = (jax.nn.silu(gate_pre.astype(jnp.float32)) * up_pre.astype(jnp.float32)).astype(jnp.bfloat16)
    proj_out = jnp.dot(grads_out.astype(jnp.float32), out_factor.astype(jnp.float32), preferred_element_type=jnp.float32)
    proj_in = jnp.dot(hidden.astype(jnp.float32), in_factor.astype(jnp.float32), preferred_element_type=jnp.float32)
    scores = (proj_out * proj_in).reshape(TOKENS, NQ, RANK).sum(axis=2).T
    return (scores, out_factor, in_factor)
```

```python
import jax
import jax.numpy as jnp
from jax import lax
from jax.experimental import pallas as pl
from jax.experimental.pallas import tpu as pltpu
from jax.sharding import PartitionSpec as P

NQ = 16
QTOK = 32
RANK = 16
ITERS = 2

damping = 0.01
ridge_scale = 1e-06

GD = ("grp", "dp")


def inverse_kernel(gram_ref, out_ref):
    gram = gram_ref[...]
    count = gram.shape[0]
    row = lax.broadcasted_iota(jnp.int32, (count, RANK, RANK), 1)
    col = lax.broadcasted_iota(jnp.int32, (count, RANK, RANK), 2)
    eye = jnp.where(row == col, 1.0, 0.0).astype(jnp.float32)
    trace = jnp.sum(jnp.sum(gram * eye, axis=2, keepdims=True), axis=1, keepdims=True)
    left = gram + ridge_scale * (trace / RANK) * eye
    right = eye
    for step in range(RANK):
        pivot = left[:, step : step + 1, step : step + 1]
        factor = jnp.where(row > step, left[:, :, step : step + 1] / pivot, 0.0)
        right = right - factor * right[:, step : step + 1, :]
        left = left - factor * left[:, step : step + 1, :]
    diagonal = jnp.sum(left * eye, axis=2, keepdims=True)
    out_ref[...] = right * lax.rsqrt(diagonal)


def lower_inverse(gram):
    return pl.pallas_call(
        inverse_kernel, out_shape=jax.ShapeDtypeStruct(gram.shape, jnp.float32)
    )(gram)


def sum_scatter(part, axes, count):
    pieces = lax.all_to_all(part.astype(jnp.bfloat16), axes, 0, 0, tiled=True)
    pieces = pieces.reshape((count, part.shape[0] // count) + part.shape[1:])
    return jnp.sum(pieces.astype(jnp.float32), axis=0)


def gather_rows(piece, axes, count):
    copies = jnp.broadcast_to(piece[None], (count,) + piece.shape)
    whole = lax.all_to_all(copies, axes, 0, 0, tiled=True)
    return whole.reshape((count * piece.shape[0],) + piece.shape[1:])


def sum_width(part, count, kind=jnp.bfloat16):
    step = 1
    total = part
    while step < count:
        sent = total.astype(kind)
        got = lax.ppermute(sent, "width", [(i, i ^ step) for i in range(count)])
        total = sent.astype(jnp.float32) + got.astype(jnp.float32)
        step *= 2
    return total


def sum_width_small(part, count):
    total = part
    for step in range(1, count):
        total = total + lax.ppermute(part, "width", [(i, i ^ step) for i in range(count)])
    return total


def make_per_device(n_gd, n_width):
    def per_device(
        query_out, query_in, eigen_out, eigen_in, eigvals, start, grads_out, gate_pre, up_pre
    ):
        D = eigen_out.shape[0] * n_gd
        part_out = jnp.dot(query_out, eigen_out, preferred_element_type=jnp.float32)
        part_in = jnp.dot(query_in, eigen_in, preferred_element_type=jnp.float32)
        rot_in = sum_width(part_in, n_width).astype(jnp.bfloat16)
        share_out = sum_scatter(part_out, GD, n_gd).astype(jnp.bfloat16)
        rot_out = gather_rows(share_out, GD, n_gd)
        rows_out = rot_out.shape[1]
        cols_in = rot_in.shape[1]
        rotated = jnp.einsum(
            "qkd,qkf->qdf",
            rot_out.reshape(NQ, QTOK, rows_out),
            rot_in.reshape(NQ, QTOK, cols_in),
            preferred_element_type=jnp.float32,
        )
        weight = 1.0 / (eigvals + damping)
        rotated = (rotated * weight).astype(jnp.bfloat16)
        basis_in = start.reshape(cols_in, NQ, RANK)
        basis_out = None
        for iteration in range(ITERS):
            image = jnp.einsum(
                "qdf,fqr->dqr", rotated, basis_in, preferred_element_type=jnp.float32
            ).reshape(rows_out, NQ * RANK)
            image = sum_scatter(image, GD, n_gd).astype(jnp.bfloat16)
            image = gather_rows(image, GD, n_gd).reshape(rows_out, NQ, RANK)
            gram = (
                jnp.einsum("dqr,dqs->qrs", image, image, preferred_element_type=jnp.float32) / D
            )
            inverse = lower_inverse(sum_width_small(gram, n_width))
            basis_out = jnp.einsum(
                "dqr,qsr->dqs",
                image.astype(jnp.float32),
                inverse,
                precision=lax.Precision.HIGHEST,
            ).astype(jnp.bfloat16)
            returned = jnp.einsum(
                "qdf,dqr->fqr", rotated, basis_out, preferred_element_type=jnp.float32
            ).reshape(cols_in, NQ * RANK)
            basis_in = (
                sum_width(returned, n_width).astype(jnp.bfloat16).reshape(cols_in, NQ, RANK)
            )
        out_cols = basis_out.reshape(rows_out, NQ * RANK)
        in_cols = basis_in.reshape(cols_in, NQ * RANK)
        part_factor_out = jnp.dot(eigen_out, out_cols, preferred_element_type=jnp.float32)
        share = sum_scatter(part_factor_out, "width", n_width).astype(jnp.bfloat16)
        piece_rows = share.shape[0]
        gathered = gather_rows(share, GD, n_gd)
        mixed = lax.all_to_all(gathered, "width", 0, 0, tiled=True)
        out_factor = (
            mixed.reshape(n_width, n_gd // n_width, piece_rows, NQ * RANK)
            .transpose(1, 0, 2, 3)
            .reshape(rows_out, NQ * RANK)
        )
        part_factor_in = jnp.dot(eigen_in, in_cols, preferred_element_type=jnp.float32)
        share_in = sum_scatter(part_factor_in, GD, n_gd).astype(jnp.bfloat16)
        in_factor = gather_rows(share_in, GD, n_gd)
        hidden = (jax.nn.silu(gate_pre.astype(jnp.float32)) * up_pre.astype(jnp.float32)).astype(
            jnp.bfloat16
        )
        proj_out = jnp.dot(grads_out, out_factor, preferred_element_type=jnp.float32)
        proj_in = jnp.dot(hidden, in_factor, preferred_element_type=jnp.float32)
        proj_out = sum_scatter(proj_out, "width", n_width)
        proj_in = sum_scatter(proj_in, "width", n_width)
        scores = (proj_out * proj_in).reshape(proj_out.shape[0], NQ, RANK).sum(axis=2).T
        return (scores, out_factor, in_factor)

    return per_device


def solution(mesh):
    n_gd = mesh.shape["grp"] * mesh.shape["dp"]
    n_width = mesh.shape["width"]
    return jax.shard_map(
        make_per_device(n_gd, n_width),
        mesh=mesh,
        in_specs=(
            P(None, GD),
            P(None, "width"),
            P(GD, "width"),
            P("width", GD),
            P("width", GD),
            P(GD, None),
            P(GD, "width"),
            P(GD, "width"),
            P(GD, "width"),
        ),
        out_specs=(P(None, GD + ("width",)), P("width", None), P("width", None)),
        check_vma=False,
    )
```

```python
import functools

import jax
import jax.numpy as jnp
from jax import lax
from jax.experimental import pallas as pl
from jax.experimental.pallas import tpu as pltpu
from jax.sharding import PartitionSpec as P

NQ = 16
QTOK = 32
RANK = 16
ITERS = 2
GROUPS = 2
NG = NQ // GROUPS
COLS = NG * RANK
LANES = 256

damping = 0.01
ridge_scale = 1e-06

GD = ("grp", "dp")
f32 = jnp.float32
bf16 = jnp.bfloat16
VMEM_LIMIT = 56 * 1024 * 1024


def params():
    return pltpu.CompilerParams(vmem_limit_bytes=VMEM_LIMIT)


def chunks(extent):
    return [(at, min(LANES, extent - at)) for at in range(0, extent, LANES)]


def lane_mask(rows, query):
    lane = lax.broadcasted_iota(jnp.int32, (rows, COLS), 1)
    return (lane >= query * RANK) & (lane < (query + 1) * RANK)


def image_block(rotated_ref, basis, query, image):
    product = jnp.dot(rotated_ref[query], basis, preferred_element_type=f32)
    return jnp.where(lane_mask(image.shape[0], query), product, image)


def form_kernel(place_ref, out_ref, in_ref, eig_ref, basis_ref, rotated_ref, image_ref, weight):
    rows, cols = eig_ref.shape
    weight[...] = 1.0 / (eig_ref[...] + damping)
    image = jnp.zeros((rows, COLS), f32)
    basis = basis_ref[...]
    for query in range(NG):
        left = out_ref[:, query * QTOK : (query + 1) * QTOK]
        for at, width in chunks(cols):
            right = in_ref[query * QTOK : (query + 1) * QTOK, at : at + width]
            block = jnp.dot(left, right, preferred_element_type=f32)
            rotated_ref[query, :, at : at + width] = (
                block * weight[:, at : at + width]
            ).astype(bf16)
        image = image_block(rotated_ref, basis, query, image)
    image_ref[...] = image.astype(image_ref.dtype)


def form_piece(place, out_piece, rot_in, eigvals, basis, piece, n_grp, n_dp, kind):
    rows = out_piece.shape[0]
    sub = rows // n_grp
    cols = rot_in.shape[1]

    def eig_block(j, place_ref):
        piece_at = lax.rem(place_ref[1] + piece + 1, n_dp)
        return piece_at * n_grp + lax.rem(place_ref[0] + j + 1, n_grp), 0

    return pl.pallas_call(
        form_kernel,
        grid_spec=pltpu.PrefetchScalarGridSpec(
            num_scalar_prefetch=1,
            grid=(n_grp,),
            in_specs=[
                pl.BlockSpec((sub, NG * QTOK), lambda j, _: (j, 0)),
                pl.BlockSpec((NG * QTOK, cols), lambda j, _: (0, 0)),
                pl.BlockSpec((sub, cols), eig_block),
                pl.BlockSpec((cols, COLS), lambda j, _: (0, 0)),
            ],
            out_specs=[
                pl.BlockSpec((NG, sub, cols), lambda j, _: (0, j, 0)),
                pl.BlockSpec((sub, COLS), lambda j, _: (j, 0)),
            ],
            scratch_shapes=[pltpu.VMEM((sub, cols), f32)],
        ),
        out_shape=[
            jax.ShapeDtypeStruct((NG, rows, cols), bf16),
            jax.ShapeDtypeStruct((rows, COLS), kind),
        ],
        compiler_params=params(),
        cost_estimate=pl.CostEstimate(
            flops=2 * NG * rows * cols * 512, bytes_accessed=NG * rows * cols * 2, transcendentals=0
        ),
        name="form",
    )(place, out_piece, rot_in, eigvals, basis)


def image_kernel(basis_ref, rotated_ref, image_ref):
    image = jnp.zeros((rotated_ref.shape[1], COLS), f32)
    basis = basis_ref[...]
    for query in range(NG):
        image = image_block(rotated_ref, basis, query, image)
    image_ref[...] = image.astype(image_ref.dtype)


def image_piece(basis, rotated, n_grp, kind):
    _, rows, cols = rotated.shape
    sub = rows // n_grp
    return pl.pallas_call(
        image_kernel,
        grid=(n_grp,),
        in_specs=[
            pl.BlockSpec((cols, COLS), lambda j: (0, 0)),
            pl.BlockSpec((NG, sub, cols), lambda j: (0, j, 0)),
        ],
        out_specs=pl.BlockSpec((sub, COLS), lambda j: (j, 0)),
        out_shape=jax.ShapeDtypeStruct((rows, COLS), kind),
        compiler_params=params(),
        cost_estimate=pl.CostEstimate(
            flops=2 * NG * rows * cols * 256, bytes_accessed=NG * rows * cols * 2, transcendentals=0
        ),
        name="image",
    )(basis, rotated)


def return_kernel(first, basis_ref, rotated_ref, *refs):
    total_ref = refs[-1]

    @pl.when(pl.program_id(0) == 0)
    def _():
        total_ref[...] = jnp.zeros_like(total_ref) if first else refs[0][...]

    for query in range(NG):
        rows = slice(query * RANK, (query + 1) * RANK)
        total_ref[rows, :] += jnp.dot(
            basis_ref[0, rows, :], rotated_ref[query], preferred_element_type=f32
        )


def return_piece(basis, rotated, piece, n_grp, total):
    _, rows, cols = rotated.shape
    sub = rows // n_grp
    first = total is None
    whole = pl.BlockSpec((COLS, cols), lambda j: (0, 0))
    return pl.pallas_call(
        functools.partial(return_kernel, first),
        grid=(n_grp,),
        in_specs=[
            pl.BlockSpec((1, COLS, sub), lambda j: (piece * n_grp + j, 0, 0)),
            pl.BlockSpec((NG, sub, cols), lambda j: (0, j, 0)),
        ]
        + ([] if first else [whole]),
        out_specs=whole,
        out_shape=jax.ShapeDtypeStruct((COLS, cols), f32),
        compiler_params=params(),
        cost_estimate=pl.CostEstimate(
            flops=2 * NG * rows * cols * 256, bytes_accessed=NG * rows * cols * 2, transcendentals=0
        ),
        name="returned",
    )(basis, rotated, *([] if first else [total]))


def roll_kernel(place_ref, part_ref, out_ref):
    out_ref[...] = part_ref[...].astype(out_ref.dtype)


def roll_piece(place, part, piece, n_grp, n_dp, kind):
    rows, cols = part.shape
    sub = rows // (n_grp * n_dp)

    def block(j, place_ref):
        piece_at = lax.rem(place_ref[1] + piece + 1, n_dp)
        return piece_at * n_grp + lax.rem(place_ref[0] + j + 1, n_grp), 0

    return pl.pallas_call(
        roll_kernel,
        grid_spec=pltpu.PrefetchScalarGridSpec(
            num_scalar_prefetch=1,
            grid=(n_grp,),
            in_specs=[pl.BlockSpec((sub, cols), block)],
            out_specs=pl.BlockSpec((sub, cols), lambda j, _: (j, 0)),
        ),
        out_shape=jax.ShapeDtypeStruct((rows // n_dp, cols), kind),
        name="roll",
    )(place, part)


def first_sum_kernel(n_grp, keep_ref, *refs):
    arrived, outs = refs[: -n_grp], refs[-n_grp:]
    sub = keep_ref.shape[0] // n_grp
    for j in range(n_grp):
        rows = slice(j * sub, (j + 1) * sub)
        total = keep_ref[rows, :]
        for ref in arrived:
            total = total + ref[rows, :].astype(f32)
        outs[j][...] = total.astype(outs[j].dtype)


def first_sum(keep, arrived, n_grp):
    rows, cols = keep.shape
    sub = rows // n_grp
    shapes = [jax.ShapeDtypeStruct((sub, cols), bf16) for _ in range(n_grp - 1)]
    return pl.pallas_call(
        functools.partial(first_sum_kernel, n_grp),
        out_shape=shapes + [jax.ShapeDtypeStruct((sub, cols), f32)],
        compiler_params=params(),
        name="first_sum",
    )(keep, *arrived)


def second_sum_kernel(keep_ref, *refs):
    total = keep_ref[...]
    for ref in refs[:-1]:
        total = total + ref[...].astype(f32)
    refs[-1][...] = total.astype(bf16)


def second_sum(keep, arrived):
    return pl.pallas_call(
        second_sum_kernel,
        out_shape=jax.ShapeDtypeStruct(keep.shape, bf16),
        compiler_params=params(),
        name="second_sum",
    )(keep, *arrived)


def reduce_gather(sends, keep, n_grp, n_dp):
    arrived = [
        lax.ppermute(send, "dp", [(i, (i + step + 1) % n_dp) for i in range(n_dp)])
        for step, send in enumerate(sends)
    ]
    *quarters, own = first_sum(keep, arrived, n_grp)
    arrived = [
        lax.ppermute(quarter, "grp", [(i, (i + step + 1) % n_grp) for i in range(n_grp)])
        for step, quarter in enumerate(quarters)
    ]
    block = second_sum(own, arrived)
    blocks = []
    for piece in range(n_dp):
        for j in range(n_grp):
            far_dp, far_grp = n_dp - 1 - piece, n_grp - 1 - j
            if far_dp == 0 and far_grp == 0:
                blocks.append(block)
                continue
            pairs = [
                (g * n_dp + d, ((g + far_grp) % n_grp) * n_dp + (d + far_dp) % n_dp)
                for g in range(n_grp)
                for d in range(n_dp)
            ]
            blocks.append(lax.ppermute(block, GD, pairs))
    return blocks


def gram_kernel(scale, *refs):
    out_ref = refs[-1]
    gram = jnp.zeros((COLS, COLS), f32)
    for ref in refs[:-1]:
        block = ref[...]
        gram = gram + lax.dot_general(
            block, block, (((0,), (0,)), ((), ())), preferred_element_type=f32
        )
    gram = jnp.where(same_query(), gram * scale, 0.0)
    compact = gram[:RANK]
    for query in range(1, NG):
        compact = compact + gram[query * RANK : (query + 1) * RANK]
    out_ref[...] = compact


def same_query():
    row = lax.broadcasted_iota(jnp.int32, (COLS, COLS), 0)
    col = lax.broadcasted_iota(jnp.int32, (COLS, COLS), 1)
    return row // RANK == col // RANK


def local_gram(blocks, scale):
    return pl.pallas_call(
        functools.partial(gram_kernel, scale),
        out_shape=jax.ShapeDtypeStruct((RANK, COLS), f32),
        compiler_params=params(),
        name="gram",
    )(*blocks)


def lower_inverse(compact):
    row = lax.broadcasted_iota(jnp.int32, (COLS, COLS), 0)
    col = lax.broadcasted_iota(jnp.int32, (COLS, COLS), 1)
    same = row // RANK == col // RANK
    eye = row == col
    gram = jnp.where(same, jnp.concatenate([compact] * NG, axis=0), 0.0)
    shape = (NG, RANK, COLS)
    gram = gram.reshape(shape)
    eye = eye.reshape(shape)
    row = lax.broadcasted_iota(jnp.int32, shape, 1)
    col = lax.broadcasted_iota(jnp.int32, shape, 2) % RANK
    trace = jnp.sum(
        jnp.sum(jnp.where(eye, gram, 0.0), axis=2, keepdims=True), axis=1, keepdims=True
    )
    left = gram + jnp.where(eye, ridge_scale * (trace / RANK), 0.0)
    right = jnp.where(eye, 1.0, 0.0)
    for step in range(RANK):
        column = jnp.sum(jnp.where(col == step, left, 0.0), axis=2, keepdims=True)
        pivot = column[:, step : step + 1, :]
        factor = jnp.where(row[:, :, :1] > step, column / pivot, 0.0)
        right = right - factor * right[:, step : step + 1, :]
        left = left - factor * left[:, step : step + 1, :]
    diagonal = jnp.sum(jnp.where(eye, left, 0.0), axis=2, keepdims=True)
    return (right * lax.rsqrt(diagonal)).reshape(COLS, COLS)


def basis_kernel(n_gram, *refs):
    grams, blocks, out_ref = refs[:n_gram], refs[n_gram:-1], refs[-1]
    compact = grams[0][...]
    for ref in grams[1:]:
        compact = compact + ref[...]
    inverse = lower_inverse(compact)
    for at, ref in enumerate(blocks):
        out_ref[at] = lax.dot_general(
            inverse,
            ref[...].astype(f32),
            (((1,), (1,)), ((), ())),
            precision=lax.Precision.HIGHEST,
            preferred_element_type=f32,
        ).astype(bf16)


def orthonormal(grams, blocks):
    sub = blocks[0].shape[0]
    return pl.pallas_call(
        functools.partial(basis_kernel, len(grams)),
        out_shape=jax.ShapeDtypeStruct((len(blocks), COLS, sub), bf16),
        compiler_params=params(),
        name="orthonormal",
    )(*grams, *blocks)


def sum_width(part, count):
    total = part + lax.ppermute(part, "width", [(i, i ^ 1) for i in range(count)])
    step = 2
    while step < count:
        sent = total.astype(bf16)
        got = lax.ppermute(sent, "width", [(i, i ^ step) for i in range(count)])
        total = total + got.astype(f32)
        step *= 2
    return total


def sum_scatter(part, axes, count):
    pieces = lax.all_to_all(part.astype(bf16), axes, 0, 0, tiled=True)
    pieces = pieces.reshape((count, part.shape[0] // count) + part.shape[1:])
    return jnp.sum(pieces.astype(f32), axis=0)


def gather_rows(piece, axes, count):
    copies = jnp.broadcast_to(piece[None], (count,) + piece.shape)
    whole = lax.all_to_all(copies, axes, 0, 0, tiled=True)
    return whole.reshape((count * piece.shape[0],) + piece.shape[1:])


def unroll_blocks(place, blocks, n_grp, n_dp):
    sub = blocks.shape[2]
    grid = blocks.reshape(n_dp, n_grp, COLS, sub)
    grid = jnp.roll(grid, place[1] + 1, axis=0)
    grid = jnp.roll(grid, place[0] + 1, axis=1)
    return grid.reshape(n_dp * n_grp, COLS, sub).transpose(1, 0, 2).reshape(COLS, -1)


def make_per_device(n_grp, n_dp, n_width):
    n_gd = n_grp * n_dp

    def per_device(
        query_out, query_in, eigen_out, eigen_in, eigvals, start, grads_out, gate_pre, up_pre
    ):
        place = jnp.stack([lax.axis_index("grp"), lax.axis_index("dp")]).astype(jnp.int32)
        scale = 1.0 / (eigen_out.shape[0] * n_gd)
        rows_out = eigvals.shape[0]
        kinds = [bf16] * (n_dp - 1) + [f32]
        finals, out_cols = [], []
        for group in range(GROUPS):
            span = slice(group * NG * QTOK, (group + 1) * NG * QTOK)
            part_out = lax.dot_general(
                eigen_out, query_out[span], (((0,), (1,)), ((), ())), preferred_element_type=f32
            )
            pieces = [
                roll_piece(place, part_out, piece, n_grp, n_dp, kind)
                for piece, kind in enumerate(kinds)
            ]
            rot_out = reduce_gather(pieces[:-1], pieces[-1], n_grp, n_dp)
            part_in = jnp.dot(query_in[span], eigen_in, preferred_element_type=f32)
            rot_in = sum_width(part_in, n_width).astype(bf16)
            basis = start[:, group * COLS : (group + 1) * COLS]
            rotated = []
            for iteration in range(ITERS):
                images = []
                for piece, kind in enumerate(kinds):
                    if iteration == 0:
                        out_piece = jnp.concatenate(
                            rot_out[piece * n_grp : (piece + 1) * n_grp], axis=0
                        )
                        block, image = form_piece(
                            place, out_piece, rot_in, eigvals, basis, piece, n_grp, n_dp, kind
                        )
                        rotated.append(block)
                    else:
                        image = image_piece(basis, rotated[piece], n_grp, kind)
                    images.append(image)
                blocks = reduce_gather(images[:-1], images[-1], n_grp, n_dp)
                gram = local_gram(blocks, scale)
                grams = [gram] + [
                    lax.ppermute(gram, "width", [(i, i ^ step) for i in range(n_width)])
                    for step in range(1, n_width)
                ]
                basis_out = orthonormal(grams, blocks)
                total = None
                for piece in range(n_dp):
                    total = return_piece(basis_out, rotated[piece], piece, n_grp, total)
                basis = sum_width(total, n_width).astype(bf16).T
            finals.append(basis)
            out_cols.append(unroll_blocks(place, basis_out, n_grp, n_dp))
        out_cols = jnp.concatenate(out_cols, axis=0)
        part_factor_out = lax.dot_general(
            eigen_out, out_cols, (((1,), (1,)), ((), ())), preferred_element_type=f32
        )
        share = sum_scatter(part_factor_out, "width", n_width).astype(bf16)
        piece_rows = share.shape[0]
        gathered = gather_rows(share, GD, n_gd)
        mixed = lax.all_to_all(gathered, "width", 0, 0, tiled=True)
        out_factor = (
            mixed.reshape(n_width, n_gd // n_width, piece_rows, NQ * RANK)
            .transpose(1, 0, 2, 3)
            .reshape(rows_out, NQ * RANK)
        )
        hidden = (jax.nn.silu(gate_pre.astype(f32)) * up_pre.astype(f32)).astype(bf16)
        in_factors = []
        for group in range(GROUPS):
            part = jnp.dot(eigen_in, finals[group], preferred_element_type=f32)
            pieces = [
                roll_piece(place, part, piece, n_grp, n_dp, kind)
                for piece, kind in enumerate(kinds)
            ]
            blocks = reduce_gather(pieces[:-1], pieces[-1], n_grp, n_dp)
            grid = jnp.stack(blocks).reshape(n_dp, n_grp, -1, COLS)
            grid = jnp.roll(grid, place[1] + 1, axis=0)
            grid = jnp.roll(grid, place[0] + 1, axis=1)
            in_factors.append(grid.reshape(-1, COLS))
        in_factor = jnp.concatenate(in_factors, axis=1)
        proj_out = jnp.dot(grads_out, out_factor, preferred_element_type=f32)
        proj_in = jnp.dot(hidden, in_factor, preferred_element_type=f32)
        proj_out = sum_scatter(proj_out, "width", n_width)
        proj_in = sum_scatter(proj_in, "width", n_width)
        scores = (proj_out * proj_in).reshape(proj_out.shape[0], NQ, RANK).sum(axis=2).T
        return (scores, out_factor, in_factor)

    return per_device


def solution(mesh):
    return jax.shard_map(
        make_per_device(mesh.shape["grp"], mesh.shape["dp"], mesh.shape["width"]),
        mesh=mesh,
        in_specs=(
            P(None, GD),
            P(None, "width"),
            P(GD, "width"),
            P("width", GD),
            P("width", GD),
            P(GD, None),
            P(GD, "width"),
            P(GD, "width"),
            P(GD, "width"),
        ),
        out_specs=(P(None, GD + ("width",)), P("width", None), P("width", None)),
        check_vma=False,
    )
```

```python
import functools

import jax
import jax.numpy as jnp
from jax import lax
from jax.experimental import pallas as pl
from jax.experimental.pallas import tpu as pltpu
from jax.sharding import PartitionSpec as P

NQ = 16
QTOK = 32
RANK = 16
ITERS = 2
CORES = 2
NG = NQ // CORES
COLS = NG * RANK
TOKS = NG * QTOK
LANES = 256
PIECES = 2

damping = 0.01
ridge_scale = 1e-06

GD = ("grp", "dp")
f32 = jnp.float32
bf16 = jnp.bfloat16


def params():
    return pltpu.CompilerParams(vmem_limit_bytes=48 * 1024 * 1024)


def chunks(extent):
    return [(at, min(LANES, extent - at)) for at in range(0, extent, LANES)]


def cost(shape, columns):
    count = shape[0] * shape[1] * shape[2]
    return pl.CostEstimate(
        flops=2 * count * columns, bytes_accessed=2 * count, transcendentals=0
    )


def add_image(product, query, image):
    lane = lax.broadcasted_iota(jnp.int32, image.shape, 1)
    image[...] = jnp.where(lane // RANK == query, product, image[...])


def write_image(image, send_ref, keep_ref):
    part, parts = pl.program_id(0), pl.num_programs(0)
    last = pl.program_id(1) == NG - 1

    @pl.when(last & (part < parts - 1))
    def _():
        send_ref[...] = image[...].astype(bf16)

    @pl.when(last & (part == parts - 1))
    def _():
        keep_ref[...] = image[...]


def form_kernel(n_dp, place_ref, *refs):
    out_refs = refs[:n_dp]
    in_ref, eig_ref, basis_ref, rotated_ref, send_ref, keep_ref = refs[n_dp : n_dp + 6]
    weight, left, right, image = refs[n_dp + 6 :]
    part, query = pl.program_id(0), pl.program_id(1)
    cols = eig_ref.shape[1]

    @pl.when(query == 0)
    def _():
        weight[...] = 1.0 / (eig_ref[...] + damping)
        right[...] = jnp.zeros_like(right)

    for at in range(n_dp):

        @pl.when((query == 0) & (part == at))
        def _(at=at):
            left[...] = out_refs[at][...]

    @pl.when(query > 0)
    def _():
        before = pl.ds(pl.multiple_of((query - 1) * QTOK, QTOK), QTOK)
        right[before, :] = jnp.zeros((QTOK, cols), bf16)

    own = pl.ds(pl.multiple_of(query * QTOK, QTOK), QTOK)
    right[own, :] = in_ref[own, :]
    for at, width in chunks(cols):
        span = slice(at, at + width)
        block = jnp.dot(left[...], right[:, span], preferred_element_type=f32)
        rotated_ref[0, :, span] = (block * weight[:, span]).astype(bf16)
    add_image(
        jnp.dot(rotated_ref[0], basis_ref[...], preferred_element_type=f32), query, image
    )
    write_image(image, send_ref, keep_ref)


def form_piece(place, out_parts, rot_in, eigvals, basis, piece):
    n_dp = len(out_parts)
    rows = out_parts[0].shape[0]
    cols = rot_in.shape[1]

    def eig_block(part, query, place_ref):
        return piece * n_dp + lax.rem(place_ref[0] + 1 + part, n_dp), 0

    def fixed(shape):
        return pl.BlockSpec(shape, lambda part, query, _: (0, 0))

    shape = (NG, n_dp * rows, cols)
    return pl.pallas_call(
        functools.partial(form_kernel, n_dp),
        grid_spec=pltpu.PrefetchScalarGridSpec(
            num_scalar_prefetch=1,
            grid=(n_dp, NG),
            in_specs=[fixed((rows, TOKS))] * n_dp
            + [
                fixed((TOKS, cols)),
                pl.BlockSpec((rows, cols), eig_block),
                fixed((cols, COLS)),
            ],
            out_specs=[
                pl.BlockSpec((1, rows, cols), lambda part, query, _: (query, part, 0)),
                pl.BlockSpec(
                    (rows, COLS), lambda part, query, _: (jnp.minimum(part, n_dp - 2), 0)
                ),
                fixed((rows, COLS)),
            ],
            scratch_shapes=[
                pltpu.VMEM((rows, cols), f32),
                pltpu.VMEM((rows, TOKS), bf16),
                pltpu.VMEM((TOKS, cols), bf16),
                pltpu.VMEM((rows, COLS), f32),
            ],
        ),
        out_shape=[
            jax.ShapeDtypeStruct(shape, bf16),
            jax.ShapeDtypeStruct(((n_dp - 1) * rows, COLS), bf16),
            jax.ShapeDtypeStruct((rows, COLS), f32),
        ],
        compiler_params=params(),
        cost_estimate=cost(shape, 600),
        name="form",
    )(place, *out_parts, rot_in, eigvals, basis)


def image_kernel(basis_ref, rotated_ref, send_ref, keep_ref, image):
    add_image(
        jnp.dot(rotated_ref[0], basis_ref[...], preferred_element_type=f32),
        pl.program_id(1),
        image,
    )
    write_image(image, send_ref, keep_ref)


def image_piece(basis, rotated, n_dp):
    _, rows, cols = rotated.shape
    rows = rows // n_dp
    return pl.pallas_call(
        image_kernel,
        grid=(n_dp, NG),
        in_specs=[
            pl.BlockSpec((cols, COLS), lambda part, query: (0, 0)),
            pl.BlockSpec((1, rows, cols), lambda part, query: (query, part, 0)),
        ],
        out_specs=[
            pl.BlockSpec((rows, COLS), lambda part, query: (jnp.minimum(part, n_dp - 2), 0)),
            pl.BlockSpec((rows, COLS), lambda part, query: (0, 0)),
        ],
        out_shape=[
            jax.ShapeDtypeStruct(((n_dp - 1) * rows, COLS), bf16),
            jax.ShapeDtypeStruct((rows, COLS), f32),
        ],
        scratch_shapes=[pltpu.VMEM((rows, COLS), f32)],
        compiler_params=params(),
        cost_estimate=cost(rotated.shape, 300),
        name="image",
    )(basis, rotated)


def return_kernel(n_dp, first, *refs):
    image_refs, rotated_ref = refs[:n_dp], refs[n_dp]
    total_ref, gram_ref, turned = refs[-3:]
    part, query = pl.program_id(0), pl.program_id(1)

    @pl.when((part == 0) & (query == 0))
    def _():
        if first:
            total_ref[...] = jnp.zeros_like(total_ref)
            gram_ref[...] = jnp.zeros_like(gram_ref)
        else:
            total_ref[...] = refs[n_dp + 1][...]
            gram_ref[...] = refs[n_dp + 2][...]

    for at in range(n_dp):

        @pl.when((query == 0) & (part == at))
        def _(at=at):
            image = image_refs[at][...]
            turned[...] = image.astype(f32).T.astype(bf16)
            gram_ref[...] += lax.dot_general(
                image, image, (((0,), (0,)), ((), ())), preferred_element_type=f32
            )

    own = pl.ds(pl.multiple_of(query * RANK, RANK), RANK)
    total_ref[own, :] += jnp.dot(turned[own, :], rotated_ref[0], preferred_element_type=f32)


def return_piece(images, rotated, before):
    n_dp = len(images)
    _, rows, cols = rotated.shape
    rows = rows // n_dp
    first = before is None

    def fixed(shape):
        return pl.BlockSpec(shape, lambda part, query: (0, 0))

    sums = [fixed((COLS, cols)), fixed((COLS, COLS))]
    return pl.pallas_call(
        functools.partial(return_kernel, n_dp, first),
        grid=(n_dp, NG),
        in_specs=[fixed((rows, COLS))] * n_dp
        + [pl.BlockSpec((1, rows, cols), lambda part, query: (query, part, 0))]
        + ([] if first else sums),
        out_specs=sums,
        out_shape=[
            jax.ShapeDtypeStruct((COLS, cols), f32),
            jax.ShapeDtypeStruct((COLS, COLS), f32),
        ],
        scratch_shapes=[pltpu.VMEM((COLS, rows), bf16)],
        compiler_params=params(),
        cost_estimate=cost(rotated.shape, 300),
        name="returned",
    )(*images, rotated, *([] if first else before))


def lower_inverse(gram):
    shape = (NG, RANK, COLS)
    row = lax.broadcasted_iota(jnp.int32, shape, 1)
    lane = lax.broadcasted_iota(jnp.int32, shape, 2)
    same = lane // RANK == lax.broadcasted_iota(jnp.int32, shape, 0)
    col = lane % RANK
    eye = same & (col == row)
    gram = jnp.where(same, gram.reshape(shape), 0.0)
    trace = jnp.sum(
        jnp.sum(jnp.where(eye, gram, 0.0), axis=2, keepdims=True), axis=1, keepdims=True
    )
    left = gram + jnp.where(eye, ridge_scale * (trace / RANK), 0.0)
    right = jnp.where(eye, 1.0, 0.0)
    for step in range(RANK):
        column = jnp.sum(jnp.where(col == step, left, 0.0), axis=2, keepdims=True)
        pivot = column[:, step : step + 1, :]
        factor = jnp.where(row[:, :, :1] > step, column / pivot, 0.0)
        right = right - factor * right[:, step : step + 1, :]
        left = left - factor * left[:, step : step + 1, :]
    diagonal = jnp.sum(jnp.where(eye, left, 0.0), axis=2, keepdims=True)
    return (right * lax.rsqrt(diagonal)).reshape(COLS, COLS)


def normalize_kernel(scale, total_ref, got_ref, gram_ref, gram_got_ref, basis_ref, inverse_ref):
    inverse = lower_inverse((gram_ref[...] + gram_got_ref[...]) * scale)
    inverse_ref[...] = inverse
    total = total_ref[...] + got_ref[...].astype(f32)
    basis_ref[...] = lax.dot_general(
        total,
        inverse,
        (((0,), (1,)), ((), ())),
        precision=lax.Precision.HIGHEST,
        preferred_element_type=f32,
    ).astype(bf16)


def normalize(total, got, gram, gram_got, scale):
    return pl.pallas_call(
        functools.partial(normalize_kernel, scale),
        out_shape=[
            jax.ShapeDtypeStruct((total.shape[1], COLS), bf16),
            jax.ShapeDtypeStruct((COLS, COLS), f32),
        ],
        compiler_params=params(),
        name="normalize",
    )(total, got, gram, gram_got)


def turned_by(count, step):
    return [(i, (i + step) % count) for i in range(count)]


def crossed(count, step):
    return [(i, i ^ step) for i in range(count)]


def swap_cores(part, n_width):
    return lax.ppermute(part, "width", crossed(n_width, 1))


def reduce_gather(sends, keep, n_grp, n_dp, even=False):
    rows = keep.shape[0]
    total = keep
    for part in range(n_dp - 1):
        send = sends[part * rows : (part + 1) * rows]
        total = total + lax.ppermute(send, "dp", turned_by(n_dp, part + 1)).astype(f32)
    step = 1
    while step < n_grp:
        sent = total.astype(bf16)
        got = lax.ppermute(sent, "grp", crossed(n_grp, step)).astype(f32)
        total = (sent.astype(f32) if even else total) + got
        step *= 2
    own = total.astype(bf16)
    others = [
        lax.ppermute(own, "dp", turned_by(n_dp, n_dp - 1 - part)) for part in range(n_dp - 1)
    ]
    return others + [own]


def unrolled(parts, dp):
    whole = jnp.stack(parts)
    whole = jnp.roll(whole, dp + 1, axis=0)
    return whole.reshape((-1,) + whole.shape[2:])


def split_parts(part, dp, n_dp, piece, pieces):
    rows = part.shape[0] // (pieces * n_dp)
    taken = [
        lax.dynamic_slice_in_dim(part, piece * n_dp * rows + (dp + 1 + at) % n_dp * rows, rows, 0)
        for at in range(n_dp)
    ]
    return jnp.concatenate(taken[:-1], axis=0).astype(bf16), taken[-1].astype(f32)


def sum_scatter(part, axes, count):
    pieces = lax.all_to_all(part.astype(bf16), axes, 0, 0, tiled=True)
    pieces = pieces.reshape((count, part.shape[0] // count) + part.shape[1:])
    return jnp.sum(pieces.astype(f32), axis=0)


def gather_rows(piece, axes, count):
    copies = jnp.broadcast_to(piece[None], (count,) + piece.shape)
    whole = lax.all_to_all(copies, axes, 0, 0, tiled=True)
    return whole.reshape((count * piece.shape[0],) + piece.shape[1:])


def make_per_device(n_grp, n_dp, n_width):
    n_gd = n_grp * n_dp

    def per_device(
        query_out, query_in, eigen_out, eigen_in, eigvals, start, grads_out, gate_pre, up_pre
    ):
        dp = lax.axis_index("dp")
        core = lax.axis_index("width") % CORES
        place = jnp.stack([dp]).astype(jnp.int32)
        scale = 1.0 / (eigen_out.shape[0] * n_gd)
        rows_out = eigvals.shape[0]

        def rows_of(array, index):
            return lax.dynamic_slice_in_dim(array, index * TOKS, TOKS, 0)

        def rotate_out(queries):
            return lax.dot_general(
                eigen_out, queries, (((0,), (1,)), ((), ())), preferred_element_type=f32
            )

        theirs_out = rotate_out(rows_of(query_out, 1 - core)).astype(bf16)
        theirs_out = swap_cores(theirs_out, n_width)
        mine_out = rotate_out(rows_of(query_out, core))
        theirs_in = jnp.dot(rows_of(query_in, 1 - core), eigen_in, preferred_element_type=f32)
        theirs_in = swap_cores(theirs_in, n_width)
        mine_in = jnp.dot(rows_of(query_in, core), eigen_in, preferred_element_type=f32)
        total_in = mine_in + theirs_in
        step = 2
        while step < n_width:
            got = lax.ppermute(total_in.astype(bf16), "width", crossed(n_width, step))
            total_in = total_in + got.astype(f32)
            step *= 2
        rot_in = total_in.astype(bf16)
        eig_sent, _, _ = lax.optimization_barrier((eigvals, theirs_out, theirs_in))
        eig_theirs = swap_cores(eig_sent, n_width)

        rot_out = []
        for part in (mine_out, theirs_out):
            for piece in range(PIECES):
                sends, keep = split_parts(part, dp, n_dp, piece, PIECES)
                rot_out.append(reduce_gather(sends, keep, n_grp, n_dp))
        basis = lax.dynamic_slice_in_dim(start, core * COLS, COLS, 1)
        count = len(rot_out)
        rotated = []
        for iteration in range(ITERS):
            images = []
            for at in range(count):
                if iteration == 0:
                    eig = eigvals if at < PIECES else eig_theirs
                    block, sends, keep = form_piece(
                        place, rot_out[at], rot_in, eig, basis, at % PIECES
                    )
                    rotated.append(block)
                else:
                    sends, keep = image_piece(basis, rotated[at], n_dp)
                images.append(reduce_gather(sends, keep, n_grp, n_dp))
            sums = None
            for at in range(count):
                sums = return_piece(images[at], rotated[at], sums)
            total, gram = sums
            step = 2
            while True:
                got = lax.ppermute(total.astype(bf16), "width", crossed(n_width, step))
                gram_got = lax.ppermute(gram, "width", crossed(n_width, step))
                step *= 2
                if step >= n_width:
                    break
                total = total + got.astype(f32)
                gram = gram + gram_got
            basis, inverse = normalize(total, got, gram, gram_got, scale)

        def columns(mine, theirs):
            return jnp.where(
                core == 0,
                jnp.concatenate([mine, theirs], axis=1),
                jnp.concatenate([theirs, mine], axis=1),
            )

        image = jnp.concatenate([unrolled(parts, dp) for parts in images], axis=0)
        basis_out = lax.dot_general(
            image.astype(f32),
            inverse,
            (((1,), (1,)), ((), ())),
            precision=lax.Precision.HIGHEST,
            preferred_element_type=f32,
        ).astype(bf16)
        out_cols = columns(basis_out[:rows_out], swap_cores(basis_out[rows_out:], n_width))
        part_factor_out = jnp.dot(eigen_out, out_cols, preferred_element_type=f32)
        share = sum_scatter(part_factor_out, "width", n_width).astype(bf16)
        piece_rows = share.shape[0]
        gathered = gather_rows(share, GD, n_gd)
        mixed = lax.all_to_all(gathered, "width", 0, 0, tiled=True)
        out_factor = (
            mixed.reshape(n_width, n_gd // n_width, piece_rows, NQ * RANK)
            .transpose(1, 0, 2, 3)
            .reshape(rows_out, NQ * RANK)
        )
        hidden = (jax.nn.silu(gate_pre.astype(f32)) * up_pre.astype(f32)).astype(bf16)
        hidden = lax.optimization_barrier(hidden)
        in_cols = columns(basis, swap_cores(basis, n_width))
        part_factor_in = jnp.dot(eigen_in, in_cols, preferred_element_type=f32)
        in_factors = []
        for piece in range(2 * PIECES):
            sends, keep = split_parts(part_factor_in, dp, n_dp, piece, 2 * PIECES)
            in_factors.append(unrolled(reduce_gather(sends, keep, n_grp, n_dp, even=True), dp))
        in_factor = jnp.concatenate(in_factors, axis=0)
        proj_out = jnp.dot(grads_out, out_factor, preferred_element_type=f32)
        proj_in = jnp.dot(hidden, in_factor, preferred_element_type=f32)
        proj_out = sum_scatter(proj_out, "width", n_width)
        proj_in = sum_scatter(proj_in, "width", n_width)
        scores = (proj_out * proj_in).reshape(proj_out.shape[0], NQ, RANK).sum(axis=2).T
        return (scores, out_factor, in_factor)

    return per_device


def solution(mesh):
    return jax.shard_map(
        make_per_device(mesh.shape["grp"], mesh.shape["dp"], mesh.shape["width"]),
        mesh=mesh,
        in_specs=(
            P(None, GD),
            P(None, "width"),
            P(GD, "width"),
            P("width", GD),
            P("width", GD),
            P(GD, None),
            P(GD, "width"),
            P(GD, "width"),
            P(GD, "width"),
        ),
        out_specs=(P(None, GD + ("width",)), P("width", None), P("width", None)),
        check_vma=False,
    )
```

```python
import functools

import jax
import jax.numpy as jnp
from jax import lax
from jax.experimental import pallas as pl
from jax.experimental.pallas import tpu as pltpu
from jax.sharding import PartitionSpec as P

NQ = 16
QTOK = 32
RANK = 16
ITERS = 2
CORES = 2
NG = NQ // CORES
COLS = NG * RANK
TOKS = NG * QTOK
LANES = 256
PIECES = 2
BLOCK = 4
FACTOR_PIECES = 4

damping = 0.01
ridge_scale = 1e-06

GD = ("grp", "dp")
f32 = jnp.float32
bf16 = jnp.bfloat16


def params():
    return pltpu.CompilerParams(vmem_limit_bytes=48 * 1024 * 1024)


def chunks(extent):
    return [(at, min(LANES, extent - at)) for at in range(0, extent, LANES)]


def cost(shape, columns):
    count = shape[0] * shape[1] * shape[2]
    return pl.CostEstimate(
        flops=2 * count * columns, bytes_accessed=2 * count, transcendentals=0
    )


def add_images(product, first, rows, image):
    lane = lax.broadcasted_iota(jnp.int32, (rows, COLS), 1) // RANK
    for at in range(BLOCK):
        image[...] = jnp.where(
            lane == first + at, product[at * rows : (at + 1) * rows], image[...]
        )


def write_image(image, send_ref, keep_ref):
    part, parts = pl.program_id(0), pl.num_programs(0)
    last = pl.program_id(1) == pl.num_programs(1) - 1

    @pl.when(last & (part < parts - 1))
    def _():
        send_ref[...] = image[...].astype(bf16)

    @pl.when(last & (part == parts - 1))
    def _():
        keep_ref[...] = image[...]


def image_of(rotated_ref, basis_ref):
    _, rows, cols = rotated_ref.shape
    return jnp.dot(
        rotated_ref[...].reshape(BLOCK * rows, cols), basis_ref[...], preferred_element_type=f32
    )


def form_kernel(n_dp, n_ties, place_ref, *refs):
    out_refs = refs[:n_dp]
    in_ref, eig_ref, basis_ref = refs[n_dp : n_dp + 3]
    rotated_ref, send_ref, keep_ref, weight, left, image = refs[n_dp + 3 + n_ties :]
    part, first = pl.program_id(0), pl.program_id(1) * BLOCK
    rows, cols = eig_ref.shape

    @pl.when(first == 0)
    def _():
        weight[...] = 1.0 / (eig_ref[...] + damping)

    for at in range(n_dp):

        @pl.when((first == 0) & (part == at))
        def _(at=at):
            for query in range(NG):
                left[query] = out_refs[at][:, query * QTOK : (query + 1) * QTOK]

    for at in range(BLOCK):
        query = first + at
        own = left[query]
        right = in_ref[pl.ds(pl.multiple_of(query * QTOK, QTOK), QTOK), :]
        for begin, width in chunks(cols):
            span = slice(begin, begin + width)
            block = jnp.dot(own, right[:, span], preferred_element_type=f32)
            rotated_ref[at, :, span] = (block * weight[:, span]).astype(bf16)
    add_images(image_of(rotated_ref, basis_ref), first, rows, image)
    write_image(image, send_ref, keep_ref)


def tied(ties):
    return [pl.BlockSpec(memory_space=pl.ANY)] * len(ties)


def form_piece(place, out_parts, rot_in, eigvals, basis, piece, ties):
    n_dp = len(out_parts)
    rows = out_parts[0].shape[0]
    cols = rot_in.shape[1]

    def eig_block(part, query, place_ref):
        return piece * n_dp + lax.rem(place_ref[0] + 1 + part, n_dp), 0

    def fixed(shape):
        return pl.BlockSpec(shape, lambda part, query, _: (0, 0))

    shape = (NG, n_dp * rows, cols)
    return pl.pallas_call(
        functools.partial(form_kernel, n_dp, len(ties)),
        grid_spec=pltpu.PrefetchScalarGridSpec(
            num_scalar_prefetch=1,
            grid=(n_dp, NG // BLOCK),
            in_specs=[fixed((rows, TOKS))] * n_dp
            + [
                fixed((TOKS, cols)),
                pl.BlockSpec((rows, cols), eig_block),
                fixed((cols, COLS)),
            ]
            + tied(ties),
            out_specs=[
                pl.BlockSpec((BLOCK, rows, cols), lambda part, query, _: (query, part, 0)),
                pl.BlockSpec(
                    (rows, COLS), lambda part, query, _: (jnp.minimum(part, n_dp - 2), 0)
                ),
                fixed((rows, COLS)),
            ],
            scratch_shapes=[
                pltpu.VMEM((rows, cols), f32),
                pltpu.VMEM((NG, rows, QTOK), bf16),
                pltpu.VMEM((rows, COLS), f32),
            ],
        ),
        out_shape=[
            jax.ShapeDtypeStruct(shape, bf16),
            jax.ShapeDtypeStruct(((n_dp - 1) * rows, COLS), bf16),
            jax.ShapeDtypeStruct((rows, COLS), f32),
        ],
        compiler_params=params(),
        cost_estimate=cost(shape, 400),
        name="form",
    )(place, *out_parts, rot_in, eigvals, basis, *ties)


def image_kernel(n_ties, basis_ref, rotated_ref, *refs):
    send_ref, keep_ref, image = refs[n_ties:]
    rows = image.shape[0]
    add_images(image_of(rotated_ref, basis_ref), pl.program_id(1) * BLOCK, rows, image)
    write_image(image, send_ref, keep_ref)


def image_piece(basis, rotated, n_dp, ties):
    _, rows, cols = rotated.shape
    rows = rows // n_dp
    return pl.pallas_call(
        functools.partial(image_kernel, len(ties)),
        grid=(n_dp, NG // BLOCK),
        in_specs=[
            pl.BlockSpec((cols, COLS), lambda part, query: (0, 0)),
            pl.BlockSpec((BLOCK, rows, cols), lambda part, query: (query, part, 0)),
        ]
        + tied(ties),
        out_specs=[
            pl.BlockSpec((rows, COLS), lambda part, query: (jnp.minimum(part, n_dp - 2), 0)),
            pl.BlockSpec((rows, COLS), lambda part, query: (0, 0)),
        ],
        out_shape=[
            jax.ShapeDtypeStruct(((n_dp - 1) * rows, COLS), bf16),
            jax.ShapeDtypeStruct((rows, COLS), f32),
        ],
        scratch_shapes=[pltpu.VMEM((rows, COLS), f32)],
        compiler_params=params(),
        cost_estimate=cost(rotated.shape, 256),
        name="image",
    )(basis, rotated, *ties)


def return_kernel(n_dp, first, *refs):
    image_refs, rotated_ref = refs[:n_dp], refs[n_dp]
    total_ref, gram_ref, turned = refs[-3:]
    part, step = pl.program_id(0), pl.program_id(1)

    @pl.when((part == 0) & (step == 0))
    def _():
        if first:
            total_ref[...] = jnp.zeros_like(total_ref)
            gram_ref[...] = jnp.zeros_like(gram_ref)
        else:
            total_ref[...] = refs[n_dp + 1][...]
            gram_ref[...] = refs[n_dp + 2][...]

    for at in range(n_dp):

        @pl.when((step == 0) & (part == at))
        def _(at=at):
            image = image_refs[at][...]
            turned[...] = image.astype(f32).T.astype(bf16)
            gram_ref[...] += lax.dot_general(
                image, image, (((0,), (0,)), ((), ())), preferred_element_type=f32
            )

    for at in range(BLOCK):
        own = pl.ds(pl.multiple_of((step * BLOCK + at) * RANK, RANK), RANK)
        total_ref[own, :] += jnp.dot(
            turned[own, :], rotated_ref[at], preferred_element_type=f32
        )


def return_piece(images, rotated, before, ties):
    n_dp = len(images)
    _, rows, cols = rotated.shape
    rows = rows // n_dp
    first = before is None

    def fixed(shape):
        return pl.BlockSpec(shape, lambda part, query: (0, 0))

    sums = [fixed((COLS, cols)), fixed((COLS, COLS))]
    return pl.pallas_call(
        functools.partial(return_kernel, n_dp, first),
        grid=(n_dp, NG // BLOCK),
        in_specs=[fixed((rows, COLS))] * n_dp
        + [pl.BlockSpec((BLOCK, rows, cols), lambda part, query: (query, part, 0))]
        + ([] if first else sums)
        + tied(ties),
        out_specs=sums,
        out_shape=[
            jax.ShapeDtypeStruct((COLS, cols), f32),
            jax.ShapeDtypeStruct((COLS, COLS), f32),
        ],
        scratch_shapes=[pltpu.VMEM((COLS, rows), bf16)],
        compiler_params=params(),
        cost_estimate=cost(rotated.shape, 256),
        name="returned",
    )(*images, rotated, *([] if first else before), *ties)


def rotate_in_kernel(place_ref, query_ref, eigen_ref, theirs_ref, mine_ref):
    for out_ref, index in ((theirs_ref, 1 - place_ref[1]), (mine_ref, place_ref[1])):
        rows = pl.ds(pl.multiple_of(index * TOKS, TOKS), TOKS)
        out_ref[...] = jnp.dot(query_ref[rows, :], eigen_ref[...], preferred_element_type=f32)


def rotate_in(place, query_in, eigen_in):
    depth, cols = eigen_in.shape
    width = LANES if cols % LANES == 0 else cols
    out = jax.ShapeDtypeStruct((TOKS, cols), f32)
    return pl.pallas_call(
        rotate_in_kernel,
        grid_spec=pltpu.PrefetchScalarGridSpec(
            num_scalar_prefetch=1,
            grid=(cols // width,),
            in_specs=[
                pl.BlockSpec(query_in.shape, lambda at, _: (0, 0)),
                pl.BlockSpec((depth, width), lambda at, _: (0, at)),
            ],
            out_specs=[pl.BlockSpec((TOKS, width), lambda at, _: (0, at))] * 2,
        ),
        out_shape=[out, out],
        compiler_params=params(),
        name="rotate_in",
    )(place, query_in, eigen_in)


def factor_kernel(n_ties, place_ref, eigen_ref, cols_ref, *refs):
    send_ref, keep_ref = refs[n_ties:]
    part, parts = pl.program_id(0), pl.num_programs(0)
    product = jnp.dot(eigen_ref[...], cols_ref[...], preferred_element_type=f32)

    @pl.when(part < parts - 1)
    def _():
        send_ref[...] = product.astype(bf16)

    @pl.when(part == parts - 1)
    def _():
        keep_ref[...] = product


def factor_piece(place, eigen_in, in_cols, piece, pieces, n_dp, ties):
    rows, depth = eigen_in.shape
    rows = rows // (pieces * n_dp)
    width = in_cols.shape[1]
    return pl.pallas_call(
        functools.partial(factor_kernel, len(ties)),
        grid_spec=pltpu.PrefetchScalarGridSpec(
            num_scalar_prefetch=1,
            grid=(n_dp,),
            in_specs=[
                pl.BlockSpec(
                    (rows, depth),
                    lambda part, place_ref: (
                        piece * n_dp + lax.rem(place_ref[0] + 1 + part, n_dp),
                        0,
                    ),
                ),
                pl.BlockSpec((depth, width), lambda part, _: (0, 0)),
            ]
            + tied(ties),
            out_specs=[
                pl.BlockSpec((rows, width), lambda part, _: (jnp.minimum(part, n_dp - 2), 0)),
                pl.BlockSpec((rows, width), lambda part, _: (0, 0)),
            ],
        ),
        out_shape=[
            jax.ShapeDtypeStruct(((n_dp - 1) * rows, width), bf16),
            jax.ShapeDtypeStruct((rows, width), f32),
        ],
        compiler_params=params(),
        name="factor",
    )(place, eigen_in, in_cols, *ties)


def project_kernel(n_dp, place_ref, hidden_ref, *refs):
    *part_refs, factor_ref, proj_ref = refs
    rows = part_refs[0].shape[0]
    for at, ref in enumerate(part_refs):
        owner = lax.rem(place_ref[0] + 1 + at % n_dp, n_dp)
        begin = (at // n_dp * n_dp + owner) * rows
        factor_ref[pl.ds(pl.multiple_of(begin, 8), rows), :] = ref[...]
    proj_ref[...] = jnp.dot(
        hidden_ref[...], factor_ref[...], preferred_element_type=f32
    ).astype(bf16)


def project(place, hidden, parts, n_dp):
    tokens, depth = hidden.shape
    width = parts[0].shape[1]
    vmem = pl.BlockSpec(memory_space=pltpu.VMEM)
    return pl.pallas_call(
        functools.partial(project_kernel, n_dp),
        in_specs=[pl.BlockSpec(memory_space=pltpu.SMEM)] + [vmem] * (1 + len(parts)),
        out_specs=[vmem, vmem],
        out_shape=[
            jax.ShapeDtypeStruct((depth, width), bf16),
            jax.ShapeDtypeStruct((tokens, width), bf16),
        ],
        compiler_params=params(),
        name="project",
    )(place, hidden, *parts)


def gram_kernel(*refs):
    gram = jnp.zeros((COLS, COLS), f32)
    for ref in refs[:-1]:
        image = ref[...]
        gram = gram + lax.dot_general(
            image, image, (((0,), (0,)), ((), ())), preferred_element_type=f32
        )
    refs[-1][...] = gram


def gram_of(images):
    return pl.pallas_call(
        gram_kernel,
        out_shape=jax.ShapeDtypeStruct((COLS, COLS), f32),
        compiler_params=params(),
        name="gram",
    )(*images)


def lower_inverse(gram):
    shape = (NG, RANK, COLS)
    row = lax.broadcasted_iota(jnp.int32, shape, 1)
    lane = lax.broadcasted_iota(jnp.int32, shape, 2)
    same = lane // RANK == lax.broadcasted_iota(jnp.int32, shape, 0)
    col = lane % RANK
    eye = same & (col == row)
    gram = jnp.where(same, gram.reshape(shape), 0.0)
    trace = jnp.sum(
        jnp.sum(jnp.where(eye, gram, 0.0), axis=2, keepdims=True), axis=1, keepdims=True
    )
    left = gram + jnp.where(eye, ridge_scale * (trace / RANK), 0.0)
    right = jnp.where(eye, 1.0, 0.0)
    for step in range(RANK):
        column = jnp.sum(jnp.where(col == step, left, 0.0), axis=2, keepdims=True)
        pivot = column[:, step : step + 1, :]
        factor = jnp.where(row[:, :, :1] > step, column / pivot, 0.0)
        right = right - factor * right[:, step : step + 1, :]
        left = left - factor * left[:, step : step + 1, :]
    diagonal = jnp.sum(jnp.where(eye, left, 0.0), axis=2, keepdims=True)
    return (right * lax.rsqrt(diagonal)).reshape(COLS, COLS)


def inverse_kernel(scale, gram_ref, gram_got_ref, inverse_ref):
    inverse_ref[...] = lower_inverse((gram_ref[...] + gram_got_ref[...]) * scale)


def inverse_of(gram, gram_got, scale):
    return pl.pallas_call(
        functools.partial(inverse_kernel, scale),
        out_shape=jax.ShapeDtypeStruct((COLS, COLS), f32),
        compiler_params=params(),
        name="inverse",
    )(gram, gram_got)


def normalize_kernel(total_ref, got_ref, inverse_ref, basis_ref):
    total = total_ref[...] + got_ref[...].astype(f32)
    basis_ref[...] = lax.dot_general(
        total,
        inverse_ref[...],
        (((0,), (1,)), ((), ())),
        precision=lax.Precision.HIGHEST,
        preferred_element_type=f32,
    ).astype(bf16)


def normalize(total, got, inverse):
    return pl.pallas_call(
        normalize_kernel,
        out_shape=jax.ShapeDtypeStruct((total.shape[1], COLS), bf16),
        compiler_params=params(),
        name="normalize",
    )(total, got, inverse)


def turned_by(count, step):
    return [(i, (i + step) % count) for i in range(count)]


def crossed(count, step):
    return [(i, i ^ step) for i in range(count)]


def swap_cores(part, n_width):
    return lax.ppermute(part, "width", crossed(n_width, 1))


class Reduction:
    def __init__(self, sends, keep, n_grp, n_dp, even=False):
        self.parts = None
        self.steps = self.run(sends, keep, n_grp, n_dp, even)
        next(self.steps)

    def advance(self):
        return next(self.steps, None) or []

    def run(self, sends, keep, n_grp, n_dp, even):
        rows = keep.shape[0]
        got = [
            lax.ppermute(
                sends[at * rows : (at + 1) * rows], "dp", turned_by(n_dp, at + 1)
            )
            for at in range(n_dp - 1)
        ]
        yield []
        total = keep
        for part in got:
            total = total + part.astype(f32)
        step = 1
        while step < n_grp:
            sent = total.astype(bf16)
            got = lax.ppermute(sent, "grp", crossed(n_grp, step))
            yield [sent]
            total = (sent.astype(f32) if even else total) + got.astype(f32)
            step *= 2
        own = total.astype(bf16)
        others = [
            lax.ppermute(own, "dp", turned_by(n_dp, n_dp - 1 - at)) for at in range(n_dp - 1)
        ]
        yield [own]
        self.parts = others + [own]


def advance_all(reductions):
    ties = []
    for reduction in reductions:
        if reduction.parts is None:
            ties += reduction.advance()
    return ties


def finish(reduction, reductions):
    ties = []
    while reduction.parts is None:
        ties = advance_all(reductions)
    return ties


def unrolled(parts, dp):
    whole = jnp.stack(parts)
    whole = jnp.roll(whole, dp + 1, axis=0)
    return whole.reshape((-1,) + whole.shape[2:])


def split_parts(part, dp, n_dp, piece, pieces):
    rows = part.shape[0] // (pieces * n_dp)
    taken = [
        lax.dynamic_slice_in_dim(part, piece * n_dp * rows + (dp + 1 + at) % n_dp * rows, rows, 0)
        for at in range(n_dp)
    ]
    return jnp.concatenate(taken[:-1], axis=0).astype(bf16), taken[-1].astype(f32)


def sum_scatter(part, axes, count):
    pieces = lax.all_to_all(part.astype(bf16), axes, 0, 0, tiled=True)
    pieces = pieces.reshape((count, part.shape[0] // count) + part.shape[1:])
    return jnp.sum(pieces.astype(f32), axis=0)


def gather_rows(piece, axes, count):
    copies = jnp.broadcast_to(piece[None], (count,) + piece.shape)
    whole = lax.all_to_all(copies, axes, 0, 0, tiled=True)
    return whole.reshape((count * piece.shape[0],) + piece.shape[1:])


def make_per_device(n_grp, n_dp, n_width):
    n_gd = n_grp * n_dp

    def per_device(
        query_out, query_in, eigen_out, eigen_in, eigvals, start, grads_out, gate_pre, up_pre
    ):
        dp = lax.axis_index("dp")
        core = lax.axis_index("width") % CORES
        place = jnp.stack([dp, core]).astype(jnp.int32)
        scale = 1.0 / (eigen_out.shape[0] * n_gd)
        rows_out = eigvals.shape[0]

        def rows_of(array, index):
            return lax.dynamic_slice_in_dim(array, index * TOKS, TOKS, 0)

        def rotate_out(queries):
            return lax.dot_general(
                eigen_out, queries, (((0,), (1,)), ((), ())), preferred_element_type=f32
            )

        def reduction(sends, keep, even=False):
            return Reduction(sends, keep, n_grp, n_dp, even)

        theirs_in, mine_in = rotate_in(place, query_in, eigen_in)
        total_in = mine_in + swap_cores(theirs_in, n_width)
        mine_out = rotate_out(rows_of(query_out, core))
        theirs_out = rotate_out(rows_of(query_out, 1 - core)).astype(bf16)
        theirs_out = swap_cores(theirs_out, n_width)
        step = 2
        while step < n_width:
            got = lax.ppermute(total_in.astype(bf16), "width", crossed(n_width, step))
            total_in = total_in + got.astype(f32)
            step *= 2
        rot_in = total_in.astype(bf16)
        eig_sent, _, _ = lax.optimization_barrier((eigvals, theirs_out, total_in))
        eig_theirs = swap_cores(eig_sent, n_width)

        turning = []
        for part in (mine_out, theirs_out):
            for piece in range(PIECES):
                advance_all(turning)
                turning.append(reduction(*split_parts(part, dp, n_dp, piece, PIECES)))
        basis = lax.dynamic_slice_in_dim(start, core * COLS, COLS, 1)
        count = len(turning)
        rotated = []
        for iteration in range(ITERS):
            summing, ties = [], []
            for at in range(count):
                if iteration == 0:
                    finish(turning[at], turning)
                    eig = eigvals if at < PIECES else eig_theirs
                    block, sends, keep = form_piece(
                        place, turning[at].parts, rot_in, eig, basis, at % PIECES, ties
                    )
                    rotated.append(block)
                    ties = advance_all(turning)
                else:
                    sends, keep = image_piece(basis, rotated[at], n_dp, ties)
                    ties = []
                ties += advance_all(summing)
                summing.append(reduction(sends, keep))
            sums = None
            for at in range(count):
                finish(summing[at], summing)
                if at == count - 1:
                    gram = gram_of([part for each in summing for part in each.parts])
                    step = 2
                    while step < n_width:
                        gram_got = lax.ppermute(gram, "width", crossed(n_width, step))
                        step *= 2
                        if step < n_width:
                            gram = gram + gram_got
                    ties = [gram]
                sums = return_piece(summing[at].parts, rotated[at], sums, ties)
                ties = advance_all(summing)
            inverse = inverse_of(gram, gram_got, scale)
            total = sums[0]
            step = 2
            while step < n_width:
                got = lax.ppermute(total.astype(bf16), "width", crossed(n_width, step))
                step *= 2
                if step < n_width:
                    total = total + got.astype(f32)
            basis = normalize(total, got, inverse)

        def columns(mine, theirs):
            return jnp.where(
                core == 0,
                jnp.concatenate([mine, theirs], axis=1),
                jnp.concatenate([theirs, mine], axis=1),
            )

        hidden = (jax.nn.silu(gate_pre.astype(f32)) * up_pre.astype(f32)).astype(bf16)
        image = jnp.concatenate([unrolled(each.parts, dp) for each in summing], axis=0)
        basis_out = lax.dot_general(
            image.astype(f32),
            inverse,
            (((1,), (1,)), ((), ())),
            precision=lax.Precision.HIGHEST,
            preferred_element_type=f32,
        ).astype(bf16)
        out_cols = columns(basis_out[:rows_out], swap_cores(basis_out[rows_out:], n_width))
        part_factor_out = jnp.dot(eigen_out, out_cols, preferred_element_type=f32)
        share = sum_scatter(part_factor_out, "width", n_width).astype(bf16)
        piece_rows = share.shape[0]
        gathered = gather_rows(share, GD, n_gd)
        mixed = lax.all_to_all(gathered, "width", 0, 0, tiled=True)
        out_factor = (
            mixed.reshape(n_width, n_gd // n_width, piece_rows, NQ * RANK)
            .transpose(1, 0, 2, 3)
            .reshape(rows_out, NQ * RANK)
        )
        in_cols = columns(basis, swap_cores(basis, n_width))
        factors, ties = [], []
        for piece in range(FACTOR_PIECES):
            sends, keep = factor_piece(
                place, eigen_in, in_cols, piece, FACTOR_PIECES, n_dp, ties
            )
            ties = advance_all(factors)
            factors.append(reduction(sends, keep, even=True))
        for each in factors:
            finish(each, factors)
        parts = [part for each in factors for part in each.parts]
        in_factor, proj_in = project(place, hidden, parts, n_dp)
        proj_out = jnp.dot(grads_out, out_factor, preferred_element_type=f32)
        proj_out = sum_scatter(proj_out, "width", n_width)
        proj_in = sum_scatter(proj_in, "width", n_width)
        scores = (proj_out * proj_in).reshape(proj_out.shape[0], NQ, RANK).sum(axis=2).T
        return (scores, out_factor, in_factor)

    return per_device


def solution(mesh):
    return jax.shard_map(
        make_per_device(mesh.shape["grp"], mesh.shape["dp"], mesh.shape["width"]),
        mesh=mesh,
        in_specs=(
            P(None, GD),
            P(None, "width"),
            P(GD, "width"),
            P("width", GD),
            P("width", GD),
            P(GD, None),
            P(GD, "width"),
            P(GD, "width"),
            P(GD, "width"),
        ),
        out_specs=(P(None, GD + ("width",)), P("width", None), P("width", None)),
        check_vma=False,
    )
```

```python
import functools

import jax
import jax.numpy as jnp
from jax import lax
from jax.experimental import pallas as pl
from jax.experimental.pallas import tpu as pltpu
from jax.sharding import PartitionSpec as P

NQ = 16
QTOK = 32
RANK = 16
ITERS = 2
CORES = 2
NG = NQ // CORES
COLS = NG * RANK
TOKS = NG * QTOK
LANES = 256
PIECES = 2
BLOCK = 4
FACTOR_PIECES = 4

damping = 0.01
ridge_scale = 1e-06

GD = ("grp", "dp")
f32 = jnp.float32
bf16 = jnp.bfloat16


def params():
    return pltpu.CompilerParams(vmem_limit_bytes=48 * 1024 * 1024)


def chunks(extent):
    return [(at, min(LANES, extent - at)) for at in range(0, extent, LANES)]


def cost(shape, columns):
    count = shape[0] * shape[1] * shape[2]
    return pl.CostEstimate(
        flops=2 * count * columns, bytes_accessed=2 * count, transcendentals=0
    )


def add_images(product, first, rows, image):
    lane = lax.broadcasted_iota(jnp.int32, (rows, COLS), 1) // RANK
    for at in range(BLOCK):
        image[...] = jnp.where(
            lane == first + at, product[at * rows : (at + 1) * rows], image[...]
        )


def write_image(image, send_ref, keep_ref):
    part, parts = pl.program_id(0), pl.num_programs(0)
    last = pl.program_id(1) == pl.num_programs(1) - 1

    @pl.when(last & (part < parts - 1))
    def _():
        send_ref[...] = image[...].astype(bf16)

    @pl.when(last & (part == parts - 1))
    def _():
        keep_ref[...] = image[...]


def image_of(rotated_ref, basis_ref):
    _, rows, cols = rotated_ref.shape
    return jnp.dot(
        rotated_ref[...].reshape(BLOCK * rows, cols), basis_ref[...], preferred_element_type=f32
    )


def form_kernel(n_dp, n_ties, place_ref, *refs):
    out_refs = refs[:n_dp]
    in_ref, eig_ref, basis_ref = refs[n_dp : n_dp + 3]
    rotated_ref, send_ref, keep_ref, weight, left, image = refs[n_dp + 3 + n_ties :]
    part, first = pl.program_id(0), pl.program_id(1) * BLOCK
    rows, cols = eig_ref.shape

    @pl.when(first == 0)
    def _():
        weight[...] = 1.0 / (eig_ref[...] + damping)

    for at in range(n_dp):

        @pl.when((first == 0) & (part == at))
        def _(at=at):
            for query in range(NG):
                left[query] = out_refs[at][:, query * QTOK : (query + 1) * QTOK]

    for at in range(BLOCK):
        query = first + at
        own = left[query]
        right = in_ref[pl.ds(pl.multiple_of(query * QTOK, QTOK), QTOK), :]
        for begin, width in chunks(cols):
            span = slice(begin, begin + width)
            block = jnp.dot(own, right[:, span], preferred_element_type=f32)
            rotated_ref[at, :, span] = (block * weight[:, span]).astype(bf16)
        product = jnp.dot(rotated_ref[at], basis_ref[...], preferred_element_type=f32)
        lane = lax.broadcasted_iota(jnp.int32, (rows, COLS), 1) // RANK
        image[...] = jnp.where(lane == query, product, image[...])
    write_image(image, send_ref, keep_ref)


def tied(ties):
    return [pl.BlockSpec(memory_space=pl.ANY)] * len(ties)


def form_piece(place, out_parts, rot_in, eigvals, basis, piece, ties):
    n_dp = len(out_parts)
    rows = out_parts[0].shape[0]
    cols = rot_in.shape[1]

    def eig_block(part, query, place_ref):
        return piece * n_dp + lax.rem(place_ref[0] + 1 + part, n_dp), 0

    def fixed(shape):
        return pl.BlockSpec(shape, lambda part, query, _: (0, 0))

    shape = (NG, n_dp * rows, cols)
    return pl.pallas_call(
        functools.partial(form_kernel, n_dp, len(ties)),
        grid_spec=pltpu.PrefetchScalarGridSpec(
            num_scalar_prefetch=1,
            grid=(n_dp, NG // BLOCK),
            in_specs=[fixed((rows, TOKS))] * n_dp
            + [
                fixed((TOKS, cols)),
                pl.BlockSpec((rows, cols), eig_block),
                fixed((cols, COLS)),
            ]
            + tied(ties),
            out_specs=[
                pl.BlockSpec((BLOCK, rows, cols), lambda part, query, _: (query, part, 0)),
                pl.BlockSpec(
                    (rows, COLS), lambda part, query, _: (jnp.minimum(part, n_dp - 2), 0)
                ),
                fixed((rows, COLS)),
            ],
            scratch_shapes=[
                pltpu.VMEM((rows, cols), f32),
                pltpu.VMEM((NG, rows, QTOK), bf16),
                pltpu.VMEM((rows, COLS), f32),
            ],
        ),
        out_shape=[
            jax.ShapeDtypeStruct(shape, bf16),
            jax.ShapeDtypeStruct(((n_dp - 1) * rows, COLS), bf16),
            jax.ShapeDtypeStruct((rows, COLS), f32),
        ],
        compiler_params=params(),
        cost_estimate=cost(shape, 400),
        name="form",
    )(place, *out_parts, rot_in, eigvals, basis, *ties)


def image_kernel(n_ties, basis_ref, rotated_ref, *refs):
    send_ref, keep_ref, image = refs[n_ties:]
    rows = image.shape[0]
    add_images(image_of(rotated_ref, basis_ref), pl.program_id(1) * BLOCK, rows, image)
    write_image(image, send_ref, keep_ref)


def image_piece(basis, rotated, n_dp, ties):
    _, rows, cols = rotated.shape
    rows = rows // n_dp
    return pl.pallas_call(
        functools.partial(image_kernel, len(ties)),
        grid=(n_dp, NG // BLOCK),
        in_specs=[
            pl.BlockSpec((cols, COLS), lambda part, query: (0, 0)),
            pl.BlockSpec((BLOCK, rows, cols), lambda part, query: (query, part, 0)),
        ]
        + tied(ties),
        out_specs=[
            pl.BlockSpec((rows, COLS), lambda part, query: (jnp.minimum(part, n_dp - 2), 0)),
            pl.BlockSpec((rows, COLS), lambda part, query: (0, 0)),
        ],
        out_shape=[
            jax.ShapeDtypeStruct(((n_dp - 1) * rows, COLS), bf16),
            jax.ShapeDtypeStruct((rows, COLS), f32),
        ],
        scratch_shapes=[pltpu.VMEM((rows, COLS), f32)],
        compiler_params=params(),
        cost_estimate=cost(rotated.shape, 256),
        name="image",
    )(basis, rotated, *ties)


def return_kernel(n_dp, first, *refs):
    image_refs, rotated_ref = refs[:n_dp], refs[n_dp]
    total_ref, gram_ref, turned = refs[-3:]
    part, step = pl.program_id(0), pl.program_id(1)

    @pl.when((part == 0) & (step == 0))
    def _():
        if first:
            total_ref[...] = jnp.zeros_like(total_ref)
            gram_ref[...] = jnp.zeros_like(gram_ref)
        else:
            total_ref[...] = refs[n_dp + 1][...]
            gram_ref[...] = refs[n_dp + 2][...]

    for at in range(n_dp):

        @pl.when((step == 0) & (part == at))
        def _(at=at):
            image = image_refs[at][...]
            turned[...] = image.astype(f32).T.astype(bf16)
            gram_ref[...] += lax.dot_general(
                image, image, (((0,), (0,)), ((), ())), preferred_element_type=f32
            )

    for at in range(BLOCK):
        own = pl.ds(pl.multiple_of((step * BLOCK + at) * RANK, RANK), RANK)
        total_ref[own, :] += jnp.dot(
            turned[own, :], rotated_ref[at], preferred_element_type=f32
        )


def return_piece(images, rotated, before, ties):
    n_dp = len(images)
    _, rows, cols = rotated.shape
    rows = rows // n_dp
    first = before is None

    def fixed(shape):
        return pl.BlockSpec(shape, lambda part, query: (0, 0))

    sums = [fixed((COLS, cols)), fixed((COLS, COLS))]
    return pl.pallas_call(
        functools.partial(return_kernel, n_dp, first),
        grid=(n_dp, NG // BLOCK),
        in_specs=[fixed((rows, COLS))] * n_dp
        + [pl.BlockSpec((BLOCK, rows, cols), lambda part, query: (query, part, 0))]
        + ([] if first else sums)
        + tied(ties),
        out_specs=sums,
        out_shape=[
            jax.ShapeDtypeStruct((COLS, cols), f32),
            jax.ShapeDtypeStruct((COLS, COLS), f32),
        ],
        scratch_shapes=[pltpu.VMEM((COLS, rows), bf16)],
        compiler_params=params(),
        cost_estimate=cost(rotated.shape, 256),
        name="returned",
    )(*images, rotated, *([] if first else before), *ties)


def rotate_out_kernel(n_dp, place_ref, query_ref, eigen_ref, *refs):
    turned = refs[-1]
    width = eigen_ref.shape[1]
    rows = width // (PIECES * n_dp)
    for side, index in ((0, place_ref[1]), (1, 1 - place_ref[1])):
        queries = query_ref[pl.ds(pl.multiple_of(index * TOKS, TOKS), TOKS), :]
        for begin, count in chunks(width):
            product = jnp.dot(
                queries, eigen_ref[:, begin : begin + count], preferred_element_type=f32
            )
            turned[begin : begin + count, :] = product.T
        for piece in range(PIECES):
            send_ref, keep_ref = refs[2 * (side * PIECES + piece) :][:2]
            for part in range(n_dp):
                at = piece * n_dp + lax.rem(place_ref[0] + 1 + part, n_dp)
                taken = turned[pl.ds(pl.multiple_of(at * rows, rows), rows), :]
                if part < n_dp - 1:
                    send_ref[part * rows : (part + 1) * rows, :] = taken.astype(bf16)
                else:
                    keep_ref[...] = taken.astype(keep_ref.dtype)


def rotate_out(place, query_out, eigen_out, n_dp):
    width = eigen_out.shape[1]
    rows = width // (PIECES * n_dp)
    shapes = []
    for kind in (f32, bf16):
        for _ in range(PIECES):
            shapes.append(jax.ShapeDtypeStruct(((n_dp - 1) * rows, TOKS), bf16))
            shapes.append(jax.ShapeDtypeStruct((rows, TOKS), kind))
    vmem = pl.BlockSpec(memory_space=pltpu.VMEM)
    return pl.pallas_call(
        functools.partial(rotate_out_kernel, n_dp),
        in_specs=[pl.BlockSpec(memory_space=pltpu.SMEM), vmem, vmem],
        out_specs=[vmem] * len(shapes),
        out_shape=shapes,
        scratch_shapes=[pltpu.VMEM((width, TOKS), f32)],
        compiler_params=params(),
        name="rotate_out",
    )(place, query_out, eigen_out)


def rotate_in_kernel(n_ties, place_ref, query_ref, eigen_ref, *refs):
    theirs_ref, mine_ref, product = refs[n_ties:]
    product[...] = jnp.dot(query_ref[...], eigen_ref[...], preferred_element_type=f32)
    for out_ref, index in ((theirs_ref, 1 - place_ref[1]), (mine_ref, place_ref[1])):
        out_ref[...] = product[pl.ds(pl.multiple_of(index * TOKS, TOKS), TOKS), :]


def rotate_in(place, query_in, eigen_in, ties):
    depth, cols = eigen_in.shape
    width = LANES if cols % LANES == 0 else cols
    out = jax.ShapeDtypeStruct((TOKS, cols), f32)
    return pl.pallas_call(
        functools.partial(rotate_in_kernel, len(ties)),
        grid_spec=pltpu.PrefetchScalarGridSpec(
            num_scalar_prefetch=1,
            grid=(cols // width,),
            in_specs=[
                pl.BlockSpec(query_in.shape, lambda at, _: (0, 0)),
                pl.BlockSpec((depth, width), lambda at, _: (0, at)),
            ]
            + tied(ties),
            out_specs=[pl.BlockSpec((TOKS, width), lambda at, _: (0, at))] * 2,
            scratch_shapes=[pltpu.VMEM((CORES * TOKS, width), f32)],
        ),
        out_shape=[out, out],
        compiler_params=params(),
        cost_estimate=pl.CostEstimate(
            flops=2 * depth * cols * CORES * TOKS, bytes_accessed=2 * depth * cols, transcendentals=0
        ),
        name="rotate_in",
    )(place, query_in, eigen_in, *ties)


def side_by_side(place_ref, mine, theirs):
    return jnp.where(
        place_ref[1] == 0,
        jnp.concatenate([mine, theirs], axis=1),
        jnp.concatenate([theirs, mine], axis=1),
    )


def factor_kernel(n_dp, place_ref, eigen_ref, mine_ref, theirs_ref, *refs):
    *out_refs, cols = refs
    step = pl.program_id(0)
    rows = eigen_ref.shape[0]

    @pl.when(step == 0)
    def _():
        cols[...] = side_by_side(place_ref, mine_ref[...], theirs_ref[...])

    product = jnp.dot(eigen_ref[...], cols[...], preferred_element_type=f32)
    for piece in range(FACTOR_PIECES):
        send_ref, keep_ref = out_refs[2 * piece : 2 * piece + 2]
        for part in range(n_dp):

            @pl.when(step == piece * n_dp + part)
            def _(part=part, send_ref=send_ref, keep_ref=keep_ref):
                if part < n_dp - 1:
                    send_ref[part * rows : (part + 1) * rows, :] = product.astype(bf16)
                else:
                    keep_ref[...] = product


def factor_in(place, eigen_in, mine, theirs, n_dp):
    rows, depth = eigen_in.shape
    rows = rows // (FACTOR_PIECES * n_dp)
    width = CORES * COLS
    fixed = pl.BlockSpec((depth, COLS), lambda at, _: (0, 0))

    def eigen_block(at, place_ref):
        return at // n_dp * n_dp + lax.rem(place_ref[0] + 1 + at % n_dp, n_dp), 0

    shapes = [
        jax.ShapeDtypeStruct(((n_dp - 1) * rows, width), bf16),
        jax.ShapeDtypeStruct((rows, width), f32),
    ] * FACTOR_PIECES
    return pl.pallas_call(
        functools.partial(factor_kernel, n_dp),
        grid_spec=pltpu.PrefetchScalarGridSpec(
            num_scalar_prefetch=1,
            grid=(FACTOR_PIECES * n_dp,),
            in_specs=[pl.BlockSpec((rows, depth), eigen_block), fixed, fixed],
            out_specs=[pl.BlockSpec(each.shape, lambda at, _: (0, 0)) for each in shapes],
            scratch_shapes=[pltpu.VMEM((depth, width), bf16)],
        ),
        out_shape=shapes,
        compiler_params=params(),
        name="factor_in",
    )(place, eigen_in, mine, theirs)


def write_shares(place_ref, total, keep_ref, send_refs):
    rows = keep_ref.shape[0]
    for step in range(len(send_refs) + 1):
        other = place_ref[2] ^ step
        share = total[pl.ds(pl.multiple_of(other * rows, rows), rows), :]
        if step == 0:
            keep_ref[...] = share
        else:
            send_refs[step - 1][...] = share.astype(bf16)


def factor_out_kernel(place_ref, eigen_ref, mine_ref, theirs_ref, keep_ref, *refs):
    *send_refs, total = refs
    total[...] = jnp.dot(
        eigen_ref[...],
        side_by_side(place_ref, mine_ref[...], theirs_ref[...]),
        preferred_element_type=f32,
    )
    write_shares(place_ref, total, keep_ref, send_refs)


def shares(rows, width, n_width):
    shape = (rows // n_width, width)
    return [jax.ShapeDtypeStruct(shape, f32)] + [jax.ShapeDtypeStruct(shape, bf16)] * (n_width - 1)


def factor_out(place, eigen_out, mine, theirs, n_width):
    rows = eigen_out.shape[0]
    width = CORES * COLS
    vmem = pl.BlockSpec(memory_space=pltpu.VMEM)
    return pl.pallas_call(
        factor_out_kernel,
        in_specs=[pl.BlockSpec(memory_space=pltpu.SMEM)] + [vmem] * 3,
        out_specs=[vmem] * n_width,
        out_shape=shares(rows, width, n_width),
        scratch_shapes=[pltpu.VMEM((rows, width), f32)],
        compiler_params=params(),
        name="factor_out",
    )(place, eigen_out, mine, theirs)


def project_kernel(n_dp, n_parts, place_ref, hidden_ref, *refs):
    part_refs = refs[:n_parts]
    factor_ref, keep_ref, *send_refs, total = refs[n_parts:]
    rows = part_refs[0].shape[0]
    for at, ref in enumerate(part_refs):
        owner = lax.rem(place_ref[0] + 1 + at % n_dp, n_dp)
        begin = (at // n_dp * n_dp + owner) * rows
        factor_ref[pl.ds(pl.multiple_of(begin, 8), rows), :] = ref[...]
    total[...] = jnp.dot(hidden_ref[...], factor_ref[...], preferred_element_type=f32)
    write_shares(place_ref, total, keep_ref, send_refs)


def project(place, hidden, parts, n_dp, n_width):
    tokens, depth = hidden.shape
    width = parts[0].shape[1]
    vmem = pl.BlockSpec(memory_space=pltpu.VMEM)
    return pl.pallas_call(
        functools.partial(project_kernel, n_dp, len(parts)),
        in_specs=[pl.BlockSpec(memory_space=pltpu.SMEM)] + [vmem] * (1 + len(parts)),
        out_specs=[vmem] * (1 + n_width),
        out_shape=[jax.ShapeDtypeStruct((depth, width), bf16)] + shares(tokens, width, n_width),
        scratch_shapes=[pltpu.VMEM((tokens, width), f32)],
        compiler_params=params(),
        name="project",
    )(place, hidden, *parts)


def turn_kernel(n_dp, place_ref, inverse_ref, *refs):
    *image_refs, mine_ref, theirs_ref = refs
    rows = image_refs[0].shape[0]
    for at, ref in enumerate(image_refs):
        out_ref = mine_ref if at < PIECES * n_dp else theirs_ref
        owner = lax.rem(place_ref[0] + 1 + at % n_dp, n_dp)
        begin = (at // n_dp % PIECES * n_dp + owner) * rows
        out_ref[pl.ds(pl.multiple_of(begin, rows), rows), :] = lax.dot_general(
            ref[...].astype(f32),
            inverse_ref[...],
            (((1,), (1,)), ((), ())),
            precision=lax.Precision.HIGHEST,
            preferred_element_type=f32,
        ).astype(bf16)


def turn(place, inverse, images, n_dp):
    out = jax.ShapeDtypeStruct((PIECES * n_dp * images[0].shape[0], COLS), bf16)
    vmem = pl.BlockSpec(memory_space=pltpu.VMEM)
    return pl.pallas_call(
        functools.partial(turn_kernel, n_dp),
        in_specs=[pl.BlockSpec(memory_space=pltpu.SMEM)] + [vmem] * (1 + len(images)),
        out_specs=[vmem, vmem],
        out_shape=[out, out],
        compiler_params=params(),
        name="turn",
    )(place, inverse, *images)


def gram_kernel(*refs):
    gram = jnp.zeros((COLS, COLS), f32)
    for ref in refs[:-1]:
        image = ref[...]
        gram = gram + lax.dot_general(
            image, image, (((0,), (0,)), ((), ())), preferred_element_type=f32
        )
    refs[-1][...] = gram


def gram_of(images):
    return pl.pallas_call(
        gram_kernel,
        out_shape=jax.ShapeDtypeStruct((COLS, COLS), f32),
        compiler_params=params(),
        name="gram",
    )(*images)


def lower_inverse(gram):
    shape = (NG, RANK, COLS)
    row = lax.broadcasted_iota(jnp.int32, shape, 1)
    lane = lax.broadcasted_iota(jnp.int32, shape, 2)
    same = lane // RANK == lax.broadcasted_iota(jnp.int32, shape, 0)
    col = lane % RANK
    eye = same & (col == row)
    gram = jnp.where(same, gram.reshape(shape), 0.0)
    trace = jnp.sum(
        jnp.sum(jnp.where(eye, gram, 0.0), axis=2, keepdims=True), axis=1, keepdims=True
    )
    left = gram + jnp.where(eye, ridge_scale * (trace / RANK), 0.0)
    right = jnp.where(eye, 1.0, 0.0)
    for step in range(RANK):
        column = jnp.sum(jnp.where(col == step, left, 0.0), axis=2, keepdims=True)
        pivot = column[:, step : step + 1, :]
        factor = jnp.where(row[:, :, :1] > step, column / pivot, 0.0)
        right = right - factor * right[:, step : step + 1, :]
        left = left - factor * left[:, step : step + 1, :]
    diagonal = jnp.sum(jnp.where(eye, left, 0.0), axis=2, keepdims=True)
    return (right * lax.rsqrt(diagonal)).reshape(COLS, COLS)


def inverse_kernel(scale, gram_ref, gram_got_ref, inverse_ref):
    inverse_ref[...] = lower_inverse((gram_ref[...] + gram_got_ref[...]) * scale)


def inverse_of(gram, gram_got, scale):
    return pl.pallas_call(
        functools.partial(inverse_kernel, scale),
        out_shape=jax.ShapeDtypeStruct((COLS, COLS), f32),
        compiler_params=params(),
        name="inverse",
    )(gram, gram_got)


def normalize_kernel(total_ref, got_ref, inverse_ref, *refs):
    basis_ref = refs[-1]
    total = total_ref[...] + got_ref[...].astype(f32)
    basis_ref[...] = lax.dot_general(
        total,
        inverse_ref[...],
        (((0,), (1,)), ((), ())),
        precision=lax.Precision.HIGHEST,
        preferred_element_type=f32,
    ).astype(bf16)


def normalize(total, got, inverse, ties):
    vmem = pl.BlockSpec(memory_space=pltpu.VMEM)
    return pl.pallas_call(
        normalize_kernel,
        in_specs=[vmem] * 3 + tied(ties),
        out_specs=vmem,
        out_shape=jax.ShapeDtypeStruct((total.shape[1], COLS), bf16),
        compiler_params=params(),
        name="normalize",
    )(total, got, inverse, *ties)


def turned_by(count, step):
    return [(i, (i + step) % count) for i in range(count)]


def crossed(count, step):
    return [(i, i ^ step) for i in range(count)]


def swap_cores(part, n_width):
    return lax.ppermute(part, "width", crossed(n_width, 1))


class Reduction:
    def __init__(self, sends, keep, n_grp, n_dp, even=False):
        self.parts = self.own = None
        self.steps = self.run(sends, keep, n_grp, n_dp, even)
        next(self.steps)

    def advance(self):
        return next(self.steps, None) or []

    def run(self, sends, keep, n_grp, n_dp, even):
        rows = keep.shape[0]
        got = [
            lax.ppermute(
                sends[at * rows : (at + 1) * rows], "dp", turned_by(n_dp, at + 1)
            )
            for at in range(n_dp - 1)
        ]
        yield []
        total = keep
        for part in got:
            total = total + part.astype(f32)
        step = 1
        while step < n_grp:
            sent = total.astype(bf16)
            got = lax.ppermute(sent, "grp", crossed(n_grp, step))
            yield [sent]
            total = (sent.astype(f32) if even else total) + got.astype(f32)
            step *= 2
        own = self.own = total.astype(bf16)
        others = [
            lax.ppermute(own, "dp", turned_by(n_dp, n_dp - 1 - at)) for at in range(n_dp - 1)
        ]
        yield [own]
        self.parts = others + [own]


def advance_all(reductions):
    ties = []
    for reduction in reductions:
        if reduction.parts is None:
            ties += reduction.advance()
    return ties


def finish(reduction, reductions):
    ties = []
    while reduction.parts is None:
        ties = advance_all(reductions)
    return ties


def after(array, others):
    return lax.optimization_barrier((array, *others))[0] if others else array


def sum_shares(keep, sends, n_width):
    total = keep
    for at, send in enumerate(sends):
        total = total + lax.ppermute(send, "width", crossed(n_width, at + 1)).astype(f32)
    return total


def sum_scatter(part, axes, count):
    pieces = lax.all_to_all(part.astype(bf16), axes, 0, 0, tiled=True)
    pieces = pieces.reshape((count, part.shape[0] // count) + part.shape[1:])
    return jnp.sum(pieces.astype(f32), axis=0)


def gather_rows(piece, axes, count):
    copies = jnp.broadcast_to(piece[None], (count,) + piece.shape)
    whole = lax.all_to_all(copies, axes, 0, 0, tiled=True)
    return whole.reshape((count * piece.shape[0],) + piece.shape[1:])


def make_per_device(n_grp, n_dp, n_width):
    n_gd = n_grp * n_dp

    def per_device(
        query_out, query_in, eigen_out, eigen_in, eigvals, start, grads_out, gate_pre, up_pre
    ):
        dp = lax.axis_index("dp")
        along = lax.axis_index("width")
        core = along % CORES
        place = jnp.stack([dp, core, along]).astype(jnp.int32)
        scale = 1.0 / (eigen_out.shape[0] * n_gd)
        rows_out = eigvals.shape[0]

        def reduction(sends, keep, even=False):
            return Reduction(sends, keep, n_grp, n_dp, even)

        def sum_gram(parts):
            gram = gram_of(parts)
            total = gram
            for step in range(1, n_dp):
                total = total + lax.ppermute(gram, "dp", turned_by(n_dp, step))
            return sum_but_last(total, f32)

        def sum_but_last(total, kind):
            step = 2
            while True:
                got = lax.ppermute(total.astype(kind), "width", crossed(n_width, step))
                step *= 2
                if step >= n_width:
                    return total, got
                total = total + got.astype(f32)

        pieces = list(rotate_out(place, query_out, eigen_out, n_dp))
        own_pieces, their_pieces = pieces[: 2 * PIECES], pieces[2 * PIECES :]
        theirs_in, mine_in = rotate_in(place, query_in, eigen_in, pieces[:1])
        turning = [reduction(own_pieces[0], own_pieces[1])]
        their_pieces = [swap_cores(each, n_width) for each in their_pieces]
        theirs_in = swap_cores(theirs_in, n_width)
        total_in, got = sum_but_last(mine_in + theirs_in, bf16)
        rot_in = (total_in + got.astype(f32)).astype(bf16)
        hops = []
        count = CORES * PIECES
        for at in range(1, count):
            hops = advance_all(turning)
            sends, keep = (own_pieces + their_pieces)[2 * at : 2 * at + 2]
            turning.append(reduction(after(sends, hops[:1]), keep))
        eig_theirs = swap_cores(after(eigvals, [theirs_in, their_pieces[-1], *hops[:1]]), n_width)
        hidden = (jax.nn.silu(gate_pre.astype(f32)) * up_pre.astype(f32)).astype(bf16)
        basis = lax.dynamic_slice_in_dim(start, core * COLS, COLS, 1)
        rotated = []
        for iteration in range(ITERS):
            summing, ties = [], [hidden] if iteration == 0 else []
            for at in range(count):
                if iteration == 0:
                    finish(turning[at], turning)
                    eig = eigvals if at < PIECES else eig_theirs
                    block, sends, keep = form_piece(
                        place, turning[at].parts, rot_in, eig, basis, at % PIECES, ties
                    )
                    rotated.append(block)
                    ties = advance_all(turning)
                else:
                    sends, keep = image_piece(basis, rotated[at], n_dp, ties)
                    ties = []
                ties += advance_all(summing)
                summing.append(reduction(sends, keep))
            sums = gram = None
            for at in range(count):
                finish(summing[at], summing)
                if gram is None and all(each.own is not None for each in summing):
                    gram, gram_got = sum_gram([each.own for each in summing])
                    ties = ties + [gram]
                elif gram is not None and at == count - 1:
                    inverse = inverse_of(gram, gram_got, scale)
                    ties = ties + [inverse]
                    if iteration == ITERS - 1:
                        images = [part for each in summing for part in each.parts]
                        mine_out, theirs_out = turn(place, inverse, images, n_dp)
                        theirs_out = swap_cores(theirs_out, n_width)
                        ties = ties + [mine_out]
                sums = return_piece(summing[at].parts, rotated[at], sums, ties)
                ties = advance_all(summing)
            total, got = sum_but_last(sums[0], bf16)
            ties = []
            if iteration == ITERS - 1:
                keep_out, *sends_out = factor_out(
                    place, eigen_out, mine_out, after(theirs_out, [total]), n_width
                )
                ties = [keep_out]
            basis = normalize(total, got, inverse, ties)

        their_basis = swap_cores(basis, n_width)
        pieces = factor_in(place, eigen_in, basis, their_basis, n_dp)
        share = sum_shares(keep_out, sends_out, n_width).astype(bf16)
        factors, hops = [], []
        for at in range(FACTOR_PIECES):
            sends, keep = pieces[2 * at : 2 * at + 2]
            factors.append(reduction(after(sends, hops[:1]), keep, even=True))
            hops = advance_all(factors)
        for each in factors:
            finish(each, factors)
        parts = [part for each in factors for part in each.parts]
        in_factor, keep_in, *sends_in = project(place, hidden, parts, n_dp, n_width)

        piece_rows = share.shape[0]
        gathered = gather_rows(share, GD, n_gd)
        mixed = lax.all_to_all(gathered, "width", 0, 0, tiled=True)
        out_factor = (
            mixed.reshape(n_width, n_gd // n_width, piece_rows, NQ * RANK)
            .transpose(1, 0, 2, 3)
            .reshape(rows_out, NQ * RANK)
        )
        proj_out = jnp.dot(grads_out, out_factor, preferred_element_type=f32)
        proj_out = sum_scatter(proj_out, "width", n_width)
        proj_in = sum_shares(keep_in, sends_in, n_width)
        scores = (proj_out * proj_in).reshape(proj_out.shape[0], NQ, RANK).sum(axis=2).T
        return (scores, out_factor, in_factor)

    return per_device


def solution(mesh):
    return jax.shard_map(
        make_per_device(mesh.shape["grp"], mesh.shape["dp"], mesh.shape["width"]),
        mesh=mesh,
        in_specs=(
            P(None, GD),
            P(None, "width"),
            P(GD, "width"),
            P("width", GD),
            P("width", GD),
            P(GD, None),
            P(GD, "width"),
            P(GD, "width"),
            P(GD, "width"),
        ),
        out_specs=(P(None, GD + ("width",)), P("width", None), P("width", None)),
        check_vma=False,
    )
```

```python
import functools

import jax
import jax.numpy as jnp
from jax import lax
from jax.experimental import pallas as pl
from jax.experimental.pallas import tpu as pltpu
from jax.sharding import PartitionSpec as P

NQ = 16
QTOK = 32
RANK = 16
ITERS = 2
CORES = 2
NG = NQ // CORES
COLS = NG * RANK
TOKS = NG * QTOK
LANES = 256
PIECES = 2
BLOCK = 4
FACTOR_PIECES = 4

damping = 0.01
ridge_scale = 1e-06

GD = ("grp", "dp")
f32 = jnp.float32
bf16 = jnp.bfloat16


def params():
    return pltpu.CompilerParams(vmem_limit_bytes=48 * 1024 * 1024)


def chunks(extent):
    return [(at, min(LANES, extent - at)) for at in range(0, extent, LANES)]


def cost(shape, columns):
    count = shape[0] * shape[1] * shape[2]
    return pl.CostEstimate(
        flops=2 * count * columns, bytes_accessed=2 * count, transcendentals=0
    )


def write_image(image, send_ref, keep_ref):
    part, parts = pl.program_id(0), pl.num_programs(0)
    last = pl.program_id(1) == pl.num_programs(1) - 1

    @pl.when(last & (part < parts - 1))
    def _():
        send_ref[...] = image[...].astype(bf16)

    @pl.when(last & (part == parts - 1))
    def _():
        keep_ref[...] = image[...]


def form_kernel(n_dp, n_ties, place_ref, *refs):
    out_refs = refs[:n_dp]
    in_ref, eig_ref, basis_ref = refs[n_dp : n_dp + 3]
    rotated_ref, send_ref, keep_ref, weight, left, image = refs[n_dp + 3 + n_ties :]
    part, first = pl.program_id(0), pl.program_id(1) * BLOCK
    rows, cols = eig_ref.shape

    @pl.when(first == 0)
    def _():
        weight[...] = 1.0 / (eig_ref[...] + damping)

    for at in range(n_dp):

        @pl.when((first == 0) & (part == at))
        def _(at=at):
            for query in range(NG):
                left[query] = out_refs[at][:, query * QTOK : (query + 1) * QTOK]

    for at in range(BLOCK):
        query = first + at
        own = left[query]
        right = in_ref[pl.ds(pl.multiple_of(query * QTOK, QTOK), QTOK), :]
        for begin, width in chunks(cols):
            span = slice(begin, begin + width)
            block = jnp.dot(own, right[:, span], preferred_element_type=f32)
            rotated_ref[at, :, span] = (block * weight[:, span]).astype(bf16)
        product = jnp.dot(rotated_ref[at], basis_ref[...], preferred_element_type=f32)
        lane = lax.broadcasted_iota(jnp.int32, (rows, COLS), 1) // RANK
        image[...] = jnp.where(lane == query, product, image[...])
    write_image(image, send_ref, keep_ref)


def tied(ties):
    return [pl.BlockSpec(memory_space=pl.ANY)] * len(ties)


def form_piece(place, out_parts, rot_in, eigvals, basis, piece, ties):
    n_dp = len(out_parts)
    rows = out_parts[0].shape[0]
    cols = rot_in.shape[1]

    def eig_block(part, query, place_ref):
        return piece * n_dp + lax.rem(place_ref[0] + 1 + part, n_dp), 0

    def fixed(shape):
        return pl.BlockSpec(shape, lambda part, query, _: (0, 0))

    shape = (NG, n_dp * rows, cols)
    return pl.pallas_call(
        functools.partial(form_kernel, n_dp, len(ties)),
        grid_spec=pltpu.PrefetchScalarGridSpec(
            num_scalar_prefetch=1,
            grid=(n_dp, NG // BLOCK),
            in_specs=[fixed((rows, TOKS))] * n_dp
            + [
                fixed((TOKS, cols)),
                pl.BlockSpec((rows, cols), eig_block),
                fixed((cols, COLS)),
            ]
            + tied(ties),
            out_specs=[
                pl.BlockSpec((BLOCK, rows, cols), lambda part, query, _: (query, part, 0)),
                pl.BlockSpec(
                    (rows, COLS), lambda part, query, _: (jnp.minimum(part, n_dp - 2), 0)
                ),
                fixed((rows, COLS)),
            ],
            scratch_shapes=[
                pltpu.VMEM((rows, cols), f32),
                pltpu.VMEM((NG, rows, QTOK), bf16),
                pltpu.VMEM((rows, COLS), f32),
            ],
        ),
        out_shape=[
            jax.ShapeDtypeStruct(shape, bf16),
            jax.ShapeDtypeStruct(((n_dp - 1) * rows, COLS), bf16),
            jax.ShapeDtypeStruct((rows, COLS), f32),
        ],
        compiler_params=params(),
        cost_estimate=cost(shape, 400),
        name="form",
    )(place, *out_parts, rot_in, eigvals, basis, *ties)


def stream(rotated_ref, buffers, sems, parts, begin, body):
    rows = buffers.shape[1]
    sets = NG // BLOCK

    def copy(turn, slot):
        part, query = turn // sets, lax.rem(turn, sets) * BLOCK + slot
        return pltpu.make_async_copy(
            rotated_ref.at[query, pl.ds(pl.multiple_of(part * rows, rows), rows), :],
            buffers.at[slot],
            sems.at[slot],
        )

    for slot in range(BLOCK):
        copy(0, slot).start()

    @pl.loop(0, parts * sets)
    def _(turn):
        part, first = turn // sets, lax.rem(turn, sets) * BLOCK

        @pl.when(first == 0)
        def _():
            begin(part)

        for slot in range(BLOCK):
            copy(turn, slot).wait()
            body(part, first + slot, buffers[slot])

            @pl.when(turn + 1 < parts * sets)
            def _(slot=slot):
                copy(turn + 1, slot).start()


def stream_scratch(rows, cols):
    return [pltpu.VMEM((BLOCK, rows, cols), bf16), pltpu.SemaphoreType.DMA((BLOCK,))]


def image_kernel(n_dp, n_ties, basis_ref, rotated_ref, *refs):
    send_ref, keep_ref, buffers, sems, image = refs[n_ties:]
    rows = image.shape[0]
    lane = lax.broadcasted_iota(jnp.int32, (rows, COLS), 1) // RANK

    def body(part, query, block):
        product = jnp.dot(block, basis_ref[...], preferred_element_type=f32)
        image[...] = jnp.where(lane == query, product, image[...])

        @pl.when((query == NG - 1) & (part < n_dp - 1))
        def _():
            send_ref[pl.ds(pl.multiple_of(part * rows, rows), rows), :] = image[...].astype(bf16)

        @pl.when((query == NG - 1) & (part == n_dp - 1))
        def _():
            keep_ref[...] = image[...]

    stream(rotated_ref, buffers, sems, n_dp, lambda part: None, body)


def image_piece(basis, rotated, n_dp, ties):
    _, rows, cols = rotated.shape
    rows = rows // n_dp
    vmem = pl.BlockSpec(memory_space=pltpu.VMEM)
    return pl.pallas_call(
        functools.partial(image_kernel, n_dp, len(ties)),
        in_specs=[vmem] + tied([rotated, *ties]),
        out_specs=[vmem, vmem],
        out_shape=[
            jax.ShapeDtypeStruct(((n_dp - 1) * rows, COLS), bf16),
            jax.ShapeDtypeStruct((rows, COLS), f32),
        ],
        scratch_shapes=stream_scratch(rows, cols) + [pltpu.VMEM((rows, COLS), f32)],
        compiler_params=params(),
        cost_estimate=cost(rotated.shape, 256),
        name="image",
    )(basis, rotated, *ties)


def return_kernel(n_dp, first, n_ties, *refs):
    image_refs, rotated_ref = refs[:n_dp], refs[n_dp]
    total_ref, rounded_ref, buffers, sems, turned = refs[-5:]
    total_ref[...] = jnp.zeros_like(total_ref) if first else refs[n_dp + 1][...]

    def begin(part):
        for at in range(n_dp):

            @pl.when(part == at)
            def _(at=at):
                turned[...] = image_refs[at][...].astype(f32).T.astype(bf16)

    def body(part, query, block):
        own = pl.ds(pl.multiple_of(query * RANK, RANK), RANK)
        total_ref[own, :] += jnp.dot(turned[own, :], block, preferred_element_type=f32)

    stream(rotated_ref, buffers, sems, n_dp, begin, body)
    rounded_ref[...] = total_ref[...].astype(bf16)


def return_piece(images, rotated, before, ties):
    n_dp = len(images)
    _, rows, cols = rotated.shape
    rows = rows // n_dp
    vmem = pl.BlockSpec(memory_space=pltpu.VMEM)
    before = [] if before is None else [before]
    return pl.pallas_call(
        functools.partial(return_kernel, n_dp, not before, len(ties)),
        in_specs=[vmem] * n_dp + tied([rotated]) + [vmem] * len(before) + tied(ties),
        out_specs=[vmem, vmem],
        out_shape=[
            jax.ShapeDtypeStruct((COLS, cols), f32),
            jax.ShapeDtypeStruct((COLS, cols), bf16),
        ],
        scratch_shapes=stream_scratch(rows, cols) + [pltpu.VMEM((COLS, rows), bf16)],
        compiler_params=params(),
        cost_estimate=cost(rotated.shape, 256),
        name="returned",
    )(*images, rotated, *before, *ties)


def rotate_out_kernel(n_dp, place_ref, query_ref, eigen_ref, *refs):
    turned = refs[-1]
    width = eigen_ref.shape[1]
    rows = width // (PIECES * n_dp)
    for side, index in ((0, place_ref[1]), (1, 1 - place_ref[1])):
        queries = query_ref[pl.ds(pl.multiple_of(index * TOKS, TOKS), TOKS), :]
        for begin, count in chunks(width):
            product = jnp.dot(
                queries, eigen_ref[:, begin : begin + count], preferred_element_type=f32
            )
            turned[begin : begin + count, :] = product.T
        for piece in range(PIECES):
            send_ref, keep_ref = refs[2 * (side * PIECES + piece) :][:2]
            for part in range(n_dp):
                at = piece * n_dp + lax.rem(place_ref[0] + 1 + part, n_dp)
                taken = turned[pl.ds(pl.multiple_of(at * rows, rows), rows), :]
                if part < n_dp - 1:
                    send_ref[part * rows : (part + 1) * rows, :] = taken.astype(bf16)
                else:
                    keep_ref[...] = taken.astype(keep_ref.dtype)


def rotate_out(place, query_out, eigen_out, n_dp):
    width = eigen_out.shape[1]
    rows = width // (PIECES * n_dp)
    shapes = []
    for kind in (f32, bf16):
        for _ in range(PIECES):
            shapes.append(jax.ShapeDtypeStruct(((n_dp - 1) * rows, TOKS), bf16))
            shapes.append(jax.ShapeDtypeStruct((rows, TOKS), kind))
    vmem = pl.BlockSpec(memory_space=pltpu.VMEM)
    return pl.pallas_call(
        functools.partial(rotate_out_kernel, n_dp),
        in_specs=[pl.BlockSpec(memory_space=pltpu.SMEM), vmem, vmem],
        out_specs=[vmem] * len(shapes),
        out_shape=shapes,
        scratch_shapes=[pltpu.VMEM((width, TOKS), f32)],
        compiler_params=params(),
        name="rotate_out",
    )(place, query_out, eigen_out)


def rotate_in_kernel(other, place_ref, query_ref, eigen_ref, *refs):
    index = 1 - place_ref[1] if other else place_ref[1]
    rows = pl.ds(pl.multiple_of(index * TOKS, TOKS), TOKS)
    refs[-1][...] = jnp.dot(query_ref[rows, :], eigen_ref[...], preferred_element_type=f32)


def rotate_in(place, query_in, eigen_in, other, ties):
    depth, cols = eigen_in.shape
    width = LANES if cols % LANES == 0 else cols
    return pl.pallas_call(
        functools.partial(rotate_in_kernel, other),
        grid_spec=pltpu.PrefetchScalarGridSpec(
            num_scalar_prefetch=1,
            grid=(cols // width,),
            in_specs=[
                pl.BlockSpec(query_in.shape, lambda at, _: (0, 0)),
                pl.BlockSpec((depth, width), lambda at, _: (0, at)),
            ]
            + tied(ties),
            out_specs=pl.BlockSpec((TOKS, width), lambda at, _: (0, at)),
        ),
        out_shape=jax.ShapeDtypeStruct((TOKS, cols), f32),
        compiler_params=params(),
        cost_estimate=pl.CostEstimate(
            flops=2 * depth * cols * TOKS, bytes_accessed=2 * depth * cols, transcendentals=0
        ),
        name="rotate_in",
    )(place, query_in, eigen_in, *ties)


def side_by_side(place_ref, mine, theirs):
    return jnp.where(
        place_ref[1] == 0,
        jnp.concatenate([mine, theirs], axis=1),
        jnp.concatenate([theirs, mine], axis=1),
    )


def factor_kernel(n_dp, n_ties, place_ref, eigen_ref, mine_ref, theirs_ref, *refs):
    *out_refs, cols = refs[n_ties:]
    step = pl.program_id(0)
    rows = eigen_ref.shape[0]

    @pl.when(step == 0)
    def _():
        cols[...] = side_by_side(place_ref, mine_ref[...], theirs_ref[...])

    product = jnp.dot(eigen_ref[...], cols[...], preferred_element_type=f32)
    for piece in range(FACTOR_PIECES):
        send_ref, keep_ref = out_refs[2 * piece : 2 * piece + 2]
        for part in range(n_dp):

            @pl.when(step == piece * n_dp + part)
            def _(part=part, send_ref=send_ref, keep_ref=keep_ref):
                if part < n_dp - 1:
                    send_ref[part * rows : (part + 1) * rows, :] = product.astype(bf16)
                else:
                    keep_ref[...] = product


def factor_in(place, eigen_in, mine, theirs, n_dp, ties):
    rows, depth = eigen_in.shape
    rows = rows // (FACTOR_PIECES * n_dp)
    width = CORES * COLS
    fixed = pl.BlockSpec((depth, COLS), lambda at, _: (0, 0))

    def eigen_block(at, place_ref):
        return at // n_dp * n_dp + lax.rem(place_ref[0] + 1 + at % n_dp, n_dp), 0

    shapes = [
        jax.ShapeDtypeStruct(((n_dp - 1) * rows, width), bf16),
        jax.ShapeDtypeStruct((rows, width), f32),
    ] * FACTOR_PIECES
    return pl.pallas_call(
        functools.partial(factor_kernel, n_dp, len(ties)),
        grid_spec=pltpu.PrefetchScalarGridSpec(
            num_scalar_prefetch=1,
            grid=(FACTOR_PIECES * n_dp,),
            in_specs=[pl.BlockSpec((rows, depth), eigen_block), fixed, fixed] + tied(ties),
            out_specs=[pl.BlockSpec(each.shape, lambda at, _: (0, 0)) for each in shapes],
            scratch_shapes=[pltpu.VMEM((depth, width), bf16)],
        ),
        out_shape=shapes,
        compiler_params=params(),
        name="factor_in",
    )(place, eigen_in, mine, theirs, *ties)


def write_shares(place_ref, total, keep_ref, send_refs):
    rows = keep_ref.shape[0]
    for step in range(len(send_refs) + 1):
        other = place_ref[2] ^ step
        share = total[pl.ds(pl.multiple_of(other * rows, rows), rows), :]
        if step == 0:
            keep_ref[...] = share
        else:
            send_refs[step - 1][...] = share.astype(bf16)


def factor_out_kernel(place_ref, eigen_ref, mine_ref, theirs_ref, keep_ref, *refs):
    *send_refs, total = refs
    total[...] = jnp.dot(
        eigen_ref[...],
        side_by_side(place_ref, mine_ref[...], theirs_ref[...]),
        preferred_element_type=f32,
    )
    write_shares(place_ref, total, keep_ref, send_refs)


def shares(rows, width, n_width):
    shape = (rows // n_width, width)
    return [jax.ShapeDtypeStruct(shape, f32)] + [jax.ShapeDtypeStruct(shape, bf16)] * (n_width - 1)


def factor_out(place, eigen_out, mine, theirs, n_width):
    rows = eigen_out.shape[0]
    width = CORES * COLS
    vmem = pl.BlockSpec(memory_space=pltpu.VMEM)
    return pl.pallas_call(
        factor_out_kernel,
        in_specs=[pl.BlockSpec(memory_space=pltpu.SMEM)] + [vmem] * 3,
        out_specs=[vmem] * n_width,
        out_shape=shares(rows, width, n_width),
        scratch_shapes=[pltpu.VMEM((rows, width), f32)],
        compiler_params=params(),
        name="factor_out",
    )(place, eigen_out, mine, theirs)


def project_kernel(n_dp, n_parts, place_ref, hidden_ref, *refs):
    part_refs = refs[:n_parts]
    factor_ref, keep_ref, *send_refs, total = refs[n_parts:]
    rows = part_refs[0].shape[0]
    for at, ref in enumerate(part_refs):
        owner = lax.rem(place_ref[0] + 1 + at % n_dp, n_dp)
        begin = (at // n_dp * n_dp + owner) * rows
        factor_ref[pl.ds(pl.multiple_of(begin, 8), rows), :] = ref[...]
    total[...] = jnp.dot(hidden_ref[...], factor_ref[...], preferred_element_type=f32)
    write_shares(place_ref, total, keep_ref, send_refs)


def project(place, hidden, parts, n_dp, n_width):
    tokens, depth = hidden.shape
    width = parts[0].shape[1]
    vmem = pl.BlockSpec(memory_space=pltpu.VMEM)
    return pl.pallas_call(
        functools.partial(project_kernel, n_dp, len(parts)),
        in_specs=[pl.BlockSpec(memory_space=pltpu.SMEM)] + [vmem] * (1 + len(parts)),
        out_specs=[vmem] * (1 + n_width),
        out_shape=[jax.ShapeDtypeStruct((depth, width), bf16)] + shares(tokens, width, n_width),
        scratch_shapes=[pltpu.VMEM((tokens, width), f32)],
        compiler_params=params(),
        name="project",
    )(place, hidden, *parts)


def turn_kernel(n_dp, place_ref, inverse_ref, *refs):
    *image_refs, mine_ref, theirs_ref = refs
    rows = image_refs[0].shape[0]
    for at, ref in enumerate(image_refs):
        out_ref = mine_ref if at < PIECES * n_dp else theirs_ref
        owner = lax.rem(place_ref[0] + 1 + at % n_dp, n_dp)
        begin = (at // n_dp % PIECES * n_dp + owner) * rows
        out_ref[pl.ds(pl.multiple_of(begin, rows), rows), :] = lax.dot_general(
            ref[...].astype(f32),
            inverse_ref[...],
            (((1,), (1,)), ((), ())),
            precision=lax.Precision.HIGHEST,
            preferred_element_type=f32,
        ).astype(bf16)


def turn(place, inverse, images, n_dp):
    out = jax.ShapeDtypeStruct((PIECES * n_dp * images[0].shape[0], COLS), bf16)
    vmem = pl.BlockSpec(memory_space=pltpu.VMEM)
    return pl.pallas_call(
        functools.partial(turn_kernel, n_dp),
        in_specs=[pl.BlockSpec(memory_space=pltpu.SMEM)] + [vmem] * (1 + len(images)),
        out_specs=[vmem, vmem],
        out_shape=[out, out],
        compiler_params=params(),
        name="turn",
    )(place, inverse, *images)


def gram_kernel(*refs):
    gram = jnp.zeros((COLS, COLS), f32)
    for ref in refs[:-1]:
        image = ref[...]
        gram = gram + lax.dot_general(
            image, image, (((0,), (0,)), ((), ())), preferred_element_type=f32
        )
    refs[-1][...] = gram


def gram_of(images):
    return pl.pallas_call(
        gram_kernel,
        out_shape=jax.ShapeDtypeStruct((COLS, COLS), f32),
        compiler_params=params(),
        name="gram",
    )(*images)


def lower_inverse(gram):
    shape = (NG, RANK, COLS)
    row = lax.broadcasted_iota(jnp.int32, shape, 1)
    lane = lax.broadcasted_iota(jnp.int32, shape, 2)
    same = lane // RANK == lax.broadcasted_iota(jnp.int32, shape, 0)
    col = lane % RANK
    eye = same & (col == row)
    gram = jnp.where(same, gram.reshape(shape), 0.0)
    trace = jnp.sum(
        jnp.sum(jnp.where(eye, gram, 0.0), axis=2, keepdims=True), axis=1, keepdims=True
    )
    left = gram + jnp.where(eye, ridge_scale * (trace / RANK), 0.0)
    right = jnp.where(eye, 1.0, 0.0)
    for step in range(RANK):
        column = jnp.sum(jnp.where(col == step, left, 0.0), axis=2, keepdims=True)
        pivot = column[:, step : step + 1, :]
        factor = jnp.where(row[:, :, :1] > step, column / pivot, 0.0)
        right = right - factor * right[:, step : step + 1, :]
        left = left - factor * left[:, step : step + 1, :]
    diagonal = jnp.sum(jnp.where(eye, left, 0.0), axis=2, keepdims=True)
    return (right * lax.rsqrt(diagonal)).reshape(COLS, COLS)


def inverse_kernel(scale, gram_ref, gram_got_ref, inverse_ref):
    inverse_ref[...] = lower_inverse((gram_ref[...] + gram_got_ref[...]) * scale)


def inverse_of(gram, gram_got, scale):
    return pl.pallas_call(
        functools.partial(inverse_kernel, scale),
        out_shape=jax.ShapeDtypeStruct((COLS, COLS), f32),
        compiler_params=params(),
        name="inverse",
    )(gram, gram_got)


def normalize_kernel(total_ref, got_ref, inverse_ref, *refs):
    basis_ref = refs[-1]
    total = total_ref[...] + got_ref[...].astype(f32)
    basis_ref[...] = lax.dot_general(
        total,
        inverse_ref[...],
        (((0,), (1,)), ((), ())),
        precision=lax.Precision.HIGHEST,
        preferred_element_type=f32,
    ).astype(bf16)


def normalize(total, got, inverse, ties):
    vmem = pl.BlockSpec(memory_space=pltpu.VMEM)
    return pl.pallas_call(
        normalize_kernel,
        in_specs=[vmem] * 3 + tied(ties),
        out_specs=vmem,
        out_shape=jax.ShapeDtypeStruct((total.shape[1], COLS), bf16),
        compiler_params=params(),
        name="normalize",
    )(total, got, inverse, *ties)


def turned_by(count, step):
    return [(i, (i + step) % count) for i in range(count)]


def crossed(count, step):
    return [(i, i ^ step) for i in range(count)]


def swap_cores(part, n_width):
    return lax.ppermute(part, "width", crossed(n_width, 1))


class Reduction:
    def __init__(self, sends, keep, n_grp, n_dp, even=False):
        self.parts = self.own = None
        self.steps = self.run(sends, keep, n_grp, n_dp, even)
        next(self.steps)

    def advance(self):
        return next(self.steps, None) or []

    def run(self, sends, keep, n_grp, n_dp, even):
        rows = keep.shape[0]
        got = [
            lax.ppermute(
                sends[at * rows : (at + 1) * rows], "dp", turned_by(n_dp, at + 1)
            )
            for at in range(n_dp - 1)
        ]
        yield []
        total = keep
        for part in got:
            total = total + part.astype(f32)
        step, odd = 1, lax.axis_index("grp") % 2
        while step < n_grp:
            if even and step == 2:
                total = lax.dynamic_slice_in_dim(total, odd * (rows // 2), rows // 2, 0)
            sent = total.astype(bf16)
            got = lax.ppermute(sent, "grp", crossed(n_grp, step))
            yield [sent]
            total = (sent.astype(f32) if even else total) + got.astype(f32)
            step *= 2
        own = self.own = total.astype(bf16)
        if even and n_grp > 2:
            got = lax.ppermute(own, "grp", crossed(n_grp, 1))
            yield [own]
            own = jnp.where(
                odd == 0, jnp.concatenate([own, got]), jnp.concatenate([got, own])
            )
        others = [
            lax.ppermute(own, "dp", turned_by(n_dp, n_dp - 1 - at)) for at in range(n_dp - 1)
        ]
        yield [own]
        self.parts = others + [own]


def advance_all(reductions):
    ties = []
    for reduction in reductions:
        if reduction.parts is None:
            ties += reduction.advance()
    return ties


def finish(reduction, reductions):
    ties = []
    while reduction.parts is None:
        ties = advance_all(reductions)
    return ties


def after(array, others):
    return lax.optimization_barrier((array, *others))[0] if others else array


def sum_shares(keep, sends, n_width):
    total = keep
    for at, send in enumerate(sends):
        total = total + lax.ppermute(send, "width", crossed(n_width, at + 1)).astype(f32)
    return total


def sum_scatter(part, axes, count):
    pieces = lax.all_to_all(part.astype(bf16), axes, 0, 0, tiled=True)
    pieces = pieces.reshape((count, part.shape[0] // count) + part.shape[1:])
    return jnp.sum(pieces.astype(f32), axis=0)


def gather_rows(piece, axes, count):
    copies = jnp.broadcast_to(piece[None], (count,) + piece.shape)
    whole = lax.all_to_all(copies, axes, 0, 0, tiled=True)
    return whole.reshape((count * piece.shape[0],) + piece.shape[1:])


def make_per_device(n_grp, n_dp, n_width):
    n_gd = n_grp * n_dp

    def per_device(
        query_out, query_in, eigen_out, eigen_in, eigvals, start, grads_out, gate_pre, up_pre
    ):
        dp = lax.axis_index("dp")
        along = lax.axis_index("width")
        core = along % CORES
        place = jnp.stack([dp, core, along]).astype(jnp.int32)
        scale = 1.0 / (eigen_out.shape[0] * n_gd)
        rows_out = eigvals.shape[0]

        def reduction(sends, keep, even=False):
            return Reduction(sends, keep, n_grp, n_dp, even)

        def sum_gram(parts):
            gram = gram_of(parts)
            total = gram
            for step in range(1, n_dp):
                total = total + lax.ppermute(gram, "dp", turned_by(n_dp, step))
            step = 2
            while True:
                got = lax.ppermute(total, "width", crossed(n_width, step))
                step *= 2
                if step >= n_width:
                    return total, got
                total = total + got

        def sum_but_last(total, sent=None):
            step = 2
            while True:
                sent = total.astype(bf16) if sent is None else sent
                got = lax.ppermute(sent, "width", crossed(n_width, step))
                step *= 2
                if step >= n_width:
                    return total, sent, got
                total, sent = total + got.astype(f32), None

        pieces = list(rotate_out(place, query_out, eigen_out, n_dp))
        own_pieces, their_pieces = pieces[: 2 * PIECES], pieces[2 * PIECES :]
        theirs_in = rotate_in(place, query_in, eigen_in, True, pieces[:1])
        mine_in = rotate_in(place, query_in, eigen_in, False, [theirs_in])
        theirs_in = swap_cores(theirs_in, n_width)
        total_in, sent_in, got = sum_but_last(mine_in + theirs_in)
        rot_in = (total_in + got.astype(f32)).astype(bf16)
        turning = [reduction(own_pieces[0], after(own_pieces[1], [sent_in]))]
        their_pieces = [swap_cores(each, n_width) for each in their_pieces]
        hops = []
        count = CORES * PIECES
        for at in range(1, count):
            hops = advance_all(turning)
            sends, keep = (own_pieces + their_pieces)[2 * at : 2 * at + 2]
            turning.append(reduction(after(sends, hops[:1]), keep))
        finish(turning[0], turning)
        eig_sent = after(eigvals, [rot_in, *turning[0].parts])
        eig_theirs = swap_cores(eig_sent, n_width)
        hidden = (jax.nn.silu(gate_pre.astype(f32)) * up_pre.astype(f32)).astype(bf16)
        basis = lax.dynamic_slice_in_dim(start, core * COLS, COLS, 1)
        rotated = []
        for iteration in range(ITERS):
            summing, ties = [], [hidden] if iteration == 0 else []
            for at in range(count):
                if iteration == 0:
                    finish(turning[at], turning)
                    eig = eigvals if at < PIECES else eig_theirs
                    block, sends, keep = form_piece(
                        place, turning[at].parts, rot_in, eig, basis, at % PIECES, ties
                    )
                    rotated.append(block)
                    ties = advance_all(turning)
                else:
                    sends, keep = image_piece(basis, rotated[at], n_dp, ties)
                    ties = []
                ties += advance_all(summing)
                summing.append(reduction(sends, keep))
            total = gram = None
            for at in range(count):
                finish(summing[at], summing)
                if gram is None and all(each.own is not None for each in summing):
                    gram, gram_got = sum_gram([each.own for each in summing])
                    ties = ties + [gram]
                elif gram is not None and at == count - 1:
                    inverse = inverse_of(gram, gram_got, scale)
                    ties = ties + [inverse]
                    if iteration == ITERS - 1:
                        images = [part for each in summing for part in each.parts]
                        mine_out, theirs_out = turn(place, inverse, images, n_dp)
                        theirs_out = swap_cores(theirs_out, n_width)
                        ties = ties + [mine_out]
                total, sent = return_piece(summing[at].parts, rotated[at], total, ties)
                ties = advance_all(summing)
            total, sent, got = sum_but_last(total, sent)
            ties = []
            if iteration == ITERS - 1:
                keep_out, *sends_out = factor_out(
                    place, eigen_out, mine_out, after(theirs_out, [sent]), n_width
                )
                ties = [keep_out]
            basis = normalize(total, got, inverse, ties)

        their_basis = swap_cores(basis, n_width)
        share = sum_shares(keep_out, sends_out, n_width).astype(bf16)
        pieces = factor_in(place, eigen_in, basis, their_basis, n_dp, [share])
        factors, hops = [], []
        for at in range(FACTOR_PIECES):
            sends, keep = pieces[2 * at : 2 * at + 2]
            factors.append(reduction(after(sends, hops[:1]), keep, even=True))
            hops = advance_all(factors)
        for each in factors:
            finish(each, factors)
        parts = [part for each in factors for part in each.parts]
        in_factor, keep_in, *sends_in = project(place, hidden, parts, n_dp, n_width)

        piece_rows = share.shape[0]
        gathered = gather_rows(share, GD, n_gd)
        mixed = lax.all_to_all(gathered, "width", 0, 0, tiled=True)
        out_factor = (
            mixed.reshape(n_width, n_gd // n_width, piece_rows, NQ * RANK)
            .transpose(1, 0, 2, 3)
            .reshape(rows_out, NQ * RANK)
        )
        proj_out = jnp.dot(grads_out, out_factor, preferred_element_type=f32)
        proj_out = sum_scatter(proj_out, "width", n_width)
        proj_in = sum_shares(keep_in, sends_in, n_width)
        scores = (proj_out * proj_in).reshape(proj_out.shape[0], NQ, RANK).sum(axis=2).T
        return (scores, out_factor, in_factor)

    return per_device


def solution(mesh):
    return jax.shard_map(
        make_per_device(mesh.shape["grp"], mesh.shape["dp"], mesh.shape["width"]),
        mesh=mesh,
        in_specs=(
            P(None, GD),
            P(None, "width"),
            P(GD, "width"),
            P("width", GD),
            P("width", GD),
            P(GD, None),
            P(GD, "width"),
            P(GD, "width"),
            P(GD, "width"),
        ),
        out_specs=(P(None, GD + ("width",)), P("width", None), P("width", None)),
        check_vma=False,
    )
```

```python
import functools

import jax
import jax.numpy as jnp
from jax import lax
from jax.experimental import pallas as pl
from jax.experimental.pallas import tpu as pltpu
from jax.sharding import PartitionSpec as P

NQ = 16
QTOK = 32
RANK = 16
ITERS = 2
CORES = 2
NG = NQ // CORES
COLS = NG * RANK
TOKS = NG * QTOK
LANES = 256
PIECES = 2
BLOCK = 4
IMAGE_BLOCK = 2
FACTOR_PIECES = 4

damping = 0.01
ridge_scale = 1e-06

GD = ("grp", "dp")
f32 = jnp.float32
bf16 = jnp.bfloat16


def params():
    return pltpu.CompilerParams(vmem_limit_bytes=48 * 1024 * 1024)


def chunks(extent):
    return [(at, min(LANES, extent - at)) for at in range(0, extent, LANES)]


def cost(shape, columns):
    count = shape[0] * shape[1] * shape[2]
    return pl.CostEstimate(
        flops=2 * count * columns, bytes_accessed=2 * count, transcendentals=0
    )


def tied(ties):
    return [pl.BlockSpec(memory_space=pl.ANY)] * len(ties)


def form_kernel(n_parts, n_ties, place_ref, *refs):
    out_refs = refs[:n_parts]
    in_ref, eig_ref, basis_ref = refs[n_parts : n_parts + 3]
    rotated_ref, image_ref, weight, left, image = refs[n_parts + 3 + n_ties :]
    part, first = pl.program_id(0), pl.program_id(1) * BLOCK
    rows, cols = eig_ref.shape

    @pl.when(first == 0)
    def _():
        weight[...] = 1.0 / (eig_ref[...] + damping)

    for at in range(n_parts):

        @pl.when((first == 0) & (part == at))
        def _(at=at):
            for query in range(NG):
                left[query] = out_refs[at][:, query * QTOK : (query + 1) * QTOK]

    lane = lax.broadcasted_iota(jnp.int32, (rows, COLS), 1) // RANK
    for at in range(BLOCK):
        query = first + at
        own = left[query]
        right = in_ref[pl.ds(pl.multiple_of(query * QTOK, QTOK), QTOK), :]
        for begin, width in chunks(cols):
            span = slice(begin, begin + width)
            block = jnp.dot(own, right[:, span], preferred_element_type=f32)
            rotated_ref[at, :, span] = (block * weight[:, span]).astype(bf16)
        product = jnp.dot(rotated_ref[at], basis_ref[...], preferred_element_type=f32)
        image[...] = jnp.where(lane == query, product, image[...])

    @pl.when(first == NG - BLOCK)
    def _():
        image_ref[...] = image[...].astype(image_ref.dtype)


def form_parts(place, out_parts, rot_in, eigvals, basis, at, n_dp, kind, ties):
    n_parts = len(out_parts)
    rows = out_parts[0].shape[0]
    cols = rot_in.shape[1]

    def eig_block(part, query, place_ref):
        return at // n_dp * n_dp + lax.rem(place_ref[0] + 1 + at % n_dp + part, n_dp), 0

    def fixed(shape):
        return pl.BlockSpec(shape, lambda part, query, _: (0, 0))

    shape = (NG, n_parts * rows, cols)
    return pl.pallas_call(
        functools.partial(form_kernel, n_parts, len(ties)),
        grid_spec=pltpu.PrefetchScalarGridSpec(
            num_scalar_prefetch=1,
            grid=(n_parts, NG // BLOCK),
            in_specs=[fixed((rows, TOKS))] * n_parts
            + [
                fixed((TOKS, cols)),
                pl.BlockSpec((rows, cols), eig_block),
                fixed((cols, COLS)),
            ]
            + tied(ties),
            out_specs=[
                pl.BlockSpec((BLOCK, rows, cols), lambda part, query, _: (query, part, 0)),
                pl.BlockSpec((rows, COLS), lambda part, query, _: (part, 0)),
            ],
            scratch_shapes=[
                pltpu.VMEM((rows, cols), f32),
                pltpu.VMEM((NG, rows, QTOK), bf16),
                pltpu.VMEM((rows, COLS), f32),
            ],
        ),
        out_shape=[
            jax.ShapeDtypeStruct(shape, bf16),
            jax.ShapeDtypeStruct((n_parts * rows, COLS), kind),
        ],
        compiler_params=params(),
        cost_estimate=cost(shape, 400),
        name="form",
    )(place, *out_parts, rot_in, eigvals, basis, *ties)


def stream(rotated_ref, buffers, sems, parts, begin, body):
    rows = buffers.shape[1]
    sets = NG // BLOCK

    def copy(turn, slot):
        part, query = turn // sets, lax.rem(turn, sets) * BLOCK + slot
        return pltpu.make_async_copy(
            rotated_ref.at[query, pl.ds(pl.multiple_of(part * rows, rows), rows), :],
            buffers.at[slot],
            sems.at[slot],
        )

    for slot in range(BLOCK):
        copy(0, slot).start()

    @pl.loop(0, parts * sets)
    def _(turn):
        part, first = turn // sets, lax.rem(turn, sets) * BLOCK

        @pl.when(first == 0)
        def _():
            begin(part)

        for slot in range(BLOCK):
            copy(turn, slot).wait()
            body(part, first + slot, buffers[slot])

            @pl.when(turn + 1 < parts * sets)
            def _(slot=slot):
                copy(turn + 1, slot).start()


def stream_scratch(rows, cols):
    return [pltpu.VMEM((BLOCK, rows, cols), bf16), pltpu.SemaphoreType.DMA((BLOCK,))]


def image_kernel(n_ties, basis_ref, rotated_ref, *refs):
    image_ref, image = refs[n_ties:]
    count, rows, cols = rotated_ref.shape
    first = pl.program_id(1) * count
    product = jnp.dot(
        rotated_ref[...].reshape(count * rows, cols), basis_ref[...], preferred_element_type=f32
    )
    lane = lax.broadcasted_iota(jnp.int32, (rows, COLS), 1) // RANK
    for at in range(count):
        image[...] = jnp.where(
            lane == first + at, product[at * rows : (at + 1) * rows], image[...]
        )

    @pl.when(first == NG - count)
    def _():
        image_ref[...] = image[...].astype(image_ref.dtype)


def image_parts(basis, rotated, rows, kind, ties):
    _, total, cols = rotated.shape
    return pl.pallas_call(
        functools.partial(image_kernel, len(ties)),
        grid=(total // rows, NG // IMAGE_BLOCK),
        in_specs=[
            pl.BlockSpec((cols, COLS), lambda part, query: (0, 0)),
            pl.BlockSpec((IMAGE_BLOCK, rows, cols), lambda part, query: (query, part, 0)),
        ]
        + tied(ties),
        out_specs=pl.BlockSpec((rows, COLS), lambda part, query: (part, 0)),
        out_shape=jax.ShapeDtypeStruct((total, COLS), kind),
        scratch_shapes=[pltpu.VMEM((rows, COLS), f32)],
        compiler_params=params(),
        cost_estimate=cost(rotated.shape, 256),
        name="image",
    )(basis, rotated, *ties)


def return_kernel(n_parts, first, *refs):
    image_refs, rotated_ref = refs[:n_parts], refs[n_parts]
    total_ref, rounded_ref, buffers, sems, turned = refs[-5:]
    total_ref[...] = jnp.zeros_like(total_ref) if first else refs[n_parts + 1][...]

    def begin(part):
        for at in range(n_parts):

            @pl.when(part == at)
            def _(at=at):
                turned[...] = image_refs[at][...].astype(f32).T.astype(bf16)

    def body(part, query, block):
        own = pl.ds(pl.multiple_of(query * RANK, RANK), RANK)
        total_ref[own, :] += jnp.dot(turned[own, :], block, preferred_element_type=f32)

    stream(rotated_ref, buffers, sems, n_parts, begin, body)
    rounded_ref[...] = total_ref[...].astype(bf16)


def return_parts(images, rotated, before, ties):
    n_parts = len(images)
    _, rows, cols = rotated.shape
    rows = rows // n_parts
    vmem = pl.BlockSpec(memory_space=pltpu.VMEM)
    before = [] if before is None else [before]
    return pl.pallas_call(
        functools.partial(return_kernel, n_parts, not before),
        in_specs=[vmem] * n_parts + tied([rotated]) + [vmem] * len(before) + tied(ties),
        out_specs=[vmem, vmem],
        out_shape=[
            jax.ShapeDtypeStruct((COLS, cols), f32),
            jax.ShapeDtypeStruct((COLS, cols), bf16),
        ],
        scratch_shapes=stream_scratch(rows, cols) + [pltpu.VMEM((COLS, rows), bf16)],
        compiler_params=params(),
        cost_estimate=cost(rotated.shape, 256),
        name="returned",
    )(*images, rotated, *before, *ties)


def rotate_out_kernel(n_dp, place_ref, query_ref, eigen_ref, *refs):
    turned = refs[-1]
    width = eigen_ref.shape[1]
    rows = width // (PIECES * n_dp)
    for side, index in ((0, place_ref[1]), (1, 1 - place_ref[1])):
        queries = query_ref[pl.ds(pl.multiple_of(index * TOKS, TOKS), TOKS), :]
        for begin, count in chunks(width):
            product = jnp.dot(
                queries, eigen_ref[:, begin : begin + count], preferred_element_type=f32
            )
            turned[begin : begin + count, :] = product.T
        for piece in range(PIECES):
            send_ref, keep_ref = refs[2 * (side * PIECES + piece) :][:2]
            for part in range(n_dp):
                at = piece * n_dp + lax.rem(place_ref[0] + 1 + part, n_dp)
                taken = turned[pl.ds(pl.multiple_of(at * rows, rows), rows), :]
                if part < n_dp - 1:
                    send_ref[part * rows : (part + 1) * rows, :] = taken.astype(bf16)
                else:
                    keep_ref[...] = taken.astype(keep_ref.dtype)


def rotate_out(place, query_out, eigen_out, n_dp):
    width = eigen_out.shape[1]
    rows = width // (PIECES * n_dp)
    shapes = []
    for kind in (f32, bf16):
        for _ in range(PIECES):
            shapes.append(jax.ShapeDtypeStruct(((n_dp - 1) * rows, TOKS), bf16))
            shapes.append(jax.ShapeDtypeStruct((rows, TOKS), kind))
    vmem = pl.BlockSpec(memory_space=pltpu.VMEM)
    return pl.pallas_call(
        functools.partial(rotate_out_kernel, n_dp),
        in_specs=[pl.BlockSpec(memory_space=pltpu.SMEM), vmem, vmem],
        out_specs=[vmem] * len(shapes),
        out_shape=shapes,
        scratch_shapes=[pltpu.VMEM((width, TOKS), f32)],
        compiler_params=params(),
        name="rotate_out",
    )(place, query_out, eigen_out)


def rotate_in_kernel(n_ties, place_ref, query_ref, eigen_ref, *refs):
    theirs_ref, mine_ref, product = refs[n_ties:]
    product[...] = jnp.dot(query_ref[...], eigen_ref[...], preferred_element_type=f32)
    for out_ref, index in ((theirs_ref, 1 - place_ref[1]), (mine_ref, place_ref[1])):
        out_ref[...] = product[pl.ds(pl.multiple_of(index * TOKS, TOKS), TOKS), :]


def rotate_in(place, query_in, eigen_in, ties):
    depth, cols = eigen_in.shape
    width = LANES if cols % LANES == 0 else cols
    out = jax.ShapeDtypeStruct((TOKS, cols), f32)
    return pl.pallas_call(
        functools.partial(rotate_in_kernel, len(ties)),
        grid_spec=pltpu.PrefetchScalarGridSpec(
            num_scalar_prefetch=1,
            grid=(cols // width,),
            in_specs=[
                pl.BlockSpec(query_in.shape, lambda at, _: (0, 0)),
                pl.BlockSpec((depth, width), lambda at, _: (0, at)),
            ]
            + tied(ties),
            out_specs=[pl.BlockSpec((TOKS, width), lambda at, _: (0, at))] * 2,
            scratch_shapes=[pltpu.VMEM((CORES * TOKS, width), f32)],
        ),
        out_shape=[out, out],
        compiler_params=params(),
        cost_estimate=pl.CostEstimate(
            flops=2 * depth * cols * CORES * TOKS, bytes_accessed=2 * depth * cols, transcendentals=0
        ),
        name="rotate_in",
    )(place, query_in, eigen_in, *ties)


def side_by_side(place_ref, mine, theirs):
    return jnp.where(
        place_ref[1] == 0,
        jnp.concatenate([mine, theirs], axis=1),
        jnp.concatenate([theirs, mine], axis=1),
    )


def factor_kernel(n_dp, n_ties, place_ref, eigen_ref, mine_ref, theirs_ref, *refs):
    *out_refs, cols = refs[n_ties:]
    step = pl.program_id(0)
    rows = eigen_ref.shape[0]

    @pl.when(step == 0)
    def _():
        cols[...] = side_by_side(place_ref, mine_ref[...], theirs_ref[...])

    product = jnp.dot(eigen_ref[...], cols[...], preferred_element_type=f32)
    for piece in range(FACTOR_PIECES):
        send_ref, keep_ref = out_refs[2 * piece : 2 * piece + 2]
        for part in range(n_dp):

            @pl.when(step == piece * n_dp + part)
            def _(part=part, send_ref=send_ref, keep_ref=keep_ref):
                if part < n_dp - 1:
                    send_ref[part * rows : (part + 1) * rows, :] = product.astype(bf16)
                else:
                    keep_ref[...] = product


def factor_in(place, eigen_in, mine, theirs, n_dp, ties):
    rows, depth = eigen_in.shape
    rows = rows // (FACTOR_PIECES * n_dp)
    width = CORES * COLS
    fixed = pl.BlockSpec((depth, COLS), lambda at, _: (0, 0))

    def eigen_block(at, place_ref):
        return at // n_dp * n_dp + lax.rem(place_ref[0] + 1 + at % n_dp, n_dp), 0

    shapes = [
        jax.ShapeDtypeStruct(((n_dp - 1) * rows, width), bf16),
        jax.ShapeDtypeStruct((rows, width), f32),
    ] * FACTOR_PIECES
    return pl.pallas_call(
        functools.partial(factor_kernel, n_dp, len(ties)),
        grid_spec=pltpu.PrefetchScalarGridSpec(
            num_scalar_prefetch=1,
            grid=(FACTOR_PIECES * n_dp,),
            in_specs=[pl.BlockSpec((rows, depth), eigen_block), fixed, fixed] + tied(ties),
            out_specs=[pl.BlockSpec(each.shape, lambda at, _: (0, 0)) for each in shapes],
            scratch_shapes=[pltpu.VMEM((depth, width), bf16)],
        ),
        out_shape=shapes,
        compiler_params=params(),
        name="factor_in",
    )(place, eigen_in, mine, theirs, *ties)


def write_shares(place_ref, total, keep_ref, send_refs):
    rows = keep_ref.shape[0]
    for step in range(len(send_refs) + 1):
        other = place_ref[2] ^ step
        share = total[pl.ds(pl.multiple_of(other * rows, rows), rows), :]
        if step == 0:
            keep_ref[...] = share
        else:
            send_refs[step - 1][...] = share.astype(bf16)


def factor_out_kernel(place_ref, eigen_ref, mine_ref, theirs_ref, keep_ref, *refs):
    *send_refs, total = refs
    total[...] = jnp.dot(
        eigen_ref[...],
        side_by_side(place_ref, mine_ref[...], theirs_ref[...]),
        preferred_element_type=f32,
    )
    write_shares(place_ref, total, keep_ref, send_refs)


def shares(rows, width, n_width):
    shape = (rows // n_width, width)
    return [jax.ShapeDtypeStruct(shape, f32)] + [jax.ShapeDtypeStruct(shape, bf16)] * (n_width - 1)


def factor_out(place, eigen_out, mine, theirs, n_width):
    rows = eigen_out.shape[0]
    width = CORES * COLS
    vmem = pl.BlockSpec(memory_space=pltpu.VMEM)
    return pl.pallas_call(
        factor_out_kernel,
        in_specs=[pl.BlockSpec(memory_space=pltpu.SMEM)] + [vmem] * 3,
        out_specs=[vmem] * n_width,
        out_shape=shares(rows, width, n_width),
        scratch_shapes=[pltpu.VMEM((rows, width), f32)],
        compiler_params=params(),
        name="factor_out",
    )(place, eigen_out, mine, theirs)


def project_kernel(n_dp, n_parts, place_ref, hidden_ref, *refs):
    part_refs = refs[:n_parts]
    factor_ref, keep_ref, *send_refs, total = refs[n_parts:]
    rows = part_refs[0].shape[0]
    for at, ref in enumerate(part_refs):
        owner = lax.rem(place_ref[0] + 1 + at % n_dp, n_dp)
        begin = (at // n_dp * n_dp + owner) * rows
        factor_ref[pl.ds(pl.multiple_of(begin, 8), rows), :] = ref[...]
    total[...] = jnp.dot(hidden_ref[...], factor_ref[...], preferred_element_type=f32)
    write_shares(place_ref, total, keep_ref, send_refs)


def project(place, hidden, parts, n_dp, n_width):
    tokens, depth = hidden.shape
    width = parts[0].shape[1]
    vmem = pl.BlockSpec(memory_space=pltpu.VMEM)
    return pl.pallas_call(
        functools.partial(project_kernel, n_dp, len(parts)),
        in_specs=[pl.BlockSpec(memory_space=pltpu.SMEM)] + [vmem] * (1 + len(parts)),
        out_specs=[vmem] * (1 + n_width),
        out_shape=[jax.ShapeDtypeStruct((depth, width), bf16)] + shares(tokens, width, n_width),
        scratch_shapes=[pltpu.VMEM((tokens, width), f32)],
        compiler_params=params(),
        name="project",
    )(place, hidden, *parts)


def turn_kernel(n_dp, place_ref, inverse_ref, *refs):
    *image_refs, mine_ref, theirs_ref = refs
    rows = image_refs[0].shape[0]
    for at, ref in enumerate(image_refs):
        out_ref = mine_ref if at < PIECES * n_dp else theirs_ref
        owner = lax.rem(place_ref[0] + 1 + at % n_dp, n_dp)
        begin = (at // n_dp % PIECES * n_dp + owner) * rows
        out_ref[pl.ds(pl.multiple_of(begin, rows), rows), :] = lax.dot_general(
            ref[...].astype(f32),
            inverse_ref[...],
            (((1,), (1,)), ((), ())),
            precision=lax.Precision.HIGHEST,
            preferred_element_type=f32,
        ).astype(bf16)


def turn(place, inverse, images, n_dp):
    out = jax.ShapeDtypeStruct((PIECES * n_dp * images[0].shape[0], COLS), bf16)
    vmem = pl.BlockSpec(memory_space=pltpu.VMEM)
    return pl.pallas_call(
        functools.partial(turn_kernel, n_dp),
        in_specs=[pl.BlockSpec(memory_space=pltpu.SMEM)] + [vmem] * (1 + len(images)),
        out_specs=[vmem, vmem],
        out_shape=[out, out],
        compiler_params=params(),
        name="turn",
    )(place, inverse, *images)


def gram_kernel(*refs):
    gram = jnp.zeros((COLS, COLS), f32)
    for ref in refs[:-1]:
        image = ref[...]
        gram = gram + lax.dot_general(
            image, image, (((0,), (0,)), ((), ())), preferred_element_type=f32
        )
    refs[-1][...] = gram


def gram_of(images):
    return pl.pallas_call(
        gram_kernel,
        out_shape=jax.ShapeDtypeStruct((COLS, COLS), f32),
        compiler_params=params(),
        name="gram",
    )(*images)


def lower_inverse(gram):
    shape = (NG, RANK, COLS)
    row = lax.broadcasted_iota(jnp.int32, shape, 1)
    lane = lax.broadcasted_iota(jnp.int32, shape, 2)
    same = lane // RANK == lax.broadcasted_iota(jnp.int32, shape, 0)
    col = lane % RANK
    eye = same & (col == row)
    gram = jnp.where(same, gram.reshape(shape), 0.0)
    trace = jnp.sum(
        jnp.sum(jnp.where(eye, gram, 0.0), axis=2, keepdims=True), axis=1, keepdims=True
    )
    left = gram + jnp.where(eye, ridge_scale * (trace / RANK), 0.0)
    right = jnp.where(eye, 1.0, 0.0)
    for step in range(RANK):
        column = jnp.sum(jnp.where(col == step, left, 0.0), axis=2, keepdims=True)
        pivot = column[:, step : step + 1, :]
        factor = jnp.where(row[:, :, :1] > step, column / pivot, 0.0)
        right = right - factor * right[:, step : step + 1, :]
        left = left - factor * left[:, step : step + 1, :]
    diagonal = jnp.sum(jnp.where(eye, left, 0.0), axis=2, keepdims=True)
    return (right * lax.rsqrt(diagonal)).reshape(COLS, COLS)


def inverse_kernel(scale, gram_ref, gram_got_ref, inverse_ref):
    inverse_ref[...] = lower_inverse((gram_ref[...] + gram_got_ref[...]) * scale)


def inverse_of(gram, gram_got, scale):
    return pl.pallas_call(
        functools.partial(inverse_kernel, scale),
        out_shape=jax.ShapeDtypeStruct((COLS, COLS), f32),
        compiler_params=params(),
        name="inverse",
    )(gram, gram_got)


def normalize_kernel(total_ref, got_ref, inverse_ref, *refs):
    basis_ref = refs[-1]
    total = total_ref[...] + got_ref[...].astype(f32)
    basis_ref[...] = lax.dot_general(
        total,
        inverse_ref[...],
        (((0,), (1,)), ((), ())),
        precision=lax.Precision.HIGHEST,
        preferred_element_type=f32,
    ).astype(bf16)


def normalize(total, got, inverse, ties):
    vmem = pl.BlockSpec(memory_space=pltpu.VMEM)
    return pl.pallas_call(
        normalize_kernel,
        in_specs=[vmem] * 3 + tied(ties),
        out_specs=vmem,
        out_shape=jax.ShapeDtypeStruct((total.shape[1], COLS), bf16),
        compiler_params=params(),
        name="normalize",
    )(total, got, inverse, *ties)


def turned_by(count, step):
    return [(i, (i + step) % count) for i in range(count)]


def crossed(count, step):
    return [(i, i ^ step) for i in range(count)]


def swap_cores(part, n_width):
    return lax.ppermute(part, "width", crossed(n_width, 1))


def after(array, others):
    return lax.optimization_barrier((array, *others))[0] if others else array


class Reduction:
    def __init__(self, sends, n_grp, n_dp, even=False, keep=None):
        self.parts = self.own = None
        self.keep = keep
        self.steps = self.run(sends, n_grp, n_dp, even)
        next(self.steps)

    def advance(self, others):
        try:
            return self.steps.send(others)
        except StopIteration:
            return []

    def run(self, sends, n_grp, n_dp, even):
        rows = sends.shape[0] // (n_dp - 1)
        got = [
            lax.ppermute(sends[at * rows : (at + 1) * rows], "dp", turned_by(n_dp, at + 1))
            for at in range(n_dp - 1)
        ]
        others = yield []
        total = after(self.keep, others)
        for part in got:
            total = total + part.astype(f32)
        step, odd = 1, lax.axis_index("grp") % 2
        while step < n_grp:
            if even and step == 2:
                total = lax.dynamic_slice_in_dim(total, odd * (rows // 2), rows // 2, 0)
            sent = total.astype(bf16)
            got = lax.ppermute(sent, "grp", crossed(n_grp, step))
            others = yield [sent]
            total = (sent.astype(f32) if even else total) + after(got, others).astype(f32)
            step *= 2
        own = total.astype(bf16)
        if even and n_grp > 2:
            got = lax.ppermute(own, "grp", crossed(n_grp, 1))
            others = yield [own]
            got = after(got, others)
            own = jnp.where(
                odd == 0, jnp.concatenate([own, got]), jnp.concatenate([got, own])
            )
        self.own = own
        parts = [
            lax.ppermute(own, "dp", turned_by(n_dp, n_dp - 1 - at)) for at in range(n_dp - 1)
        ]
        yield [own]
        self.parts = parts + [own]


class Steps:
    def __init__(self, steps):
        self.steps, self.count = steps, 0

    def advance(self, others):
        self.count += 1
        try:
            return self.steps.send(others if self.count > 1 else None)
        except StopIteration:
            return []


def boundary(others, reductions):
    ties = []
    for reduction in reductions:
        if reduction.parts is None and reduction.keep is not None:
            hop = reduction.advance(others)
            ties += hop
            others = hop or others
    return ties


def sum_shares(keep, sends, n_width):
    total = keep
    for at, send in enumerate(sends):
        total = total + lax.ppermute(send, "width", crossed(n_width, at + 1)).astype(f32)
    return total


def sum_scatter(part, axes, count):
    pieces = lax.all_to_all(part.astype(bf16), axes, 0, 0, tiled=True)
    pieces = pieces.reshape((count, part.shape[0] // count) + part.shape[1:])
    return jnp.sum(pieces.astype(f32), axis=0)


def gather_rows(piece, axes, count):
    copies = jnp.broadcast_to(piece[None], (count,) + piece.shape)
    whole = lax.all_to_all(copies, axes, 0, 0, tiled=True)
    return whole.reshape((count * piece.shape[0],) + piece.shape[1:])


def make_per_device(n_grp, n_dp, n_width):
    n_gd = n_grp * n_dp

    def per_device(
        query_out, query_in, eigen_out, eigen_in, eigvals, start, grads_out, gate_pre, up_pre
    ):
        dp = lax.axis_index("dp")
        along = lax.axis_index("width")
        core = along % CORES
        place = jnp.stack([dp, core, along]).astype(jnp.int32)
        scale = 1.0 / (eigen_out.shape[0] * n_gd)
        rows_out = eigvals.shape[0]

        def last_hop(total, sent=None):
            step = 2
            while True:
                sent = total.astype(bf16) if sent is None else sent
                got = lax.ppermute(sent, "width", crossed(n_width, step))
                step *= 2
                if step >= n_width:
                    return total, sent, got
                total, sent = total + got.astype(f32), None

        def output_side(summing, last):
            gram = gram_of([each.own for each in summing])
            got = [lax.ppermute(gram, "dp", turned_by(n_dp, at)) for at in range(1, n_dp)]
            others = yield [gram]
            gram = after(gram, others)
            for each in got:
                gram = gram + each
            step = 2
            while True:
                got = lax.ppermute(gram, "width", crossed(n_width, step))
                step *= 2
                if step >= n_width:
                    break
                gram = gram + got
            others = yield [gram]
            inverse = found["inverse"] = inverse_of(after(gram, others), got, scale)
            if not last:
                return
            images = [part for each in summing for part in each.parts]
            mine, theirs = turn(place, inverse, images, n_dp)
            theirs = swap_cores(theirs, n_width)
            others = yield [mine]
            keep, *sends = factor_out(place, eigen_out, after(mine, others), theirs, n_width)
            sends = [
                lax.ppermute(send, "width", crossed(n_width, at + 1))
                for at, send in enumerate(sends)
            ]
            others = yield [keep]
            share = after(keep, others)
            for send in sends:
                share = share + send.astype(f32)
            share = share.astype(bf16)
            piece_rows = share.shape[0]
            gathered = gather_rows(share, GD, n_gd)
            others = yield [share]
            mixed = lax.all_to_all(after(gathered, others), "width", 0, 0, tiled=True)
            others = yield [gathered]
            out_factor = found["out_factor"] = (
                after(mixed, others)
                .reshape(n_width, n_gd // n_width, piece_rows, NQ * RANK)
                .transpose(1, 0, 2, 3)
                .reshape(rows_out, NQ * RANK)
            )
            proj_out = jnp.dot(grads_out, out_factor, preferred_element_type=f32)
            found["proj_out"] = sum_scatter(proj_out, "width", n_width)

        found = {}
        count = CORES * PIECES
        pieces = list(rotate_out(place, query_out, eigen_out, n_dp))
        own_pieces, their_pieces = pieces[: 2 * PIECES], pieces[2 * PIECES :]
        turning = [Reduction(own_pieces[0], n_grp, n_dp, keep=own_pieces[1])]
        theirs_in, mine_in = rotate_in(place, query_in, eigen_in, pieces[:1])
        theirs_in = swap_cores(theirs_in, n_width)
        their_pieces = [swap_cores(each, n_width) for each in their_pieces]
        hops = boundary([mine_in], turning)
        total_in, sent_in, got_in = last_hop(after(mine_in, hops) + theirs_in)
        last = [sent_in]
        for at in range(1, count):
            sends, keep = (own_pieces + their_pieces)[2 * at : 2 * at + 2]
            turning.append(Reduction(after(sends, last), n_grp, n_dp, keep=keep))
            last = boundary(last, turning)[:1] or last
        hidden = (jax.nn.silu(gate_pre.astype(f32)) * up_pre.astype(f32)).astype(bf16)
        rot_in = (total_in + got_in.astype(f32)).astype(bf16)
        basis = lax.dynamic_slice_in_dim(start, core * COLS, COLS, 1)
        rotated, eig_theirs, ties = [], None, [hidden]
        for iteration in range(ITERS):
            summing = []
            found.clear()
            for at in range(count):
                if iteration == 0:
                    while turning[at].parts is None:
                        last = boundary(last, turning) or last
                    if eig_theirs is None:
                        eig_sent = after(eigvals, [rot_in, *turning[0].parts])
                        eig_theirs = swap_cores(eig_sent, n_width)
                    rotated.append([None, None])
                for side, kind in ((0, bf16), (1, f32)):
                    if iteration == 0:
                        parts = turning[at].parts
                        block, image = form_parts(
                            place,
                            parts[-1:] if side else parts[:-1],
                            rot_in,
                            eigvals if at < PIECES else eig_theirs,
                            basis,
                            at % PIECES * n_dp + side * (n_dp - 1),
                            n_dp,
                            kind,
                            ties,
                        )
                        rotated[at][side] = block
                    else:
                        rows = rotated[at][1].shape[1]
                        image = image_parts(basis, rotated[at][side], rows, kind, ties)
                    if side:
                        summing[at].keep = image
                    last = [image]
                    ties = boundary(last, turning + summing)
                    if not side:
                        summing.append(Reduction(image, n_grp, n_dp))
            total = path = None
            for at in range(count):
                while summing[at].parts is None:
                    last = boundary(last, summing) or last
                for side in range(2):
                    parts = summing[at].parts
                    total, sent = return_parts(
                        parts[-1:] if side else parts[:-1], rotated[at][side], total, ties
                    )
                    last = [sent]
                    ties = boundary(last, summing)
                    if path is None and all(each.own is not None for each in summing):
                        path = Steps(output_side(summing, iteration == ITERS - 1))
                    if path is not None and path.count < 5:
                        ties += path.advance(last)
            while "inverse" not in found:
                path.advance([])
            total, sent, got = last_hop(total, sent)
            basis = normalize(total, got, found["inverse"], ties)
            ties = []

        their_basis = swap_cores(basis, n_width)
        pieces = factor_in(place, eigen_in, basis, their_basis, n_dp, [])
        factors, last = [], [pieces[0]]
        for at in range(FACTOR_PIECES):
            sends, keep = pieces[2 * at : 2 * at + 2]
            factors.append(Reduction(after(sends, last[:1]), n_grp, n_dp, True, keep))
            last = boundary(last, factors)
            if at % 2:
                path.advance(last)
        while any(each.parts is None for each in factors):
            last = boundary(last, factors) or last
        parts = [part for each in factors for part in each.parts]
        in_factor, keep_in, *sends_in = project(place, hidden, parts, n_dp, n_width)
        while "proj_out" not in found:
            path.advance([])
        proj_in = sum_shares(keep_in, sends_in, n_width)
        scores = (found["proj_out"] * proj_in).reshape(proj_in.shape[0], NQ, RANK).sum(axis=2).T
        return (scores, found["out_factor"], in_factor)

    return per_device


def solution(mesh):
    return jax.shard_map(
        make_per_device(mesh.shape["grp"], mesh.shape["dp"], mesh.shape["width"]),
        mesh=mesh,
        in_specs=(
            P(None, GD),
            P(None, "width"),
            P(GD, "width"),
            P("width", GD),
            P("width", GD),
            P(GD, None),
            P(GD, "width"),
            P(GD, "width"),
            P(GD, "width"),
        ),
        out_specs=(P(None, GD + ("width",)), P("width", None), P("width", None)),
        check_vma=False,
    )
```

```python
import functools

import jax
import jax.numpy as jnp
from jax import lax
from jax.experimental import pallas as pl
from jax.experimental.pallas import tpu as pltpu
from jax.sharding import PartitionSpec as P

NQ = 16
QTOK = 32
RANK = 16
ITERS = 2
CORES = 2
NG = NQ // CORES
COLS = NG * RANK
TOKS = NG * QTOK
LANES = 256
PIECES = 2
BLOCK = 4
FACTOR_PIECES = 2

damping = 0.01
ridge_scale = 1e-06

GD = ("grp", "dp")
f32 = jnp.float32
bf16 = jnp.bfloat16


def params():
    return pltpu.CompilerParams(vmem_limit_bytes=48 * 1024 * 1024)


def chunks(extent):
    return [(at, min(LANES, extent - at)) for at in range(0, extent, LANES)]


def cost(shape, columns):
    count = shape[0] * shape[1] * shape[2]
    return pl.CostEstimate(
        flops=2 * count * columns, bytes_accessed=2 * count, transcendentals=0
    )


def tied(ties):
    return [pl.BlockSpec(memory_space=pl.ANY)] * len(ties)


def write_image(image, n_keep, refs):
    part = pl.program_id(0)
    done = pl.program_id(1) == pl.num_programs(1) - 1

    if n_keep:

        @pl.when(done & (part == 0))
        def _():
            refs[0][...] = image[...]

    if len(refs) > n_keep:

        @pl.when(done & (part >= n_keep))
        def _():
            refs[-1][...] = image[...].astype(bf16)


def image_outputs(n_keep, n_send, rows):
    shapes, specs = [], []
    if n_keep:
        shapes.append(jax.ShapeDtypeStruct((rows, COLS), f32))
        specs.append(pl.BlockSpec((rows, COLS), lambda part, query, *_: (0, 0)))
    if n_send:
        shapes.append(jax.ShapeDtypeStruct((n_send * rows, COLS), bf16))
        specs.append(
            pl.BlockSpec(
                (rows, COLS), lambda part, query, *_: (jnp.maximum(part - n_keep, 0), 0)
            )
        )
    return shapes, specs


def add_images(product, first, rows, image):
    lane = lax.broadcasted_iota(jnp.int32, (rows, COLS), 1) // RANK
    for at in range(BLOCK):
        image[...] = jnp.where(
            lane == first + at, product[at * rows : (at + 1) * rows], image[...]
        )


def form_kernel(n_keep, n_parts, n_ties, place_ref, *refs):
    out_refs = refs[:n_parts]
    in_ref, eig_ref, basis_ref = refs[n_parts : n_parts + 3]
    rotated_ref, *image_refs, weight, left, image = refs[n_parts + 3 + n_ties :]
    part, first = pl.program_id(0), pl.program_id(1) * BLOCK
    rows, cols = eig_ref.shape

    @pl.when(first == 0)
    def _():
        weight[...] = 1.0 / (eig_ref[...] + damping)

    for at in range(n_parts):

        @pl.when((first == 0) & (part == at))
        def _(at=at):
            for query in range(NG):
                left[query] = out_refs[at][:, query * QTOK : (query + 1) * QTOK]

    for at in range(BLOCK):
        query = first + at
        own = left[query]
        right = in_ref[pl.ds(pl.multiple_of(query * QTOK, QTOK), QTOK), :]
        for begin, width in chunks(cols):
            span = slice(begin, begin + width)
            block = jnp.dot(own, right[:, span], preferred_element_type=f32)
            rotated_ref[at, :, span] = (block * weight[:, span]).astype(bf16)
    product = jnp.dot(
        rotated_ref[...].reshape(BLOCK * rows, cols), basis_ref[...], preferred_element_type=f32
    )
    add_images(product, first, rows, image)
    write_image(image, n_keep, image_refs)


def form_parts(place, kept, sent, pieces, rot_in, eigvals, basis, n_dp, ties):
    n_keep, n_parts = len(kept), len(kept) + len(sent)
    rows = (kept + sent)[0].shape[0]
    cols = rot_in.shape[1]
    keep_piece, send_piece = pieces

    def eig_block(part, query, place_ref):
        at = send_piece * n_dp + lax.rem(place_ref[0] + 1 + part + n_dp - n_keep, n_dp)
        return jnp.where(part < n_keep, keep_piece * n_dp + place_ref[0], at), 0

    def fixed(shape):
        return pl.BlockSpec(shape, lambda part, query, _: (0, 0))

    shape = (NG, n_parts * rows, cols)
    shapes, specs = image_outputs(n_keep, len(sent), rows)
    return pl.pallas_call(
        functools.partial(form_kernel, n_keep, n_parts, len(ties)),
        grid_spec=pltpu.PrefetchScalarGridSpec(
            num_scalar_prefetch=1,
            grid=(n_parts, NG // BLOCK),
            in_specs=[fixed((rows, TOKS))] * n_parts
            + [
                fixed((TOKS, cols)),
                pl.BlockSpec((rows, cols), eig_block),
                fixed((cols, COLS)),
            ]
            + tied(ties),
            out_specs=[
                pl.BlockSpec((BLOCK, rows, cols), lambda part, query, _: (query, part, 0))
            ]
            + specs,
            scratch_shapes=[
                pltpu.VMEM((rows, cols), f32),
                pltpu.VMEM((NG, rows, QTOK), bf16),
                pltpu.VMEM((rows, COLS), f32),
            ],
        ),
        out_shape=[jax.ShapeDtypeStruct(shape, bf16)] + shapes,
        compiler_params=params(),
        cost_estimate=cost(shape, 400),
        name="form",
    )(place, *kept, *sent, rot_in, eigvals, basis, *ties)


def stream(rotated_ref, buffers, sems, parts, begin, body):
    rows = buffers.shape[1]
    sets = NG // BLOCK

    def copy(turn, slot):
        part, query = turn // sets, lax.rem(turn, sets) * BLOCK + slot
        return pltpu.make_async_copy(
            rotated_ref.at[query, pl.ds(pl.multiple_of(part * rows, rows), rows), :],
            buffers.at[slot],
            sems.at[slot],
        )

    for slot in range(BLOCK):
        copy(0, slot).start()

    @pl.loop(0, parts * sets)
    def _(turn):
        part, first = turn // sets, lax.rem(turn, sets) * BLOCK

        @pl.when(first == 0)
        def _():
            begin(part)

        for slot in range(BLOCK):
            copy(turn, slot).wait()
            body(part, first + slot, buffers[slot])

            @pl.when(turn + 1 < parts * sets)
            def _(slot=slot):
                copy(turn + 1, slot).start()


def stream_scratch(rows, cols):
    return [pltpu.VMEM((BLOCK, rows, cols), bf16), pltpu.SemaphoreType.DMA((BLOCK,))]


def image_kernel(n_keep, n_ties, basis_ref, rotated_ref, *refs):
    *image_refs, image = refs[n_ties:]
    _, rows, cols = rotated_ref.shape
    product = jnp.dot(
        rotated_ref[...].reshape(BLOCK * rows, cols), basis_ref[...], preferred_element_type=f32
    )
    add_images(product, pl.program_id(1) * BLOCK, rows, image)
    write_image(image, n_keep, image_refs)


def image_parts(basis, rotated, n_keep, n_send, ties):
    _, rows, cols = rotated.shape
    rows = rows // (n_keep + n_send)
    shapes, specs = image_outputs(n_keep, n_send, rows)
    return pl.pallas_call(
        functools.partial(image_kernel, n_keep, len(ties)),
        grid=(n_keep + n_send, NG // BLOCK),
        in_specs=[
            pl.BlockSpec((cols, COLS), lambda part, query: (0, 0)),
            pl.BlockSpec((BLOCK, rows, cols), lambda part, query: (query, part, 0)),
        ]
        + tied(ties),
        out_specs=specs,
        out_shape=shapes,
        scratch_shapes=[pltpu.VMEM((rows, COLS), f32)],
        compiler_params=params(),
        cost_estimate=cost(rotated.shape, 256),
        name="image",
    )(basis, rotated, *ties)


def return_kernel(n_parts, first, *refs):
    image_refs, rotated_ref = refs[:n_parts], refs[n_parts]
    total_ref, rounded_ref, buffers, sems, turned = refs[-5:]
    total_ref[...] = jnp.zeros_like(total_ref) if first else refs[n_parts + 1][...]

    def begin(part):
        for at in range(n_parts):

            @pl.when(part == at)
            def _(at=at):
                turned[...] = image_refs[at][...].astype(f32).T.astype(bf16)

    def body(part, query, block):
        own = pl.ds(pl.multiple_of(query * RANK, RANK), RANK)
        total_ref[own, :] += jnp.dot(turned[own, :], block, preferred_element_type=f32)

    stream(rotated_ref, buffers, sems, n_parts, begin, body)
    rounded_ref[...] = total_ref[...].astype(bf16)


def return_parts(images, rotated, before, ties):
    n_parts = len(images)
    _, rows, cols = rotated.shape
    rows = rows // n_parts
    vmem = pl.BlockSpec(memory_space=pltpu.VMEM)
    before = [] if before is None else [before]
    return pl.pallas_call(
        functools.partial(return_kernel, n_parts, not before),
        in_specs=[vmem] * n_parts + tied([rotated]) + [vmem] * len(before) + tied(ties),
        out_specs=[vmem, vmem],
        out_shape=[
            jax.ShapeDtypeStruct((COLS, cols), f32),
            jax.ShapeDtypeStruct((COLS, cols), bf16),
        ],
        scratch_shapes=stream_scratch(rows, cols) + [pltpu.VMEM((COLS, rows), bf16)],
        compiler_params=params(),
        cost_estimate=cost(rotated.shape, 256),
        name="returned",
    )(*images, rotated, *before, *ties)


def rotate_out_kernel(n_dp, place_ref, query_ref, eigen_ref, *refs):
    turned = refs[-1]
    width = eigen_ref.shape[1]
    rows = width // (PIECES * n_dp)
    for side, index in ((0, place_ref[1]), (1, 1 - place_ref[1])):
        queries = query_ref[pl.ds(pl.multiple_of(index * TOKS, TOKS), TOKS), :]
        for begin, count in chunks(width):
            product = jnp.dot(
                queries, eigen_ref[:, begin : begin + count], preferred_element_type=f32
            )
            turned[begin : begin + count, :] = product.T
        for piece in range(PIECES):
            send_ref, keep_ref = refs[2 * (side * PIECES + piece) :][:2]
            for part in range(n_dp):
                at = piece * n_dp + lax.rem(place_ref[0] + 1 + part, n_dp)
                taken = turned[pl.ds(pl.multiple_of(at * rows, rows), rows), :]
                if part < n_dp - 1:
                    send_ref[part * rows : (part + 1) * rows, :] = taken.astype(bf16)
                else:
                    keep_ref[...] = taken.astype(keep_ref.dtype)


def rotate_out(place, query_out, eigen_out, n_dp):
    width = eigen_out.shape[1]
    rows = width // (PIECES * n_dp)
    shapes = []
    for kind in (f32, bf16):
        for _ in range(PIECES):
            shapes.append(jax.ShapeDtypeStruct(((n_dp - 1) * rows, TOKS), bf16))
            shapes.append(jax.ShapeDtypeStruct((rows, TOKS), kind))
    vmem = pl.BlockSpec(memory_space=pltpu.VMEM)
    return pl.pallas_call(
        functools.partial(rotate_out_kernel, n_dp),
        in_specs=[pl.BlockSpec(memory_space=pltpu.SMEM), vmem, vmem],
        out_specs=[vmem] * len(shapes),
        out_shape=shapes,
        scratch_shapes=[pltpu.VMEM((width, TOKS), f32)],
        compiler_params=params(),
        name="rotate_out",
    )(place, query_out, eigen_out)


def rotate_in_kernel(n_ties, place_ref, query_ref, eigen_ref, *refs):
    theirs_ref, mine_ref, product = refs[n_ties:]
    product[...] = jnp.dot(query_ref[...], eigen_ref[...], preferred_element_type=f32)
    for out_ref, index in ((theirs_ref, 1 - place_ref[1]), (mine_ref, place_ref[1])):
        out_ref[...] = product[pl.ds(pl.multiple_of(index * TOKS, TOKS), TOKS), :]


def rotate_in(place, query_in, eigen_in, ties):
    depth, cols = eigen_in.shape
    width = LANES if cols % LANES == 0 else cols
    out = jax.ShapeDtypeStruct((TOKS, cols), f32)
    return pl.pallas_call(
        functools.partial(rotate_in_kernel, len(ties)),
        grid_spec=pltpu.PrefetchScalarGridSpec(
            num_scalar_prefetch=1,
            grid=(cols // width,),
            in_specs=[
                pl.BlockSpec(query_in.shape, lambda at, _: (0, 0)),
                pl.BlockSpec((depth, width), lambda at, _: (0, at)),
            ]
            + tied(ties),
            out_specs=[pl.BlockSpec((TOKS, width), lambda at, _: (0, at))] * 2,
            scratch_shapes=[pltpu.VMEM((CORES * TOKS, width), f32)],
        ),
        out_shape=[out, out],
        compiler_params=params(),
        cost_estimate=pl.CostEstimate(
            flops=2 * depth * cols * CORES * TOKS, bytes_accessed=2 * depth * cols, transcendentals=0
        ),
        name="rotate_in",
    )(place, query_in, eigen_in, *ties)


def side_by_side(place_ref, mine, theirs):
    return jnp.where(
        place_ref[1] == 0,
        jnp.concatenate([mine, theirs], axis=1),
        jnp.concatenate([theirs, mine], axis=1),
    )


def factor_kernel(place_ref, eigen_ref, mine_ref, theirs_ref, send_ref, keep_ref, cols):
    part, parts = pl.program_id(0), pl.num_programs(0)

    @pl.when(part == 0)
    def _():
        cols[...] = side_by_side(place_ref, mine_ref[...], theirs_ref[...])

    product = jnp.dot(eigen_ref[...], cols[...], preferred_element_type=f32)

    @pl.when(part < parts - 1)
    def _():
        send_ref[...] = product.astype(bf16)

    @pl.when(part == parts - 1)
    def _():
        keep_ref[...] = product


def factor_piece(place, eigen_in, mine, theirs, piece, n_dp):
    rows, depth = eigen_in.shape
    rows = rows // (FACTOR_PIECES * n_dp)
    width = CORES * COLS
    fixed = pl.BlockSpec((depth, COLS), lambda part, _: (0, 0))

    def eigen_block(part, place_ref):
        return piece * n_dp + lax.rem(place_ref[0] + 1 + part, n_dp), 0

    return pl.pallas_call(
        factor_kernel,
        grid_spec=pltpu.PrefetchScalarGridSpec(
            num_scalar_prefetch=1,
            grid=(n_dp,),
            in_specs=[pl.BlockSpec((rows, depth), eigen_block), fixed, fixed],
            out_specs=[
                pl.BlockSpec((rows, width), lambda part, _: (jnp.minimum(part, n_dp - 2), 0)),
                pl.BlockSpec((rows, width), lambda part, _: (0, 0)),
            ],
            scratch_shapes=[pltpu.VMEM((depth, width), bf16)],
        ),
        out_shape=[
            jax.ShapeDtypeStruct(((n_dp - 1) * rows, width), bf16),
            jax.ShapeDtypeStruct((rows, width), f32),
        ],
        compiler_params=params(),
        name="factor",
    )(place, eigen_in, mine, theirs)


def write_shares(place_ref, total, keep_ref, send_refs):
    rows = keep_ref.shape[0]
    for step in range(len(send_refs) + 1):
        other = place_ref[2] ^ step
        share = total[pl.ds(pl.multiple_of(other * rows, rows), rows), :]
        if step == 0:
            keep_ref[...] = share
        else:
            send_refs[step - 1][...] = share.astype(bf16)


def factor_out_kernel(place_ref, eigen_ref, mine_ref, theirs_ref, keep_ref, *refs):
    *send_refs, total = refs
    total[...] = jnp.dot(
        eigen_ref[...],
        side_by_side(place_ref, mine_ref[...], theirs_ref[...]),
        preferred_element_type=f32,
    )
    write_shares(place_ref, total, keep_ref, send_refs)


def shares(rows, width, n_width):
    shape = (rows // n_width, width)
    return [jax.ShapeDtypeStruct(shape, f32)] + [jax.ShapeDtypeStruct(shape, bf16)] * (n_width - 1)


def factor_out(place, eigen_out, mine, theirs, n_width):
    rows = eigen_out.shape[0]
    width = CORES * COLS
    vmem = pl.BlockSpec(memory_space=pltpu.VMEM)
    return pl.pallas_call(
        factor_out_kernel,
        in_specs=[pl.BlockSpec(memory_space=pltpu.SMEM)] + [vmem] * 3,
        out_specs=[vmem] * n_width,
        out_shape=shares(rows, width, n_width),
        scratch_shapes=[pltpu.VMEM((rows, width), f32)],
        compiler_params=params(),
        name="factor_out",
    )(place, eigen_out, mine, theirs)


def project_kernel(n_dp, n_parts, place_ref, hidden_ref, *refs):
    part_refs = refs[:n_parts]
    factor_ref, keep_ref, *send_refs, total = refs[n_parts:]
    rows = part_refs[0].shape[0]
    for at, ref in enumerate(part_refs):
        owner = lax.rem(place_ref[0] + 1 + at % n_dp, n_dp)
        begin = (at // n_dp * n_dp + owner) * rows
        factor_ref[pl.ds(pl.multiple_of(begin, 8), rows), :] = ref[...]
    total[...] = jnp.dot(hidden_ref[...], factor_ref[...], preferred_element_type=f32)
    write_shares(place_ref, total, keep_ref, send_refs)


def project(place, hidden, parts, n_dp, n_width):
    tokens, depth = hidden.shape
    width = parts[0].shape[1]
    vmem = pl.BlockSpec(memory_space=pltpu.VMEM)
    return pl.pallas_call(
        functools.partial(project_kernel, n_dp, len(parts)),
        in_specs=[pl.BlockSpec(memory_space=pltpu.SMEM)] + [vmem] * (1 + len(parts)),
        out_specs=[vmem] * (1 + n_width),
        out_shape=[jax.ShapeDtypeStruct((depth, width), bf16)] + shares(tokens, width, n_width),
        scratch_shapes=[pltpu.VMEM((tokens, width), f32)],
        compiler_params=params(),
        name="project",
    )(place, hidden, *parts)


def turn_kernel(n_dp, place_ref, inverse_ref, *refs):
    *image_refs, mine_ref, theirs_ref = refs
    rows = image_refs[0].shape[0]
    for at, ref in enumerate(image_refs):
        out_ref = mine_ref if at < PIECES * n_dp else theirs_ref
        owner = lax.rem(place_ref[0] + 1 + at % n_dp, n_dp)
        begin = (at // n_dp % PIECES * n_dp + owner) * rows
        out_ref[pl.ds(pl.multiple_of(begin, rows), rows), :] = lax.dot_general(
            ref[...].astype(f32),
            inverse_ref[...],
            (((1,), (1,)), ((), ())),
            precision=lax.Precision.HIGHEST,
            preferred_element_type=f32,
        ).astype(bf16)


def turn(place, inverse, images, n_dp):
    out = jax.ShapeDtypeStruct((PIECES * n_dp * images[0].shape[0], COLS), bf16)
    vmem = pl.BlockSpec(memory_space=pltpu.VMEM)
    return pl.pallas_call(
        functools.partial(turn_kernel, n_dp),
        in_specs=[pl.BlockSpec(memory_space=pltpu.SMEM)] + [vmem] * (1 + len(images)),
        out_specs=[vmem, vmem],
        out_shape=[out, out],
        compiler_params=params(),
        name="turn",
    )(place, inverse, *images)


def gram_kernel(*refs):
    gram = jnp.zeros((COLS, COLS), f32)
    for ref in refs[:-1]:
        image = ref[...]
        gram = gram + lax.dot_general(
            image, image, (((0,), (0,)), ((), ())), preferred_element_type=f32
        )
    refs[-1][...] = gram


def gram_of(images):
    return pl.pallas_call(
        gram_kernel,
        out_shape=jax.ShapeDtypeStruct((COLS, COLS), f32),
        compiler_params=params(),
        name="gram",
    )(*images)


def lower_inverse(gram):
    shape = (NG, RANK, COLS)
    row = lax.broadcasted_iota(jnp.int32, shape, 1)
    lane = lax.broadcasted_iota(jnp.int32, shape, 2)
    same = lane // RANK == lax.broadcasted_iota(jnp.int32, shape, 0)
    col = lane % RANK
    eye = same & (col == row)
    gram = jnp.where(same, gram.reshape(shape), 0.0)
    trace = jnp.sum(
        jnp.sum(jnp.where(eye, gram, 0.0), axis=2, keepdims=True), axis=1, keepdims=True
    )
    left = gram + jnp.where(eye, ridge_scale * (trace / RANK), 0.0)
    right = jnp.where(eye, 1.0, 0.0)
    for step in range(RANK):
        column = jnp.sum(jnp.where(col == step, left, 0.0), axis=2, keepdims=True)
        pivot = column[:, step : step + 1, :]
        factor = jnp.where(row[:, :, :1] > step, column / pivot, 0.0)
        right = right - factor * right[:, step : step + 1, :]
        left = left - factor * left[:, step : step + 1, :]
    diagonal = jnp.sum(jnp.where(eye, left, 0.0), axis=2, keepdims=True)
    return (right * lax.rsqrt(diagonal)).reshape(COLS, COLS)


def inverse_kernel(scale, gram_ref, gram_got_ref, inverse_ref):
    inverse_ref[...] = lower_inverse((gram_ref[...] + gram_got_ref[...]) * scale)


def inverse_of(gram, gram_got, scale):
    return pl.pallas_call(
        functools.partial(inverse_kernel, scale),
        out_shape=jax.ShapeDtypeStruct((COLS, COLS), f32),
        compiler_params=params(),
        name="inverse",
    )(gram, gram_got)


def normalize_kernel(total_ref, got_ref, inverse_ref, *refs):
    basis_ref = refs[-1]
    total = total_ref[...] + got_ref[...].astype(f32)
    basis_ref[...] = lax.dot_general(
        total,
        inverse_ref[...],
        (((0,), (1,)), ((), ())),
        precision=lax.Precision.HIGHEST,
        preferred_element_type=f32,
    ).astype(bf16)


def normalize(total, got, inverse, ties):
    vmem = pl.BlockSpec(memory_space=pltpu.VMEM)
    return pl.pallas_call(
        normalize_kernel,
        in_specs=[vmem] * 3 + tied(ties),
        out_specs=vmem,
        out_shape=jax.ShapeDtypeStruct((total.shape[1], COLS), bf16),
        compiler_params=params(),
        name="normalize",
    )(total, got, inverse, *ties)


def turned_by(count, step):
    return [(i, (i + step) % count) for i in range(count)]


def crossed(count, step):
    return [(i, i ^ step) for i in range(count)]


def swap_cores(part, n_width):
    return lax.ppermute(part, "width", crossed(n_width, 1))


def after(array, others):
    return lax.optimization_barrier((array, *others))[0] if others else array


class Reduction:
    def __init__(self, sends, n_grp, n_dp, even=False, keep=None):
        self.parts = self.own = None
        self.keep = keep
        self.steps = self.run(sends, n_grp, n_dp, even)
        next(self.steps)

    def advance(self, others):
        try:
            return self.steps.send(others)
        except StopIteration:
            return []

    def run(self, sends, n_grp, n_dp, even):
        rows = sends.shape[0] // (n_dp - 1)
        got = [
            lax.ppermute(sends[at * rows : (at + 1) * rows], "dp", turned_by(n_dp, at + 1))
            for at in range(n_dp - 1)
        ]
        others = yield []
        total = after(self.keep, others)
        for part in got:
            total = total + part.astype(f32)
        step = 1
        while step < n_grp:
            sent = total.astype(bf16)
            got = lax.ppermute(sent, "grp", crossed(n_grp, step))
            others = yield [sent]
            total = (sent.astype(f32) if even else total) + after(got, others).astype(f32)
            step *= 2
        own = self.own = total.astype(bf16)
        self.parts = [
            lax.ppermute(own, "dp", turned_by(n_dp, n_dp - 1 - at)) for at in range(n_dp - 1)
        ] + [own]
        yield [own]


class Steps:
    def __init__(self, steps):
        self.steps, self.count = steps, 0

    def advance(self, others):
        self.count += 1
        try:
            return self.steps.send(others if self.count > 1 else None)
        except StopIteration:
            return []


def boundary(others, reductions):
    ties = []
    for reduction in reversed(reductions):
        if reduction.parts is None and reduction.keep is not None:
            hop = reduction.advance(others)
            ties = hop + ties
            others = hop or others
    return ties


def sum_shares(keep, sends, n_width):
    total = keep
    for at, send in enumerate(sends):
        total = total + lax.ppermute(send, "width", crossed(n_width, at + 1)).astype(f32)
    return total


def sum_scatter(part, axes, count):
    pieces = lax.all_to_all(part.astype(bf16), axes, 0, 0, tiled=True)
    pieces = pieces.reshape((count, part.shape[0] // count) + part.shape[1:])
    return jnp.sum(pieces.astype(f32), axis=0)


def gather_rows(piece, axes, count):
    copies = jnp.broadcast_to(piece[None], (count,) + piece.shape)
    whole = lax.all_to_all(copies, axes, 0, 0, tiled=True)
    return whole.reshape((count * piece.shape[0],) + piece.shape[1:])


def make_per_device(n_grp, n_dp, n_width):
    n_gd = n_grp * n_dp

    def per_device(
        query_out, query_in, eigen_out, eigen_in, eigvals, start, grads_out, gate_pre, up_pre
    ):
        dp = lax.axis_index("dp")
        along = lax.axis_index("width")
        core = along % CORES
        place = jnp.stack([dp, core, along]).astype(jnp.int32)
        scale = 1.0 / (eigen_out.shape[0] * n_gd)
        rows_out = eigvals.shape[0]

        def last_hop(total, sent=None):
            step = 2
            while True:
                sent = total.astype(bf16) if sent is None else sent
                got = lax.ppermute(sent, "width", crossed(n_width, step))
                step *= 2
                if step >= n_width:
                    return total, sent, got
                total, sent = total + got.astype(f32), None

        def output_side(summing, last):
            gram = gram_of([each.own for each in summing])
            got = [lax.ppermute(gram, "dp", turned_by(n_dp, at)) for at in range(1, n_dp)]
            others = yield [gram]
            gram = after(gram, others)
            for each in got:
                gram = gram + each
            step = 2
            while True:
                got = lax.ppermute(gram, "width", crossed(n_width, step))
                step *= 2
                if step >= n_width:
                    break
                gram = gram + got
            others = yield [gram]
            inverse = found["inverse"] = inverse_of(after(gram, others), got, scale)
            if not last:
                return
            images = [part for each in summing for part in each.parts]
            mine, theirs = turn(place, inverse, images, n_dp)
            theirs = swap_cores(theirs, n_width)
            others = yield [mine]
            keep, *sends = factor_out(place, eigen_out, after(mine, others), theirs, n_width)
            sends = [
                lax.ppermute(send, "width", crossed(n_width, at + 1))
                for at, send in enumerate(sends)
            ]
            others = yield [keep]
            share = after(keep, others)
            for send in sends:
                share = share + send.astype(f32)
            share = share.astype(bf16)
            piece_rows = share.shape[0]
            gathered = gather_rows(share, GD, n_gd)
            others = yield [share]
            mixed = lax.all_to_all(after(gathered, others), "width", 0, 0, tiled=True)
            others = yield [gathered]
            out_factor = found["out_factor"] = (
                after(mixed, others)
                .reshape(n_width, n_gd // n_width, piece_rows, NQ * RANK)
                .transpose(1, 0, 2, 3)
                .reshape(rows_out, NQ * RANK)
            )
            proj_out = jnp.dot(grads_out, out_factor, preferred_element_type=f32)
            found["proj_out"] = sum_scatter(proj_out, "width", n_width)

        found = {}
        count = CORES * PIECES
        pieces = list(rotate_out(place, query_out, eigen_out, n_dp))
        own_pieces, their_pieces = pieces[: 2 * PIECES], pieces[2 * PIECES :]
        turning = [Reduction(own_pieces[0], n_grp, n_dp, keep=own_pieces[1])]
        theirs_in, mine_in = rotate_in(place, query_in, eigen_in, pieces[:1])
        theirs_in = swap_cores(theirs_in, n_width)
        their_pieces = [swap_cores(each, n_width) for each in their_pieces]
        hops = boundary([mine_in], turning)
        total_in, sent_in, got_in = last_hop(after(mine_in, hops) + theirs_in)
        last = [sent_in]
        for at in range(1, count):
            sends, keep = (own_pieces + their_pieces)[2 * at : 2 * at + 2]
            turning.append(Reduction(after(sends, last), n_grp, n_dp, keep=keep))
            if turning[0].parts is None:
                last = boundary(last, turning)[:1]
        hidden = (jax.nn.silu(gate_pre.astype(f32)) * up_pre.astype(f32)).astype(bf16)
        rot_in = (total_in + got_in.astype(f32)).astype(bf16)
        eig_sent = after(eigvals, [rot_in, *turning[0].parts])
        eig_theirs = swap_cores(eig_sent, n_width)
        basis = lax.dynamic_slice_in_dim(start, core * COLS, COLS, 1)
        calls = []
        for begin in range(0, count, PIECES):
            span = list(range(begin, begin + PIECES))
            calls += zip([None] + span, span + [None])
        rotated, ties = [None] * len(calls), [hidden]

        def parts_of(reductions, pieces):
            for piece in pieces:
                while piece is not None and reductions[piece].parts is None:
                    boundary([], reductions)
            keep, send = pieces
            return (
                [] if keep is None else reductions[keep].parts[-1:],
                [] if send is None else reductions[send].parts[:-1],
            )

        for iteration in range(ITERS):
            summing = []
            found.clear()
            for at, (keep, send) in enumerate(calls):
                n_keep, n_send = int(keep is not None), (n_dp - 1) * int(send is not None)
                if iteration == 0:
                    ours = (keep if send is None else send) < PIECES
                    rotated[at], *images = form_parts(
                        place,
                        *parts_of(turning, (keep, send)),
                        [0 if each is None else each % PIECES for each in (keep, send)],
                        rot_in,
                        eigvals if ours else eig_theirs,
                        basis,
                        n_dp,
                        ties,
                    )
                else:
                    images = image_parts(basis, rotated[at], n_keep, n_send, ties)
                if n_keep:
                    summing[keep].keep = images[0]
                ties = boundary(images[:1], summing + turning)
                if n_send:
                    summing.append(Reduction(images[-1], n_grp, n_dp))
            total = path = None
            for at, pieces in enumerate(calls):
                kept, sent = parts_of(summing, pieces)
                total, rounded = return_parts(kept + sent, rotated[at], total, ties)
                ties = boundary([rounded], summing)
                if path is None and all(each.own is not None for each in summing):
                    path = Steps(output_side(summing, iteration == ITERS - 1))
                if path is not None and path.count < 5:
                    ties = ties + path.advance([rounded])
            while "inverse" not in found:
                path.advance([])
            total, sent, got = last_hop(total, rounded)
            basis = normalize(total, got, found["inverse"], ties)
            ties = []

        their_basis = swap_cores(basis, n_width)
        factors, last = [], []
        for piece in range(FACTOR_PIECES):
            sends, keep = factor_piece(place, eigen_in, basis, their_basis, piece, n_dp)
            if piece:
                last = boundary([keep], factors)
            factors.append(Reduction(sends, n_grp, n_dp, True, keep))
        path.advance(last)
        while any(each.parts is None for each in factors):
            last = boundary(last, factors)[:1]
        parts = [part for each in factors for part in each.parts]
        in_factor, keep_in, *sends_in = project(place, hidden, parts, n_dp, n_width)
        while "proj_out" not in found:
            path.advance([])
        proj_in = sum_shares(keep_in, sends_in, n_width)
        scores = (found["proj_out"] * proj_in).reshape(proj_in.shape[0], NQ, RANK).sum(axis=2).T
        return (scores, found["out_factor"], in_factor)

    return per_device


def solution(mesh):
    return jax.shard_map(
        make_per_device(mesh.shape["grp"], mesh.shape["dp"], mesh.shape["width"]),
        mesh=mesh,
        in_specs=(
            P(None, GD),
            P(None, "width"),
            P(GD, "width"),
            P("width", GD),
            P("width", GD),
            P(GD, None),
            P(GD, "width"),
            P(GD, "width"),
            P(GD, "width"),
        ),
        out_specs=(P(None, GD + ("width",)), P("width", None), P("width", None)),
        check_vma=False,
    )
```

```python
import functools

import jax
import jax.numpy as jnp
from jax import lax
from jax.experimental import pallas as pl
from jax.experimental.pallas import tpu as pltpu
from jax.sharding import PartitionSpec as P

NQ = 16
QTOK = 32
RANK = 16
ITERS = 2
CORES = 2
NG = NQ // CORES
COLS = NG * RANK
TOKS = NG * QTOK
LANES = 256
PIECES = 2
BLOCK = 4
FACTOR_PIECES = 2

damping = 0.01
ridge_scale = 1e-06

GD = ("grp", "dp")
f32 = jnp.float32
bf16 = jnp.bfloat16


def params():
    return pltpu.CompilerParams(vmem_limit_bytes=48 * 1024 * 1024)


def chunks(extent):
    return [(at, min(LANES, extent - at)) for at in range(0, extent, LANES)]


def cost(shape, columns):
    count = shape[0] * shape[1] * shape[2]
    return pl.CostEstimate(
        flops=2 * count * columns, bytes_accessed=2 * count, transcendentals=0
    )


def tied(ties):
    return [pl.BlockSpec(memory_space=pl.ANY)] * len(ties)


def write_image(image, n_keep, refs):
    part = pl.program_id(0)
    done = pl.program_id(1) == pl.num_programs(1) - 1

    if n_keep:

        @pl.when(done & (part == 0))
        def _():
            refs[0][...] = image[...]

    if len(refs) > n_keep:

        @pl.when(done & (part >= n_keep))
        def _():
            refs[-1][...] = image[...].astype(bf16)


def image_outputs(n_keep, n_send, rows):
    shapes, specs = [], []
    if n_keep:
        shapes.append(jax.ShapeDtypeStruct((rows, COLS), f32))
        specs.append(pl.BlockSpec((rows, COLS), lambda part, query, *_: (0, 0)))
    if n_send:
        shapes.append(jax.ShapeDtypeStruct((n_send * rows, COLS), bf16))
        specs.append(
            pl.BlockSpec(
                (rows, COLS), lambda part, query, *_: (jnp.maximum(part - n_keep, 0), 0)
            )
        )
    return shapes, specs


def add_images(product, first, rows, image):
    lane = lax.broadcasted_iota(jnp.int32, (rows, COLS), 1) // RANK
    for at in range(BLOCK):
        image[...] = jnp.where(
            lane == first + at, product[at * rows : (at + 1) * rows], image[...]
        )


def form_kernel(n_keep, n_parts, n_ties, place_ref, *refs):
    out_refs = refs[:n_parts]
    in_ref, eig_ref, basis_ref = refs[n_parts : n_parts + 3]
    rotated_ref, *image_refs, weight, left, image = refs[n_parts + 3 + n_ties :]
    part, first = pl.program_id(0), pl.program_id(1) * BLOCK
    rows, cols = eig_ref.shape

    @pl.when(first == 0)
    def _():
        weight[...] = 1.0 / (eig_ref[...] + damping)

    for at in range(n_parts):

        @pl.when((first == 0) & (part == at))
        def _(at=at):
            for query in range(NG):
                left[query] = out_refs[at][:, query * QTOK : (query + 1) * QTOK]

    for at in range(BLOCK):
        query = first + at
        own = left[query]
        right = in_ref[pl.ds(pl.multiple_of(query * QTOK, QTOK), QTOK), :]
        for begin, width in chunks(cols):
            span = slice(begin, begin + width)
            block = jnp.dot(own, right[:, span], preferred_element_type=f32)
            rotated_ref[at, :, span] = (block * weight[:, span]).astype(bf16)
    product = jnp.dot(
        rotated_ref[...].reshape(BLOCK * rows, cols), basis_ref[...], preferred_element_type=f32
    )
    add_images(product, first, rows, image)
    write_image(image, n_keep, image_refs)


def form_parts(place, kept, sent, pieces, rot_in, eigvals, basis, n_dp, ties):
    n_keep, n_parts = len(kept), len(kept) + len(sent)
    rows = (kept + sent)[0].shape[0]
    cols = rot_in.shape[1]
    keep_piece, send_piece = pieces

    def eig_block(part, query, place_ref):
        at = send_piece * n_dp + lax.rem(place_ref[0] + 1 + part + n_dp - n_keep, n_dp)
        return jnp.where(part < n_keep, keep_piece * n_dp + place_ref[0], at), 0

    def fixed(shape):
        return pl.BlockSpec(shape, lambda part, query, _: (0, 0))

    shape = (NG, n_parts * rows, cols)
    shapes, specs = image_outputs(n_keep, len(sent), rows)
    return pl.pallas_call(
        functools.partial(form_kernel, n_keep, n_parts, len(ties)),
        grid_spec=pltpu.PrefetchScalarGridSpec(
            num_scalar_prefetch=1,
            grid=(n_parts, NG // BLOCK),
            in_specs=[fixed((rows, TOKS))] * n_parts
            + [
                fixed((TOKS, cols)),
                pl.BlockSpec((rows, cols), eig_block),
                fixed((cols, COLS)),
            ]
            + tied(ties),
            out_specs=[
                pl.BlockSpec((BLOCK, rows, cols), lambda part, query, _: (query, part, 0))
            ]
            + specs,
            scratch_shapes=[
                pltpu.VMEM((rows, cols), f32),
                pltpu.VMEM((NG, rows, QTOK), bf16),
                pltpu.VMEM((rows, COLS), f32),
            ],
        ),
        out_shape=[jax.ShapeDtypeStruct(shape, bf16)] + shapes,
        compiler_params=params(),
        cost_estimate=cost(shape, 400),
        name="form",
    )(place, *kept, *sent, rot_in, eigvals, basis, *ties)


def stream(rotated_ref, buffers, sems, parts, begin, body):
    rows = buffers.shape[1]
    sets = NG // BLOCK

    def copy(turn, slot):
        part, query = turn // sets, lax.rem(turn, sets) * BLOCK + slot
        return pltpu.make_async_copy(
            rotated_ref.at[query, pl.ds(pl.multiple_of(part * rows, rows), rows), :],
            buffers.at[slot],
            sems.at[slot],
        )

    for slot in range(BLOCK):
        copy(0, slot).start()

    @pl.loop(0, parts * sets)
    def _(turn):
        part, first = turn // sets, lax.rem(turn, sets) * BLOCK

        @pl.when(first == 0)
        def _():
            begin(part)

        for slot in range(BLOCK):
            copy(turn, slot).wait()
            body(part, first + slot, buffers[slot])

            @pl.when(turn + 1 < parts * sets)
            def _(slot=slot):
                copy(turn + 1, slot).start()


def stream_scratch(rows, cols):
    return [pltpu.VMEM((BLOCK, rows, cols), bf16), pltpu.SemaphoreType.DMA((BLOCK,))]


def image_kernel(n_keep, n_ties, basis_ref, rotated_ref, *refs):
    *image_refs, image = refs[n_ties:]
    _, rows, cols = rotated_ref.shape
    product = jnp.dot(
        rotated_ref[...].reshape(BLOCK * rows, cols), basis_ref[...], preferred_element_type=f32
    )
    add_images(product, pl.program_id(1) * BLOCK, rows, image)
    write_image(image, n_keep, image_refs)


def image_parts(basis, rotated, n_keep, n_send, ties):
    _, rows, cols = rotated.shape
    rows = rows // (n_keep + n_send)
    shapes, specs = image_outputs(n_keep, n_send, rows)
    return pl.pallas_call(
        functools.partial(image_kernel, n_keep, len(ties)),
        grid=(n_keep + n_send, NG // BLOCK),
        in_specs=[
            pl.BlockSpec((cols, COLS), lambda part, query: (0, 0)),
            pl.BlockSpec((BLOCK, rows, cols), lambda part, query: (query, part, 0)),
        ]
        + tied(ties),
        out_specs=specs,
        out_shape=shapes,
        scratch_shapes=[pltpu.VMEM((rows, COLS), f32)],
        compiler_params=params(),
        cost_estimate=cost(rotated.shape, 256),
        name="image",
    )(basis, rotated, *ties)


def return_kernel(n_parts, first, *refs):
    image_refs, rotated_ref = refs[:n_parts], refs[n_parts]
    total_ref, rounded_ref, buffers, sems, turned = refs[-5:]
    total_ref[...] = jnp.zeros_like(total_ref) if first else refs[n_parts + 1][...]

    def begin(part):
        for at in range(n_parts):

            @pl.when(part == at)
            def _(at=at):
                turned[...] = image_refs[at][...].astype(f32).T.astype(bf16)

    def body(part, query, block):
        own = pl.ds(pl.multiple_of(query * RANK, RANK), RANK)
        total_ref[own, :] += jnp.dot(turned[own, :], block, preferred_element_type=f32)

    stream(rotated_ref, buffers, sems, n_parts, begin, body)
    rounded_ref[...] = total_ref[...].astype(bf16)


def return_parts(images, rotated, before, ties):
    n_parts = len(images)
    _, rows, cols = rotated.shape
    rows = rows // n_parts
    vmem = pl.BlockSpec(memory_space=pltpu.VMEM)
    before = [] if before is None else [before]
    return pl.pallas_call(
        functools.partial(return_kernel, n_parts, not before),
        in_specs=[vmem] * n_parts + tied([rotated]) + [vmem] * len(before) + tied(ties),
        out_specs=[vmem, vmem],
        out_shape=[
            jax.ShapeDtypeStruct((COLS, cols), f32),
            jax.ShapeDtypeStruct((COLS, cols), bf16),
        ],
        scratch_shapes=stream_scratch(rows, cols) + [pltpu.VMEM((COLS, rows), bf16)],
        compiler_params=params(),
        cost_estimate=cost(rotated.shape, 256),
        name="returned",
    )(*images, rotated, *before, *ties)


def rotate_out_kernel(n_dp, place_ref, query_ref, eigen_ref, *refs):
    turned = refs[-1]
    width = eigen_ref.shape[1]
    rows = width // (PIECES * n_dp)
    for side, index in ((0, place_ref[1]), (1, 1 - place_ref[1])):
        queries = query_ref[pl.ds(pl.multiple_of(index * TOKS, TOKS), TOKS), :]
        for begin, count in chunks(width):
            product = jnp.dot(
                queries, eigen_ref[:, begin : begin + count], preferred_element_type=f32
            )
            turned[begin : begin + count, :] = product.T
        for piece in range(PIECES):
            send_ref, keep_ref = refs[2 * (side * PIECES + piece) :][:2]
            for part in range(n_dp):
                at = piece * n_dp + lax.rem(place_ref[0] + 1 + part, n_dp)
                taken = turned[pl.ds(pl.multiple_of(at * rows, rows), rows), :]
                if part < n_dp - 1:
                    send_ref[part * rows : (part + 1) * rows, :] = taken.astype(bf16)
                else:
                    keep_ref[...] = taken.astype(keep_ref.dtype)


def rotate_out(place, query_out, eigen_out, n_dp):
    width = eigen_out.shape[1]
    rows = width // (PIECES * n_dp)
    shapes = []
    for kind in (f32, bf16):
        for _ in range(PIECES):
            shapes.append(jax.ShapeDtypeStruct(((n_dp - 1) * rows, TOKS), bf16))
            shapes.append(jax.ShapeDtypeStruct((rows, TOKS), kind))
    vmem = pl.BlockSpec(memory_space=pltpu.VMEM)
    return pl.pallas_call(
        functools.partial(rotate_out_kernel, n_dp),
        in_specs=[pl.BlockSpec(memory_space=pltpu.SMEM), vmem, vmem],
        out_specs=[vmem] * len(shapes),
        out_shape=shapes,
        scratch_shapes=[pltpu.VMEM((width, TOKS), f32)],
        compiler_params=params(),
        name="rotate_out",
    )(place, query_out, eigen_out)


def rotate_in_kernel(n_ties, place_ref, query_ref, eigen_ref, *refs):
    theirs_ref, mine_ref, product = refs[n_ties:]
    product[...] = jnp.dot(query_ref[...], eigen_ref[...], preferred_element_type=f32)
    for out_ref, index in ((theirs_ref, 1 - place_ref[1]), (mine_ref, place_ref[1])):
        out_ref[...] = product[pl.ds(pl.multiple_of(index * TOKS, TOKS), TOKS), :]


def rotate_in(place, query_in, eigen_in, ties):
    depth, cols = eigen_in.shape
    width = LANES if cols % LANES == 0 else cols
    out = jax.ShapeDtypeStruct((TOKS, cols), f32)
    return pl.pallas_call(
        functools.partial(rotate_in_kernel, len(ties)),
        grid_spec=pltpu.PrefetchScalarGridSpec(
            num_scalar_prefetch=1,
            grid=(cols // width,),
            in_specs=[
                pl.BlockSpec(query_in.shape, lambda at, _: (0, 0)),
                pl.BlockSpec((depth, width), lambda at, _: (0, at)),
            ]
            + tied(ties),
            out_specs=[pl.BlockSpec((TOKS, width), lambda at, _: (0, at))] * 2,
            scratch_shapes=[pltpu.VMEM((CORES * TOKS, width), f32)],
        ),
        out_shape=[out, out],
        compiler_params=params(),
        cost_estimate=pl.CostEstimate(
            flops=2 * depth * cols * CORES * TOKS, bytes_accessed=2 * depth * cols, transcendentals=0
        ),
        name="rotate_in",
    )(place, query_in, eigen_in, *ties)


def side_by_side(place_ref, mine, theirs):
    return jnp.where(
        place_ref[1] == 0,
        jnp.concatenate([mine, theirs], axis=1),
        jnp.concatenate([theirs, mine], axis=1),
    )


def factor_kernel(place_ref, eigen_ref, mine_ref, theirs_ref, send_ref, keep_ref, cols):
    part, parts = pl.program_id(0), pl.num_programs(0)

    @pl.when(part == 0)
    def _():
        cols[...] = side_by_side(place_ref, mine_ref[...], theirs_ref[...])

    product = jnp.dot(eigen_ref[...], cols[...], preferred_element_type=f32)

    @pl.when(part < parts - 1)
    def _():
        send_ref[...] = product.astype(bf16)

    @pl.when(part == parts - 1)
    def _():
        keep_ref[...] = product


def factor_piece(place, eigen_in, mine, theirs, piece, n_dp):
    rows, depth = eigen_in.shape
    rows = rows // (FACTOR_PIECES * n_dp)
    width = CORES * COLS
    fixed = pl.BlockSpec((depth, COLS), lambda part, _: (0, 0))

    def eigen_block(part, place_ref):
        return piece * n_dp + lax.rem(place_ref[0] + 1 + part, n_dp), 0

    return pl.pallas_call(
        factor_kernel,
        grid_spec=pltpu.PrefetchScalarGridSpec(
            num_scalar_prefetch=1,
            grid=(n_dp,),
            in_specs=[pl.BlockSpec((rows, depth), eigen_block), fixed, fixed],
            out_specs=[
                pl.BlockSpec((rows, width), lambda part, _: (jnp.minimum(part, n_dp - 2), 0)),
                pl.BlockSpec((rows, width), lambda part, _: (0, 0)),
            ],
            scratch_shapes=[pltpu.VMEM((depth, width), bf16)],
        ),
        out_shape=[
            jax.ShapeDtypeStruct(((n_dp - 1) * rows, width), bf16),
            jax.ShapeDtypeStruct((rows, width), f32),
        ],
        compiler_params=params(),
        name="factor",
    )(place, eigen_in, mine, theirs)


def write_shares(place_ref, total, keep_ref, send_refs):
    rows = keep_ref.shape[0]
    for step in range(len(send_refs) + 1):
        other = place_ref[2] ^ step
        share = total[pl.ds(pl.multiple_of(other * rows, rows), rows), :]
        if step == 0:
            keep_ref[...] = share
        else:
            send_refs[step - 1][...] = share.astype(bf16)


def factor_out_kernel(n_ties, place_ref, eigen_ref, mine_ref, theirs_ref, *refs):
    keep_ref, *send_refs, total = refs[n_ties:]
    total[...] = jnp.dot(
        eigen_ref[...],
        side_by_side(place_ref, mine_ref[...], theirs_ref[...]),
        preferred_element_type=f32,
    )
    write_shares(place_ref, total, keep_ref, send_refs)


def shares(rows, width, n_width):
    shape = (rows // n_width, width)
    return [jax.ShapeDtypeStruct(shape, f32)] + [jax.ShapeDtypeStruct(shape, bf16)] * (n_width - 1)


def factor_out(place, eigen_out, mine, theirs, n_width, ties):
    rows = eigen_out.shape[0]
    width = CORES * COLS
    vmem = pl.BlockSpec(memory_space=pltpu.VMEM)
    return pl.pallas_call(
        functools.partial(factor_out_kernel, len(ties)),
        in_specs=[pl.BlockSpec(memory_space=pltpu.SMEM)] + [vmem] * 3 + tied(ties),
        out_specs=[vmem] * n_width,
        out_shape=shares(rows, width, n_width),
        scratch_shapes=[pltpu.VMEM((rows, width), f32)],
        compiler_params=params(),
        name="factor_out",
    )(place, eigen_out, mine, theirs, *ties)


def project_kernel(n_dp, n_parts, place_ref, hidden_ref, *refs):
    part_refs = refs[:n_parts]
    factor_ref, keep_ref, *send_refs, total = refs[n_parts:]
    rows = part_refs[0].shape[0]
    for at, ref in enumerate(part_refs):
        owner = lax.rem(place_ref[0] + 1 + at % n_dp, n_dp)
        begin = (at // n_dp * n_dp + owner) * rows
        factor_ref[pl.ds(pl.multiple_of(begin, 8), rows), :] = ref[...]
    total[...] = jnp.dot(hidden_ref[...], factor_ref[...], preferred_element_type=f32)
    write_shares(place_ref, total, keep_ref, send_refs)


def project(place, hidden, parts, n_dp, n_width):
    tokens, depth = hidden.shape
    width = parts[0].shape[1]
    vmem = pl.BlockSpec(memory_space=pltpu.VMEM)
    return pl.pallas_call(
        functools.partial(project_kernel, n_dp, len(parts)),
        in_specs=[pl.BlockSpec(memory_space=pltpu.SMEM)] + [vmem] * (1 + len(parts)),
        out_specs=[vmem] * (1 + n_width),
        out_shape=[jax.ShapeDtypeStruct((depth, width), bf16)] + shares(tokens, width, n_width),
        scratch_shapes=[pltpu.VMEM((tokens, width), f32)],
        compiler_params=params(),
        name="project",
    )(place, hidden, *parts)


def turn_kernel(n_dp, place_ref, inverse_ref, *refs):
    *image_refs, mine_ref, theirs_ref = refs
    rows = image_refs[0].shape[0]
    for at, ref in enumerate(image_refs):
        out_ref = mine_ref if at < PIECES * n_dp else theirs_ref
        owner = lax.rem(place_ref[0] + 1 + at % n_dp, n_dp)
        begin = (at // n_dp % PIECES * n_dp + owner) * rows
        out_ref[pl.ds(pl.multiple_of(begin, rows), rows), :] = lax.dot_general(
            ref[...].astype(f32),
            inverse_ref[...],
            (((1,), (1,)), ((), ())),
            precision=lax.Precision.HIGHEST,
            preferred_element_type=f32,
        ).astype(bf16)


def turn(place, inverse, images, n_dp):
    out = jax.ShapeDtypeStruct((PIECES * n_dp * images[0].shape[0], COLS), bf16)
    vmem = pl.BlockSpec(memory_space=pltpu.VMEM)
    return pl.pallas_call(
        functools.partial(turn_kernel, n_dp),
        in_specs=[pl.BlockSpec(memory_space=pltpu.SMEM)] + [vmem] * (1 + len(images)),
        out_specs=[vmem, vmem],
        out_shape=[out, out],
        compiler_params=params(),
        name="turn",
    )(place, inverse, *images)


def gram_kernel(*refs):
    gram = jnp.zeros((COLS, COLS), f32)
    for ref in refs[:-1]:
        image = ref[...]
        gram = gram + lax.dot_general(
            image, image, (((0,), (0,)), ((), ())), preferred_element_type=f32
        )
    refs[-1][...] = gram


def gram_of(images):
    return pl.pallas_call(
        gram_kernel,
        out_shape=jax.ShapeDtypeStruct((COLS, COLS), f32),
        compiler_params=params(),
        name="gram",
    )(*images)


def lower_inverse(gram):
    shape = (NG, RANK, COLS)
    row = lax.broadcasted_iota(jnp.int32, shape, 1)
    lane = lax.broadcasted_iota(jnp.int32, shape, 2)
    same = lane // RANK == lax.broadcasted_iota(jnp.int32, shape, 0)
    col = lane % RANK
    eye = same & (col == row)
    gram = jnp.where(same, gram.reshape(shape), 0.0)
    trace = jnp.sum(
        jnp.sum(jnp.where(eye, gram, 0.0), axis=2, keepdims=True), axis=1, keepdims=True
    )
    left = gram + jnp.where(eye, ridge_scale * (trace / RANK), 0.0)
    right = jnp.where(eye, 1.0, 0.0)
    for step in range(RANK):
        column = jnp.sum(jnp.where(col == step, left, 0.0), axis=2, keepdims=True)
        pivot = column[:, step : step + 1, :]
        factor = jnp.where(row[:, :, :1] > step, column / pivot, 0.0)
        right = right - factor * right[:, step : step + 1, :]
        left = left - factor * left[:, step : step + 1, :]
    diagonal = jnp.sum(jnp.where(eye, left, 0.0), axis=2, keepdims=True)
    return (right * lax.rsqrt(diagonal)).reshape(COLS, COLS)


def inverse_kernel(scale, gram_ref, gram_got_ref, *refs):
    refs[-1][...] = lower_inverse((gram_ref[...] + gram_got_ref[...]) * scale)


def inverse_of(gram, gram_got, scale, ties):
    vmem = pl.BlockSpec(memory_space=pltpu.VMEM)
    return pl.pallas_call(
        functools.partial(inverse_kernel, scale),
        in_specs=[vmem, vmem] + tied(ties),
        out_specs=vmem,
        out_shape=jax.ShapeDtypeStruct((COLS, COLS), f32),
        compiler_params=params(),
        name="inverse",
    )(gram, gram_got, *ties)


def normalize_kernel(total_ref, got_ref, inverse_ref, *refs):
    basis_ref = refs[-1]
    total = total_ref[...] + got_ref[...].astype(f32)
    basis_ref[...] = lax.dot_general(
        total,
        inverse_ref[...],
        (((0,), (1,)), ((), ())),
        precision=lax.Precision.HIGHEST,
        preferred_element_type=f32,
    ).astype(bf16)


def normalize(total, got, inverse, ties):
    vmem = pl.BlockSpec(memory_space=pltpu.VMEM)
    return pl.pallas_call(
        normalize_kernel,
        in_specs=[vmem] * 3 + tied(ties),
        out_specs=vmem,
        out_shape=jax.ShapeDtypeStruct((total.shape[1], COLS), bf16),
        compiler_params=params(),
        name="normalize",
    )(total, got, inverse, *ties)


def turned_by(count, step):
    return [(i, (i + step) % count) for i in range(count)]


def crossed(count, step):
    return [(i, i ^ step) for i in range(count)]


def swap_cores(part, n_width):
    return lax.ppermute(part, "width", crossed(n_width, 1))


def after(array, others):
    return lax.optimization_barrier((array, *others))[0] if others else array


def hop_kernel(n_got, n_ties, total_ref, *refs):
    total = total_ref[...]
    for ref in refs[:n_got]:
        total = total + ref[...].astype(f32)
    rounded_ref, *total_refs = refs[n_got + n_ties :]
    rounded_ref[...] = total.astype(bf16)
    for ref in total_refs:
        ref[...] = total


def hop_sum(total, got, others, last):
    vmem = pl.BlockSpec(memory_space=pltpu.VMEM)
    shapes = [jax.ShapeDtypeStruct(total.shape, bf16), jax.ShapeDtypeStruct(total.shape, f32)]
    shapes = shapes[:1] if last else shapes
    return pl.pallas_call(
        functools.partial(hop_kernel, len(got), len(others)),
        in_specs=[vmem] * (1 + len(got)) + tied(others),
        out_specs=[vmem] * len(shapes),
        out_shape=shapes,
        compiler_params=params(),
        name="hop",
    )(total, *got, *others)


class Reduction:
    def __init__(self, sends, n_grp, n_dp, even=False, keep=None):
        self.parts = self.own = None
        self.keep = keep
        self.steps = self.run(sends, n_grp, n_dp, even)
        next(self.steps)

    def advance(self, others):
        try:
            return self.steps.send(others)
        except StopIteration:
            return []

    def run(self, sends, n_grp, n_dp, even):
        rows = sends.shape[0] // (n_dp - 1)
        got = [
            lax.ppermute(sends[at * rows : (at + 1) * rows], "dp", turned_by(n_dp, at + 1))
            for at in range(n_dp - 1)
        ]
        others = yield []
        total, step, odd = self.keep, 1, lax.axis_index("grp") % 2
        while True:
            last = step >= n_grp
            if even:
                total = after(total, others)
                for part in got:
                    total = total + part.astype(f32)
                if step == 2:
                    total = lax.dynamic_slice_in_dim(total, odd * (rows // 2), rows // 2, 0)
                own = sent = total.astype(bf16)
                total = sent.astype(f32)
            else:
                sent, *totals = hop_sum(total, got, others, last)
                own, total = sent, totals[0] if totals else None
            if last:
                break
            got = [lax.ppermute(sent, "grp", crossed(n_grp, step))]
            others = yield [sent]
            step *= 2
        if even and n_grp > 2:
            got = lax.ppermute(own, "grp", crossed(n_grp, 1))
            others = yield [own]
            got = after(got, others)
            own = jnp.where(
                odd == 0, jnp.concatenate([own, got]), jnp.concatenate([got, own])
            )
        self.own = own
        self.parts = [
            lax.ppermute(own, "dp", turned_by(n_dp, n_dp - 1 - at)) for at in range(n_dp - 1)
        ] + [own]
        yield [own]


class Steps:
    def __init__(self, steps):
        self.steps, self.count = steps, 0

    def advance(self, others):
        self.count += 1
        try:
            return self.steps.send(others if self.count > 1 else None)
        except StopIteration:
            return []


def boundary(others, reductions):
    ties = []
    for reduction in reversed(reductions):
        if reduction.parts is None and reduction.keep is not None:
            hop = reduction.advance(others)
            ties = hop + ties
            others = hop or others
    return ties


def sum_shares(keep, sends, n_width):
    total = keep
    for at, send in enumerate(sends):
        total = total + lax.ppermute(send, "width", crossed(n_width, at + 1)).astype(f32)
    return total


def sum_scatter(part, axes, count):
    pieces = lax.all_to_all(part.astype(bf16), axes, 0, 0, tiled=True)
    pieces = pieces.reshape((count, part.shape[0] // count) + part.shape[1:])
    return jnp.sum(pieces.astype(f32), axis=0)


def make_per_device(n_grp, n_dp, n_width):
    n_gd = n_grp * n_dp

    def per_device(
        query_out, query_in, eigen_out, eigen_in, eigvals, start, grads_out, gate_pre, up_pre
    ):
        dp = lax.axis_index("dp")
        along = lax.axis_index("width")
        core = along % CORES
        place = jnp.stack([dp, core, along]).astype(jnp.int32)
        scale = 1.0 / (eigen_out.shape[0] * n_gd)
        rows_out = eigvals.shape[0]

        def last_hop(total, sent=None):
            step = 2
            while True:
                sent = total.astype(bf16) if sent is None else sent
                got = lax.ppermute(sent, "width", crossed(n_width, step))
                step *= 2
                if step >= n_width:
                    return total, sent, got
                total, sent = total + got.astype(f32), None

        def output_side(summing, last):
            gram = gram_of([each.own for each in summing])
            got = [lax.ppermute(gram, "dp", turned_by(n_dp, at)) for at in range(1, n_dp)]
            for each in got:
                gram = gram + each
            step = 2
            while True:
                got = lax.ppermute(gram, "width", crossed(n_width, step))
                step *= 2
                if step >= n_width:
                    break
                gram = gram + got
            others = yield [gram]
            inverse = found["inverse"] = inverse_of(gram, got, scale, others)
            if not last:
                return
            images = [part for each in summing for part in each.parts]
            mine, theirs = turn(place, inverse, images, n_dp)
            theirs = swap_cores(theirs, n_width)
            others = yield [mine]
            keep, *sends = factor_out(place, eigen_out, mine, theirs, n_width, others)
            sends = [
                lax.ppermute(send, "width", crossed(n_width, at + 1))
                for at, send in enumerate(sends)
            ]
            others = yield [keep]
            share = after(keep, others)
            for send in sends:
                share = share + send.astype(f32)
            share = share.astype(bf16)
            piece_rows = share.shape[0]
            others = yield [share]
            copies = jnp.broadcast_to(after(share, others)[None], (n_gd,) + share.shape)
            gathered = lax.all_to_all(copies, GD, 0, 0, tiled=True)
            gathered = gathered.reshape(n_gd * piece_rows, -1)
            others = yield [copies]
            mixed = lax.all_to_all(after(gathered, others), "width", 0, 0, tiled=True)
            others = yield [gathered]
            out_factor = found["out_factor"] = (
                after(mixed, others)
                .reshape(n_width, n_gd // n_width, piece_rows, NQ * RANK)
                .transpose(1, 0, 2, 3)
                .reshape(rows_out, NQ * RANK)
            )
            proj_out = jnp.dot(grads_out, out_factor, preferred_element_type=f32)
            found["proj_out"] = sum_scatter(proj_out, "width", n_width)

        found = {}
        count = CORES * PIECES
        pieces = list(rotate_out(place, query_out, eigen_out, n_dp))
        own_pieces, their_pieces = pieces[: 2 * PIECES], pieces[2 * PIECES :]
        turning = [Reduction(own_pieces[0], n_grp, n_dp, keep=own_pieces[1])]
        theirs_in, mine_in = rotate_in(place, query_in, eigen_in, pieces[:1])
        theirs_in = swap_cores(theirs_in, n_width)
        their_pieces = [swap_cores(each, n_width) for each in their_pieces]
        hidden = (jax.nn.silu(gate_pre.astype(f32)) * up_pre.astype(f32)).astype(bf16)
        hops = boundary([mine_in], turning)
        total_in, sent_in, got_in = last_hop(after(mine_in, hops) + theirs_in)
        last = [sent_in]
        for at in range(1, count):
            sends, keep = (own_pieces + their_pieces)[2 * at : 2 * at + 2]
            turning.append(Reduction(after(sends, last), n_grp, n_dp, keep=keep))
            if turning[0].parts is None:
                last = boundary(last + [hidden] if at == 2 else last, turning)[:1]
        rot_in = (total_in + got_in.astype(f32)).astype(bf16)
        eig_sent = after(eigvals, [rot_in, *turning[0].parts, *their_pieces])
        eig_theirs = swap_cores(eig_sent, n_width)
        basis = lax.dynamic_slice_in_dim(start, core * COLS, COLS, 1)
        calls = []
        for begin in range(0, count, PIECES):
            span = list(range(begin, begin + PIECES))
            calls += zip([None] + span, span + [None])
        rotated, ties = [None] * len(calls), [hidden]

        def parts_of(reductions, pieces):
            for piece in pieces:
                while piece is not None and reductions[piece].parts is None:
                    boundary([], reductions)
            keep, send = pieces
            return (
                [] if keep is None else reductions[keep].parts[-1:],
                [] if send is None else reductions[send].parts[:-1],
            )

        for iteration in range(ITERS):
            summing = []
            found.clear()
            for at, (keep, send) in enumerate(calls):
                n_keep, n_send = int(keep is not None), (n_dp - 1) * int(send is not None)
                if iteration == 0:
                    ours = (keep if send is None else send) < PIECES
                    rotated[at], *images = form_parts(
                        place,
                        *parts_of(turning, (keep, send)),
                        [0 if each is None else each % PIECES for each in (keep, send)],
                        rot_in,
                        eigvals if ours else eig_theirs,
                        basis,
                        n_dp,
                        ties,
                    )
                else:
                    images = image_parts(basis, rotated[at], n_keep, n_send, ties)
                if n_keep:
                    summing[keep].keep = images[0]
                ties = boundary(images[:1], summing + turning)
                if n_send:
                    summing.append(Reduction(images[-1], n_grp, n_dp))
            total = path = None
            for at, pieces in enumerate(calls):
                kept, sent = parts_of(summing, pieces)
                total, rounded = return_parts(kept + sent, rotated[at], total, ties)
                ties = boundary([rounded], summing)
                if path is None and all(each.own is not None for each in summing):
                    path = Steps(output_side(summing, iteration == ITERS - 1))
                if path is not None and path.count < 5:
                    ties = ties + path.advance([rounded])
            while "inverse" not in found:
                path.advance([])
            total, sent, got = last_hop(total, rounded)
            basis = normalize(total, got, found["inverse"], ties)
            ties = []

        their_basis = swap_cores(basis, n_width)
        factors, last = [], []
        for piece in range(FACTOR_PIECES):
            sends, keep = factor_piece(place, eigen_in, basis, their_basis, piece, n_dp)
            if piece:
                last = boundary([keep], factors)
            factors.append(Reduction(sends, n_grp, n_dp, True, keep))
        path.advance(last)
        while any(each.parts is None for each in factors):
            last = boundary(last, factors[::-1])[:1]
        parts = [part for each in factors for part in each.parts]
        in_factor, keep_in, *sends_in = project(place, hidden, parts, n_dp, n_width)
        while "proj_out" not in found:
            path.advance([])
        proj_in = sum_shares(keep_in, sends_in, n_width)
        scores = (found["proj_out"] * proj_in).reshape(proj_in.shape[0], NQ, RANK).sum(axis=2).T
        return (scores, found["out_factor"], in_factor)

    return per_device


def solution(mesh):
    return jax.shard_map(
        make_per_device(mesh.shape["grp"], mesh.shape["dp"], mesh.shape["width"]),
        mesh=mesh,
        in_specs=(
            P(None, GD),
            P(None, "width"),
            P(GD, "width"),
            P("width", GD),
            P("width", GD),
            P(GD, None),
            P(GD, "width"),
            P(GD, "width"),
            P(GD, "width"),
        ),
        out_specs=(P(None, GD + ("width",)), P("width", None), P("width", None)),
        check_vma=False,
    )
```

```python
import functools

import jax
import jax.numpy as jnp
from jax import lax
from jax.experimental import pallas as pl
from jax.experimental.pallas import tpu as pltpu
from jax.sharding import PartitionSpec as P

NQ = 16
QTOK = 32
RANK = 16
ITERS = 2
CORES = 2
NG = NQ // CORES
COLS = NG * RANK
TOKS = NG * QTOK
LANES = 256
PIECES = 2
BLOCK = 4
FACTOR_PIECES = 2

damping = 0.01
ridge_scale = 1e-06

GD = ("grp", "dp")
f32 = jnp.float32
bf16 = jnp.bfloat16


def params():
    return pltpu.CompilerParams(vmem_limit_bytes=48 * 1024 * 1024)


def chunks(extent):
    return [(at, min(LANES, extent - at)) for at in range(0, extent, LANES)]


def cost(shape, columns):
    count = shape[0] * shape[1] * shape[2]
    return pl.CostEstimate(
        flops=2 * count * columns, bytes_accessed=2 * count, transcendentals=0
    )


def tied(ties):
    return [pl.BlockSpec(memory_space=pl.ANY)] * len(ties)


def write_image(image, n_keep, refs):
    part = pl.program_id(0)
    done = pl.program_id(1) == pl.num_programs(1) - 1

    if n_keep:

        @pl.when(done & (part == 0))
        def _():
            refs[0][...] = image[...]

    if len(refs) > n_keep:

        @pl.when(done & (part >= n_keep))
        def _():
            refs[-1][...] = image[...].astype(bf16)


def image_outputs(n_keep, n_send, rows):
    shapes, specs = [], []
    if n_keep:
        shapes.append(jax.ShapeDtypeStruct((rows, COLS), f32))
        specs.append(pl.BlockSpec((rows, COLS), lambda part, query, *_: (0, 0)))
    if n_send:
        shapes.append(jax.ShapeDtypeStruct((n_send * rows, COLS), bf16))
        specs.append(
            pl.BlockSpec(
                (rows, COLS), lambda part, query, *_: (jnp.maximum(part - n_keep, 0), 0)
            )
        )
    return shapes, specs


def add_images(product, first, rows, image):
    lane = lax.broadcasted_iota(jnp.int32, (rows, COLS), 1) // RANK
    for at in range(BLOCK):
        image[...] = jnp.where(
            lane == first + at, product[at * rows : (at + 1) * rows], image[...]
        )


def form_kernel(n_keep, n_parts, n_ties, place_ref, *refs):
    out_refs = refs[:n_parts]
    in_ref, eig_ref, basis_ref = refs[n_parts : n_parts + 3]
    rotated_ref, *image_refs, weight, left, image = refs[n_parts + 3 + n_ties :]
    part, first = pl.program_id(0), pl.program_id(1) * BLOCK
    rows, cols = eig_ref.shape

    @pl.when(first == 0)
    def _():
        weight[...] = 1.0 / (eig_ref[...] + damping)

    for at in range(n_parts):

        @pl.when((first == 0) & (part == at))
        def _(at=at):
            for query in range(NG):
                left[query] = out_refs[at][:, query * QTOK : (query + 1) * QTOK]

    for at in range(BLOCK):
        query = first + at
        own = left[query]
        right = in_ref[pl.ds(pl.multiple_of(query * QTOK, QTOK), QTOK), :]
        for begin, width in chunks(cols):
            span = slice(begin, begin + width)
            block = jnp.dot(own, right[:, span], preferred_element_type=f32)
            rotated_ref[at, :, span] = (block * weight[:, span]).astype(bf16)
    product = jnp.dot(
        rotated_ref[...].reshape(BLOCK * rows, cols), basis_ref[...], preferred_element_type=f32
    )
    add_images(product, first, rows, image)
    write_image(image, n_keep, image_refs)


def form_parts(place, kept, sent, pieces, rot_in, eigvals, basis, n_dp, ties):
    n_keep, n_parts = len(kept), len(kept) + len(sent)
    rows = (kept + sent)[0].shape[0]
    cols = rot_in.shape[1]
    keep_piece, send_piece = pieces

    def eig_block(part, query, place_ref):
        at = send_piece * n_dp + lax.rem(place_ref[0] + 1 + part + n_dp - n_keep, n_dp)
        return jnp.where(part < n_keep, keep_piece * n_dp + place_ref[0], at), 0

    def fixed(shape):
        return pl.BlockSpec(shape, lambda part, query, _: (0, 0))

    shape = (NG, n_parts * rows, cols)
    shapes, specs = image_outputs(n_keep, len(sent), rows)
    return pl.pallas_call(
        functools.partial(form_kernel, n_keep, n_parts, len(ties)),
        grid_spec=pltpu.PrefetchScalarGridSpec(
            num_scalar_prefetch=1,
            grid=(n_parts, NG // BLOCK),
            in_specs=[fixed((rows, TOKS))] * n_parts
            + [
                fixed((TOKS, cols)),
                pl.BlockSpec((rows, cols), eig_block),
                fixed((cols, COLS)),
            ]
            + tied(ties),
            out_specs=[
                pl.BlockSpec((BLOCK, rows, cols), lambda part, query, _: (query, part, 0))
            ]
            + specs,
            scratch_shapes=[
                pltpu.VMEM((rows, cols), f32),
                pltpu.VMEM((NG, rows, QTOK), bf16),
                pltpu.VMEM((rows, COLS), f32),
            ],
        ),
        out_shape=[jax.ShapeDtypeStruct(shape, bf16)] + shapes,
        compiler_params=params(),
        cost_estimate=cost(shape, 400),
        name="form",
    )(place, *kept, *sent, rot_in, eigvals, basis, *ties)


def stream(rotated_ref, buffers, sems, parts, begin, body):
    rows = buffers.shape[1]
    sets = NG // BLOCK

    def copy(turn, slot):
        part, query = turn // sets, lax.rem(turn, sets) * BLOCK + slot
        return pltpu.make_async_copy(
            rotated_ref.at[query, pl.ds(pl.multiple_of(part * rows, rows), rows), :],
            buffers.at[slot],
            sems.at[slot],
        )

    for slot in range(BLOCK):
        copy(0, slot).start()

    @pl.loop(0, parts * sets)
    def _(turn):
        part, first = turn // sets, lax.rem(turn, sets) * BLOCK

        @pl.when(first == 0)
        def _():
            begin(part)

        for slot in range(BLOCK):
            copy(turn, slot).wait()
            body(part, first + slot, buffers[slot])

            @pl.when(turn + 1 < parts * sets)
            def _(slot=slot):
                copy(turn + 1, slot).start()


def stream_scratch(rows, cols):
    return [pltpu.VMEM((BLOCK, rows, cols), bf16), pltpu.SemaphoreType.DMA((BLOCK,))]


def image_kernel(n_keep, n_ties, basis_ref, rotated_ref, *refs):
    *image_refs, image = refs[n_ties:]
    _, rows, cols = rotated_ref.shape
    product = jnp.dot(
        rotated_ref[...].reshape(BLOCK * rows, cols), basis_ref[...], preferred_element_type=f32
    )
    add_images(product, pl.program_id(1) * BLOCK, rows, image)
    write_image(image, n_keep, image_refs)


def image_parts(basis, rotated, n_keep, n_send, ties):
    _, rows, cols = rotated.shape
    rows = rows // (n_keep + n_send)
    shapes, specs = image_outputs(n_keep, n_send, rows)
    return pl.pallas_call(
        functools.partial(image_kernel, n_keep, len(ties)),
        grid=(n_keep + n_send, NG // BLOCK),
        in_specs=[
            pl.BlockSpec((cols, COLS), lambda part, query: (0, 0)),
            pl.BlockSpec((BLOCK, rows, cols), lambda part, query: (query, part, 0)),
        ]
        + tied(ties),
        out_specs=specs,
        out_shape=shapes,
        scratch_shapes=[pltpu.VMEM((rows, COLS), f32)],
        compiler_params=params(),
        cost_estimate=cost(rotated.shape, 256),
        name="image",
    )(basis, rotated, *ties)


def return_kernel(n_parts, first, *refs):
    image_refs, rotated_ref = refs[:n_parts], refs[n_parts]
    total_ref, rounded_ref, buffers, sems, turned = refs[-5:]
    total_ref[...] = jnp.zeros_like(total_ref) if first else refs[n_parts + 1][...]

    def begin(part):
        for at in range(n_parts):

            @pl.when(part == at)
            def _(at=at):
                turned[...] = image_refs[at][...].astype(f32).T.astype(bf16)

    def body(part, query, block):
        own = pl.ds(pl.multiple_of(query * RANK, RANK), RANK)
        total_ref[own, :] += jnp.dot(turned[own, :], block, preferred_element_type=f32)

    stream(rotated_ref, buffers, sems, n_parts, begin, body)
    rounded_ref[...] = total_ref[...].astype(bf16)


def return_parts(images, rotated, before, ties):
    n_parts = len(images)
    _, rows, cols = rotated.shape
    rows = rows // n_parts
    vmem = pl.BlockSpec(memory_space=pltpu.VMEM)
    before = [] if before is None else [before]
    return pl.pallas_call(
        functools.partial(return_kernel, n_parts, not before),
        in_specs=[vmem] * n_parts + tied([rotated]) + [vmem] * len(before) + tied(ties),
        out_specs=[vmem, vmem],
        out_shape=[
            jax.ShapeDtypeStruct((COLS, cols), f32),
            jax.ShapeDtypeStruct((COLS, cols), bf16),
        ],
        scratch_shapes=stream_scratch(rows, cols) + [pltpu.VMEM((COLS, rows), bf16)],
        compiler_params=params(),
        cost_estimate=cost(rotated.shape, 256),
        name="returned",
    )(*images, rotated, *before, *ties)


def rotate_out_kernel(n_dp, n_ties, place_ref, query_ref, eigen_ref, *refs):
    refs = refs[n_ties:]
    turned = refs[-1]
    width = eigen_ref.shape[1]
    rows = width // (PIECES * n_dp)
    for side, index in ((0, place_ref[1]), (1, 1 - place_ref[1])):
        queries = query_ref[pl.ds(pl.multiple_of(index * TOKS, TOKS), TOKS), :]
        for begin, count in chunks(width):
            product = jnp.dot(
                queries, eigen_ref[:, begin : begin + count], preferred_element_type=f32
            )
            turned[begin : begin + count, :] = product.T
        for piece in range(PIECES):
            send_ref, keep_ref = refs[2 * (side * PIECES + piece) :][:2]
            for part in range(n_dp):
                at = piece * n_dp + lax.rem(place_ref[0] + 1 + part, n_dp)
                taken = turned[pl.ds(pl.multiple_of(at * rows, rows), rows), :]
                if part < n_dp - 1:
                    send_ref[part * rows : (part + 1) * rows, :] = taken.astype(bf16)
                else:
                    keep_ref[...] = taken.astype(keep_ref.dtype)


def rotate_out(place, query_out, eigen_out, n_dp, ties):
    width = eigen_out.shape[1]
    rows = width // (PIECES * n_dp)
    shapes = []
    for kind in (f32, bf16):
        for _ in range(PIECES):
            shapes.append(jax.ShapeDtypeStruct(((n_dp - 1) * rows, TOKS), bf16))
            shapes.append(jax.ShapeDtypeStruct((rows, TOKS), kind))
    vmem = pl.BlockSpec(memory_space=pltpu.VMEM)
    return pl.pallas_call(
        functools.partial(rotate_out_kernel, n_dp, len(ties)),
        in_specs=[pl.BlockSpec(memory_space=pltpu.SMEM), vmem, vmem] + tied(ties),
        out_specs=[vmem] * len(shapes),
        out_shape=shapes,
        scratch_shapes=[pltpu.VMEM((width, TOKS), f32)],
        compiler_params=params(),
        name="rotate_out",
    )(place, query_out, eigen_out, *ties)


def rotate_in_kernel(place_ref, query_ref, eigen_ref, theirs_ref, mine_ref, product):
    product[...] = jnp.dot(query_ref[...], eigen_ref[...], preferred_element_type=f32)
    for out_ref, index in ((theirs_ref, 1 - place_ref[1]), (mine_ref, place_ref[1])):
        out_ref[...] = product[pl.ds(pl.multiple_of(index * TOKS, TOKS), TOKS), :]


def rotate_in(place, query_in, eigen_in):
    depth, cols = eigen_in.shape
    width = LANES if cols % LANES == 0 else cols
    out = jax.ShapeDtypeStruct((TOKS, cols), f32)
    return pl.pallas_call(
        rotate_in_kernel,
        grid_spec=pltpu.PrefetchScalarGridSpec(
            num_scalar_prefetch=1,
            grid=(cols // width,),
            in_specs=[
                pl.BlockSpec(query_in.shape, lambda at, _: (0, 0)),
                pl.BlockSpec((depth, width), lambda at, _: (0, at)),
            ],
            out_specs=[pl.BlockSpec((TOKS, width), lambda at, _: (0, at))] * 2,
            scratch_shapes=[pltpu.VMEM((CORES * TOKS, width), f32)],
        ),
        out_shape=[out, out],
        compiler_params=params(),
        cost_estimate=pl.CostEstimate(
            flops=2 * depth * cols * CORES * TOKS, bytes_accessed=2 * depth * cols, transcendentals=0
        ),
        name="rotate_in",
    )(place, query_in, eigen_in)


def side_by_side(place_ref, mine, theirs):
    return jnp.where(
        place_ref[1] == 0,
        jnp.concatenate([mine, theirs], axis=1),
        jnp.concatenate([theirs, mine], axis=1),
    )


def factor_kernel(n_ties, place_ref, eigen_ref, mine_ref, theirs_ref, *refs):
    send_ref, keep_ref, cols = refs[n_ties:]
    part, parts = pl.program_id(0), pl.num_programs(0)

    @pl.when(part == 0)
    def _():
        cols[...] = side_by_side(place_ref, mine_ref[...], theirs_ref[...])

    product = jnp.dot(eigen_ref[...], cols[...], preferred_element_type=f32)

    @pl.when(part < parts - 1)
    def _():
        send_ref[...] = product.astype(bf16)

    @pl.when(part == parts - 1)
    def _():
        keep_ref[...] = product


def factor_piece(place, eigen_in, mine, theirs, piece, n_dp, ties):
    rows, depth = eigen_in.shape
    rows = rows // (FACTOR_PIECES * n_dp)
    width = CORES * COLS
    fixed = pl.BlockSpec((depth, COLS), lambda part, _: (0, 0))

    def eigen_block(part, place_ref):
        return piece * n_dp + lax.rem(place_ref[0] + 1 + part, n_dp), 0

    return pl.pallas_call(
        functools.partial(factor_kernel, len(ties)),
        grid_spec=pltpu.PrefetchScalarGridSpec(
            num_scalar_prefetch=1,
            grid=(n_dp,),
            in_specs=[pl.BlockSpec((rows, depth), eigen_block), fixed, fixed] + tied(ties),
            out_specs=[
                pl.BlockSpec((rows, width), lambda part, _: (jnp.minimum(part, n_dp - 2), 0)),
                pl.BlockSpec((rows, width), lambda part, _: (0, 0)),
            ],
            scratch_shapes=[pltpu.VMEM((depth, width), bf16)],
        ),
        out_shape=[
            jax.ShapeDtypeStruct(((n_dp - 1) * rows, width), bf16),
            jax.ShapeDtypeStruct((rows, width), f32),
        ],
        compiler_params=params(),
        name="factor",
    )(place, eigen_in, mine, theirs, *ties)


def write_shares(place_ref, total, keep_ref, send_refs):
    rows = keep_ref.shape[0]
    for step in range(len(send_refs) + 1):
        other = place_ref[2] ^ step
        share = total[pl.ds(pl.multiple_of(other * rows, rows), rows), :]
        if step == 0:
            keep_ref[...] = share
        else:
            send_refs[step - 1][...] = share.astype(bf16)


def factor_out_kernel(n_ties, place_ref, eigen_ref, mine_ref, theirs_ref, *refs):
    keep_ref, *send_refs, total = refs[n_ties:]
    total[...] = jnp.dot(
        eigen_ref[...],
        side_by_side(place_ref, mine_ref[...], theirs_ref[...]),
        preferred_element_type=f32,
    )
    write_shares(place_ref, total, keep_ref, send_refs)


def shares(rows, width, n_width):
    shape = (rows // n_width, width)
    return [jax.ShapeDtypeStruct(shape, f32)] + [jax.ShapeDtypeStruct(shape, bf16)] * (n_width - 1)


def factor_out(place, eigen_out, mine, theirs, n_width, ties):
    rows = eigen_out.shape[0]
    width = CORES * COLS
    vmem = pl.BlockSpec(memory_space=pltpu.VMEM)
    return pl.pallas_call(
        functools.partial(factor_out_kernel, len(ties)),
        in_specs=[pl.BlockSpec(memory_space=pltpu.SMEM)] + [vmem] * 3 + tied(ties),
        out_specs=[vmem] * n_width,
        out_shape=shares(rows, width, n_width),
        scratch_shapes=[pltpu.VMEM((rows, width), f32)],
        compiler_params=params(),
        name="factor_out",
    )(place, eigen_out, mine, theirs, *ties)


def project_kernel(n_dp, n_parts, place_ref, hidden_ref, *refs):
    part_refs = refs[:n_parts]
    factor_ref, keep_ref, *send_refs, total = refs[n_parts:]
    rows = part_refs[0].shape[0]
    for at, ref in enumerate(part_refs):
        owner = lax.rem(place_ref[0] + 1 + at % n_dp, n_dp)
        begin = (at // n_dp * n_dp + owner) * rows
        factor_ref[pl.ds(pl.multiple_of(begin, 8), rows), :] = ref[...]
    total[...] = jnp.dot(hidden_ref[...], factor_ref[...], preferred_element_type=f32)
    write_shares(place_ref, total, keep_ref, send_refs)


def project(place, hidden, parts, n_dp, n_width):
    tokens, depth = hidden.shape
    width = parts[0].shape[1]
    vmem = pl.BlockSpec(memory_space=pltpu.VMEM)
    return pl.pallas_call(
        functools.partial(project_kernel, n_dp, len(parts)),
        in_specs=[pl.BlockSpec(memory_space=pltpu.SMEM)] + [vmem] * (1 + len(parts)),
        out_specs=[vmem] * (1 + n_width),
        out_shape=[jax.ShapeDtypeStruct((depth, width), bf16)] + shares(tokens, width, n_width),
        scratch_shapes=[pltpu.VMEM((tokens, width), f32)],
        compiler_params=params(),
        name="project",
    )(place, hidden, *parts)


def turn_kernel(n_dp, place_ref, inverse_ref, *refs):
    *image_refs, mine_ref, theirs_ref = refs
    rows = image_refs[0].shape[0]
    for at, ref in enumerate(image_refs):
        out_ref = mine_ref if at < PIECES * n_dp else theirs_ref
        owner = lax.rem(place_ref[0] + 1 + at % n_dp, n_dp)
        begin = (at // n_dp % PIECES * n_dp + owner) * rows
        out_ref[pl.ds(pl.multiple_of(begin, rows), rows), :] = lax.dot_general(
            ref[...].astype(f32),
            inverse_ref[...],
            (((1,), (1,)), ((), ())),
            precision=lax.Precision.HIGHEST,
            preferred_element_type=f32,
        ).astype(bf16)


def turn(place, inverse, images, n_dp):
    out = jax.ShapeDtypeStruct((PIECES * n_dp * images[0].shape[0], COLS), bf16)
    vmem = pl.BlockSpec(memory_space=pltpu.VMEM)
    return pl.pallas_call(
        functools.partial(turn_kernel, n_dp),
        in_specs=[pl.BlockSpec(memory_space=pltpu.SMEM)] + [vmem] * (1 + len(images)),
        out_specs=[vmem, vmem],
        out_shape=[out, out],
        compiler_params=params(),
        name="turn",
    )(place, inverse, *images)


def gram_kernel(*refs):
    gram = jnp.zeros((COLS, COLS), f32)
    for ref in refs[:-1]:
        image = ref[...]
        gram = gram + lax.dot_general(
            image, image, (((0,), (0,)), ((), ())), preferred_element_type=f32
        )
    refs[-1][...] = gram


def gram_of(images):
    return pl.pallas_call(
        gram_kernel,
        out_shape=jax.ShapeDtypeStruct((COLS, COLS), f32),
        compiler_params=params(),
        name="gram",
    )(*images)


def lower_inverse(gram):
    shape = (NG, RANK, COLS)
    row = lax.broadcasted_iota(jnp.int32, shape, 1)
    lane = lax.broadcasted_iota(jnp.int32, shape, 2)
    same = lane // RANK == lax.broadcasted_iota(jnp.int32, shape, 0)
    col = lane % RANK
    eye = same & (col == row)
    gram = jnp.where(same, gram.reshape(shape), 0.0)
    trace = jnp.sum(
        jnp.sum(jnp.where(eye, gram, 0.0), axis=2, keepdims=True), axis=1, keepdims=True
    )
    left = gram + jnp.where(eye, ridge_scale * (trace / RANK), 0.0)
    right = jnp.where(eye, 1.0, 0.0)
    for step in range(RANK):
        column = jnp.sum(jnp.where(col == step, left, 0.0), axis=2, keepdims=True)
        pivot = column[:, step : step + 1, :]
        factor = jnp.where(row[:, :, :1] > step, column / pivot, 0.0)
        right = right - factor * right[:, step : step + 1, :]
        left = left - factor * left[:, step : step + 1, :]
    diagonal = jnp.sum(jnp.where(eye, left, 0.0), axis=2, keepdims=True)
    return (right * lax.rsqrt(diagonal)).reshape(COLS, COLS)


def inverse_kernel(scale, gram_ref, gram_got_ref, *refs):
    refs[-1][...] = lower_inverse((gram_ref[...] + gram_got_ref[...]) * scale)


def inverse_of(gram, gram_got, scale, ties):
    vmem = pl.BlockSpec(memory_space=pltpu.VMEM)
    return pl.pallas_call(
        functools.partial(inverse_kernel, scale),
        in_specs=[vmem, vmem] + tied(ties),
        out_specs=vmem,
        out_shape=jax.ShapeDtypeStruct((COLS, COLS), f32),
        compiler_params=params(),
        name="inverse",
    )(gram, gram_got, *ties)


def normalize_kernel(total_ref, got_ref, inverse_ref, *refs):
    basis_ref = refs[-1]
    total = total_ref[...] + got_ref[...].astype(f32)
    basis_ref[...] = lax.dot_general(
        total,
        inverse_ref[...],
        (((0,), (1,)), ((), ())),
        precision=lax.Precision.HIGHEST,
        preferred_element_type=f32,
    ).astype(bf16)


def normalize(total, got, inverse, ties):
    vmem = pl.BlockSpec(memory_space=pltpu.VMEM)
    return pl.pallas_call(
        normalize_kernel,
        in_specs=[vmem] * 3 + tied(ties),
        out_specs=vmem,
        out_shape=jax.ShapeDtypeStruct((total.shape[1], COLS), bf16),
        compiler_params=params(),
        name="normalize",
    )(total, got, inverse, *ties)


def turned_by(count, step):
    return [(i, (i + step) % count) for i in range(count)]


def crossed(count, step):
    return [(i, i ^ step) for i in range(count)]


def swap_cores(part, n_width):
    return lax.ppermute(part, "width", crossed(n_width, 1))


def after(array, others):
    return lax.optimization_barrier((array, *others))[0] if others else array


def hop_kernel(n_got, n_ties, total_ref, *refs):
    total = total_ref[...].astype(f32)
    for ref in refs[:n_got]:
        total = total + ref[...].astype(f32)
    rounded_ref, *total_refs = refs[n_got + n_ties :]
    rounded_ref[...] = total.astype(bf16)
    for ref in total_refs:
        ref[...] = total


def hop_sum(total, got, others, last):
    vmem = pl.BlockSpec(memory_space=pltpu.VMEM)
    shapes = [jax.ShapeDtypeStruct(total.shape, bf16), jax.ShapeDtypeStruct(total.shape, f32)]
    shapes = shapes[:1] if last else shapes
    return pl.pallas_call(
        functools.partial(hop_kernel, len(got), len(others)),
        in_specs=[vmem] * (1 + len(got)) + tied(others),
        out_specs=[vmem] * len(shapes),
        out_shape=shapes,
        compiler_params=params(),
        name="hop",
    )(total, *got, *others)


class Reduction:
    def __init__(self, sends, n_grp, n_dp, even=False, keep=None):
        self.parts = self.own = None
        self.keep = keep
        self.steps = self.run(sends, n_grp, n_dp, even)
        next(self.steps)

    def advance(self, others):
        try:
            return self.steps.send(others)
        except StopIteration:
            return []

    def run(self, sends, n_grp, n_dp, even):
        rows = sends.shape[0] // (n_dp - 1)
        got = [
            lax.ppermute(sends[at * rows : (at + 1) * rows], "dp", turned_by(n_dp, at + 1))
            for at in range(n_dp - 1)
        ]
        others = yield []
        total, step, odd = self.keep, 1, lax.axis_index("grp") % 2
        while True:
            last = step >= n_grp
            if even and step == 2:
                total = after(total, others).astype(f32) + got[0].astype(f32)
                total = lax.dynamic_slice_in_dim(total, odd * (rows // 2), rows // 2, 0)
                own = sent = total = total.astype(bf16)
            else:
                sent, *totals = hop_sum(total, got, others, last or even)
                own, total = sent, totals[0] if totals else sent
            if last:
                break
            got = [lax.ppermute(sent, "grp", crossed(n_grp, step))]
            others = yield [sent]
            step *= 2
        if even and n_grp > 2:
            got = lax.ppermute(own, "grp", crossed(n_grp, 1))
            others = yield [own]
            got = after(got, others)
            own = jnp.where(
                odd == 0, jnp.concatenate([own, got]), jnp.concatenate([got, own])
            )
        self.own = own
        self.parts = [
            lax.ppermute(own, "dp", turned_by(n_dp, n_dp - 1 - at)) for at in range(n_dp - 1)
        ] + [own]
        yield [own]


class Steps:
    def __init__(self, steps):
        self.steps, self.count = steps, 0

    def advance(self, others):
        self.count += 1
        try:
            return self.steps.send(others if self.count > 1 else None)
        except StopIteration:
            return []


def boundary(others, reductions):
    ties = []
    for reduction in reversed(reductions):
        if reduction.parts is None and reduction.keep is not None:
            hop = reduction.advance(others)
            ties = hop + ties
            others = hop or others
    return ties


def sum_shares(keep, sends, n_width):
    total = keep
    for at, send in enumerate(sends):
        total = total + lax.ppermute(send, "width", crossed(n_width, at + 1)).astype(f32)
    return total


def sum_scatter(part, axes, count):
    pieces = lax.all_to_all(part.astype(bf16), axes, 0, 0, tiled=True)
    pieces = pieces.reshape((count, part.shape[0] // count) + part.shape[1:])
    return jnp.sum(pieces.astype(f32), axis=0)


def make_per_device(n_grp, n_dp, n_width):
    n_gd = n_grp * n_dp

    def per_device(
        query_out, query_in, eigen_out, eigen_in, eigvals, start, grads_out, gate_pre, up_pre
    ):
        dp = lax.axis_index("dp")
        along = lax.axis_index("width")
        core = along % CORES
        place = jnp.stack([dp, core, along]).astype(jnp.int32)
        scale = 1.0 / (eigen_out.shape[0] * n_gd)
        rows_out = eigvals.shape[0]

        def last_hop(total, sent=None):
            step = 2
            while True:
                sent = total.astype(bf16) if sent is None else sent
                got = lax.ppermute(sent, "width", crossed(n_width, step))
                step *= 2
                if step >= n_width:
                    return total, sent, got
                total, sent = total + got.astype(f32), None

        def output_side(summing, last):
            gram = gram_of([each.own for each in summing])
            got = [lax.ppermute(gram, "dp", turned_by(n_dp, at)) for at in range(1, n_dp)]
            for each in got:
                gram = gram + each
            step = 2
            while True:
                got = lax.ppermute(gram, "width", crossed(n_width, step))
                step *= 2
                if step >= n_width:
                    break
                gram = gram + got
            others = yield [gram]
            inverse = found["inverse"] = inverse_of(gram, got, scale, others)
            if not last:
                return
            images = [part for each in summing for part in each.parts]
            mine, theirs = turn(place, inverse, images, n_dp)
            theirs = swap_cores(theirs, n_width)
            others = yield [mine]
            keep, *sends = factor_out(place, eigen_out, mine, theirs, n_width, others)
            sends = [
                lax.ppermute(send, "width", crossed(n_width, at + 1))
                for at, send in enumerate(sends)
            ]
            others = yield [keep]
            share = after(keep, others)
            for send in sends:
                share = share + send.astype(f32)
            share = share.astype(bf16)
            piece_rows = share.shape[0]
            copies = jnp.broadcast_to(share[None], (n_gd,) + share.shape)
            gathered = lax.all_to_all(copies, GD, 0, 0, tiled=True)
            gathered = gathered.reshape(n_gd * piece_rows, -1)
            others = yield [copies]
            mixed = lax.all_to_all(after(gathered, others), "width", 0, 0, tiled=True)
            others = yield [gathered]
            out_factor = found["out_factor"] = (
                after(mixed, others)
                .reshape(n_width, n_gd // n_width, piece_rows, NQ * RANK)
                .transpose(1, 0, 2, 3)
                .reshape(rows_out, NQ * RANK)
            )
            proj_out = jnp.dot(grads_out, out_factor, preferred_element_type=f32)
            found["proj_out"] = sum_scatter(proj_out, "width", n_width)

        found = {}
        count = CORES * PIECES
        theirs_in, mine_in = rotate_in(place, query_in, eigen_in)
        pieces = list(rotate_out(place, query_out, eigen_out, n_dp, [mine_in]))
        own_pieces, their_pieces = pieces[: 2 * PIECES], pieces[2 * PIECES :]
        turning = [Reduction(own_pieces[0], n_grp, n_dp, keep=own_pieces[1])]
        theirs_in = swap_cores(theirs_in, n_width)
        their_pieces = [swap_cores(each, n_width) for each in their_pieces]
        hidden = (jax.nn.silu(gate_pre.astype(f32)) * up_pre.astype(f32)).astype(bf16)
        hops = boundary([mine_in], turning)
        total_in, sent_in, got_in = last_hop(after(mine_in, hops) + theirs_in)
        last = [sent_in]
        for at in range(1, count):
            sends, keep = (own_pieces + their_pieces)[2 * at : 2 * at + 2]
            turning.append(Reduction(after(sends, last), n_grp, n_dp, keep=keep))
            if turning[0].parts is None:
                last = boundary(last + [hidden] if at == 2 else last, turning)[:1]
        rot_in = (total_in + got_in.astype(f32)).astype(bf16)
        eig_sent = after(eigvals, [rot_in, *turning[0].parts, *their_pieces])
        eig_theirs = swap_cores(eig_sent, n_width)
        basis = lax.dynamic_slice_in_dim(start, core * COLS, COLS, 1)
        calls = []
        for begin in range(0, count, PIECES):
            span = list(range(begin, begin + PIECES))
            calls += zip([None] + span, span + [None])
        rotated, ties = [None] * len(calls), [hidden]

        def parts_of(reductions, pieces):
            for piece in pieces:
                while piece is not None and reductions[piece].parts is None:
                    boundary([], reductions)
            keep, send = pieces
            return (
                [] if keep is None else reductions[keep].parts[-1:],
                [] if send is None else reductions[send].parts[:-1],
            )

        for iteration in range(ITERS):
            summing = []
            found.clear()
            for at, (keep, send) in enumerate(calls):
                n_keep, n_send = int(keep is not None), (n_dp - 1) * int(send is not None)
                if iteration == 0:
                    ours = (keep if send is None else send) < PIECES
                    rotated[at], *images = form_parts(
                        place,
                        *parts_of(turning, (keep, send)),
                        [0 if each is None else each % PIECES for each in (keep, send)],
                        rot_in,
                        eigvals if ours else eig_theirs,
                        basis,
                        n_dp,
                        ties,
                    )
                else:
                    images = image_parts(basis, rotated[at], n_keep, n_send, ties)
                if n_keep:
                    summing[keep].keep = images[0]
                ties = boundary(images[:1], summing + turning)
                if n_send:
                    summing.append(Reduction(images[-1], n_grp, n_dp))
            total = path = None
            for at, pieces in enumerate(calls):
                kept, sent = parts_of(summing, pieces)
                total, rounded = return_parts(kept + sent, rotated[at], total, ties)
                ties = boundary([rounded], summing)
                if path is None and all(each.own is not None for each in summing):
                    path = Steps(output_side(summing, iteration == ITERS - 1))
                if path is not None and path.count < 4:
                    ties = ties + path.advance([rounded])
            while "inverse" not in found:
                path.advance([])
            total, sent, got = last_hop(total, rounded)
            basis = normalize(total, got, found["inverse"], ties)
            ties = []

        their_basis = swap_cores(basis, n_width)
        factors, last = [], []
        for piece in range(FACTOR_PIECES):
            sends, keep = factor_piece(place, eigen_in, basis, their_basis, piece, n_dp, [])
            if piece:
                last = boundary([keep], factors)
            factors.append(Reduction(sends, n_grp, n_dp, True, keep))
        path.advance(last)
        while any(each.parts is None for each in factors):
            last = boundary(last, factors[::-1])[:1]
        parts = [part for each in factors for part in each.parts]
        in_factor, keep_in, *sends_in = project(place, hidden, parts, n_dp, n_width)
        while "proj_out" not in found:
            path.advance([])
        proj_in = sum_shares(keep_in, sends_in, n_width)
        scores = (found["proj_out"] * proj_in).reshape(proj_in.shape[0], NQ, RANK).sum(axis=2).T
        return (scores, found["out_factor"], in_factor)

    return per_device


def solution(mesh):
    return jax.shard_map(
        make_per_device(mesh.shape["grp"], mesh.shape["dp"], mesh.shape["width"]),
        mesh=mesh,
        in_specs=(
            P(None, GD),
            P(None, "width"),
            P(GD, "width"),
            P("width", GD),
            P("width", GD),
            P(GD, None),
            P(GD, "width"),
            P(GD, "width"),
            P(GD, "width"),
        ),
        out_specs=(P(None, GD + ("width",)), P("width", None), P("width", None)),
        check_vma=False,
    )
```

```python
import functools

import jax
import jax.numpy as jnp
from jax import lax
from jax.experimental import pallas as pl
from jax.experimental.pallas import tpu as pltpu
from jax.sharding import PartitionSpec as P

NQ = 16
QTOK = 32
RANK = 16
ITERS = 2
CORES = 2
NG = NQ // CORES
COLS = NG * RANK
TOKS = NG * QTOK
LANES = 256
PIECES = 2
BLOCK = 4
FACTOR_PIECES = 2

damping = 0.01
ridge_scale = 1e-06

GD = ("grp", "dp")
f32 = jnp.float32
bf16 = jnp.bfloat16


def params():
    return pltpu.CompilerParams(vmem_limit_bytes=48 * 1024 * 1024)


def chunks(extent):
    return [(at, min(LANES, extent - at)) for at in range(0, extent, LANES)]


def cost(shape, columns):
    count = shape[0] * shape[1] * shape[2]
    return pl.CostEstimate(
        flops=2 * count * columns, bytes_accessed=2 * count, transcendentals=0
    )


def tied(ties):
    return [pl.BlockSpec(memory_space=pl.ANY)] * len(ties)


def write_image(image, n_keep, refs):
    part = pl.program_id(0)
    done = pl.program_id(1) == pl.num_programs(1) - 1

    if n_keep:

        @pl.when(done & (part == 0))
        def _():
            refs[0][...] = image[...]

    if len(refs) > n_keep:

        @pl.when(done & (part >= n_keep))
        def _():
            refs[-1][...] = image[...].astype(bf16)


def image_outputs(n_keep, n_send, rows):
    shapes, specs = [], []
    if n_keep:
        shapes.append(jax.ShapeDtypeStruct((rows, COLS), f32))
        specs.append(pl.BlockSpec((rows, COLS), lambda part, query, *_: (0, 0)))
    if n_send:
        shapes.append(jax.ShapeDtypeStruct((n_send * rows, COLS), bf16))
        specs.append(
            pl.BlockSpec(
                (rows, COLS), lambda part, query, *_: (jnp.maximum(part - n_keep, 0), 0)
            )
        )
    return shapes, specs


def add_images(product, first, rows, image):
    lane = lax.broadcasted_iota(jnp.int32, (rows, COLS), 1) // RANK
    for at in range(BLOCK):
        image[...] = jnp.where(
            lane == first + at, product[at * rows : (at + 1) * rows], image[...]
        )


def form_kernel(n_keep, n_parts, n_ties, place_ref, *refs):
    out_refs = refs[:n_parts]
    in_ref, eig_ref, basis_ref = refs[n_parts : n_parts + 3]
    rotated_ref, *image_refs, weight, left, image = refs[n_parts + 3 + n_ties :]
    part, first = pl.program_id(0), pl.program_id(1) * BLOCK
    rows, cols = eig_ref.shape

    @pl.when(first == 0)
    def _():
        weight[...] = 1.0 / (eig_ref[...] + damping)

    for at in range(n_parts):

        @pl.when((first == 0) & (part == at))
        def _(at=at):
            for query in range(NG):
                left[query] = out_refs[at][:, query * QTOK : (query + 1) * QTOK]

    for at in range(BLOCK):
        query = first + at
        own = left[query]
        right = in_ref[pl.ds(pl.multiple_of(query * QTOK, QTOK), QTOK), :]
        for begin, width in chunks(cols):
            span = slice(begin, begin + width)
            block = jnp.dot(own, right[:, span], preferred_element_type=f32)
            rotated_ref[at, :, span] = (block * weight[:, span]).astype(bf16)
    product = jnp.dot(
        rotated_ref[...].reshape(BLOCK * rows, cols), basis_ref[...], preferred_element_type=f32
    )
    add_images(product, first, rows, image)
    write_image(image, n_keep, image_refs)


def form_parts(place, kept, sent, pieces, rot_in, eigvals, basis, n_dp, ties):
    n_keep, n_parts = len(kept), len(kept) + len(sent)
    rows = (kept + sent)[0].shape[0]
    cols = rot_in.shape[1]
    keep_piece, send_piece = pieces

    def eig_block(part, query, place_ref):
        at = send_piece * n_dp + lax.rem(place_ref[0] + 1 + part + n_dp - n_keep, n_dp)
        return jnp.where(part < n_keep, keep_piece * n_dp + place_ref[0], at), 0

    def fixed(shape):
        return pl.BlockSpec(shape, lambda part, query, _: (0, 0))

    shape = (NG, n_parts * rows, cols)
    shapes, specs = image_outputs(n_keep, len(sent), rows)
    return pl.pallas_call(
        functools.partial(form_kernel, n_keep, n_parts, len(ties)),
        grid_spec=pltpu.PrefetchScalarGridSpec(
            num_scalar_prefetch=1,
            grid=(n_parts, NG // BLOCK),
            in_specs=[fixed((rows, TOKS))] * n_parts
            + [
                fixed((TOKS, cols)),
                pl.BlockSpec((rows, cols), eig_block),
                fixed((cols, COLS)),
            ]
            + tied(ties),
            out_specs=[
                pl.BlockSpec((BLOCK, rows, cols), lambda part, query, _: (query, part, 0))
            ]
            + specs,
            scratch_shapes=[
                pltpu.VMEM((rows, cols), f32),
                pltpu.VMEM((NG, rows, QTOK), bf16),
                pltpu.VMEM((rows, COLS), f32),
            ],
        ),
        out_shape=[jax.ShapeDtypeStruct(shape, bf16)] + shapes,
        compiler_params=params(),
        cost_estimate=cost(shape, 400),
        name="form",
    )(place, *kept, *sent, rot_in, eigvals, basis, *ties)


def stream(rotated_ref, buffers, sems, parts, begin, body):
    rows = buffers.shape[1]
    sets = NG // BLOCK

    def copy(turn, slot):
        part, query = turn // sets, lax.rem(turn, sets) * BLOCK + slot
        return pltpu.make_async_copy(
            rotated_ref.at[query, pl.ds(pl.multiple_of(part * rows, rows), rows), :],
            buffers.at[slot],
            sems.at[slot],
        )

    for slot in range(BLOCK):
        copy(0, slot).start()

    @pl.loop(0, parts * sets)
    def _(turn):
        part, first = turn // sets, lax.rem(turn, sets) * BLOCK

        @pl.when(first == 0)
        def _():
            begin(part)

        for slot in range(BLOCK):
            copy(turn, slot).wait()
            body(part, first + slot, buffers[slot])

            @pl.when(turn + 1 < parts * sets)
            def _(slot=slot):
                copy(turn + 1, slot).start()


def stream_scratch(rows, cols):
    return [pltpu.VMEM((BLOCK, rows, cols), bf16), pltpu.SemaphoreType.DMA((BLOCK,))]


def image_kernel(n_keep, n_ties, basis_ref, rotated_ref, *refs):
    *image_refs, image = refs[n_ties:]
    _, rows, cols = rotated_ref.shape
    product = jnp.dot(
        rotated_ref[...].reshape(BLOCK * rows, cols), basis_ref[...], preferred_element_type=f32
    )
    add_images(product, pl.program_id(1) * BLOCK, rows, image)
    write_image(image, n_keep, image_refs)


def image_parts(basis, rotated, n_keep, n_send, ties):
    _, rows, cols = rotated.shape
    rows = rows // (n_keep + n_send)
    shapes, specs = image_outputs(n_keep, n_send, rows)
    return pl.pallas_call(
        functools.partial(image_kernel, n_keep, len(ties)),
        grid=(n_keep + n_send, NG // BLOCK),
        in_specs=[
            pl.BlockSpec((cols, COLS), lambda part, query: (0, 0)),
            pl.BlockSpec((BLOCK, rows, cols), lambda part, query: (query, part, 0)),
        ]
        + tied(ties),
        out_specs=specs,
        out_shape=shapes,
        scratch_shapes=[pltpu.VMEM((rows, COLS), f32)],
        compiler_params=params(),
        cost_estimate=cost(rotated.shape, 256),
        name="image",
    )(basis, rotated, *ties)


def return_kernel(n_parts, first, *refs):
    image_refs, rotated_ref = refs[:n_parts], refs[n_parts]
    total_ref, rounded_ref, buffers, sems, turned = refs[-5:]
    total_ref[...] = jnp.zeros_like(total_ref) if first else refs[n_parts + 1][...]

    def begin(part):
        for at in range(n_parts):

            @pl.when(part == at)
            def _(at=at):
                turned[...] = image_refs[at][...].astype(f32).T.astype(bf16)

    def body(part, query, block):
        own = pl.ds(pl.multiple_of(query * RANK, RANK), RANK)
        total_ref[own, :] += jnp.dot(turned[own, :], block, preferred_element_type=f32)

    stream(rotated_ref, buffers, sems, n_parts, begin, body)
    rounded_ref[...] = total_ref[...].astype(bf16)


def return_parts(images, rotated, before, ties):
    n_parts = len(images)
    _, rows, cols = rotated.shape
    rows = rows // n_parts
    vmem = pl.BlockSpec(memory_space=pltpu.VMEM)
    before = [] if before is None else [before]
    return pl.pallas_call(
        functools.partial(return_kernel, n_parts, not before),
        in_specs=[vmem] * n_parts + tied([rotated]) + [vmem] * len(before) + tied(ties),
        out_specs=[vmem, vmem],
        out_shape=[
            jax.ShapeDtypeStruct((COLS, cols), f32),
            jax.ShapeDtypeStruct((COLS, cols), bf16),
        ],
        scratch_shapes=stream_scratch(rows, cols) + [pltpu.VMEM((COLS, rows), bf16)],
        compiler_params=params(),
        cost_estimate=cost(rotated.shape, 256),
        name="returned",
    )(*images, rotated, *before, *ties)


def rotate_out_kernel(n_dp, n_ties, place_ref, query_ref, eigen_ref, *refs):
    refs = refs[n_ties:]
    turned = refs[-1]
    width = eigen_ref.shape[1]
    rows = width // (PIECES * n_dp)
    for side, index in ((0, place_ref[1]), (1, 1 - place_ref[1])):
        queries = query_ref[pl.ds(pl.multiple_of(index * TOKS, TOKS), TOKS), :]
        for begin, count in chunks(width):
            product = jnp.dot(
                queries, eigen_ref[:, begin : begin + count], preferred_element_type=f32
            )
            turned[begin : begin + count, :] = product.T
        for piece in range(PIECES):
            send_ref, keep_ref = refs[2 * (side * PIECES + piece) :][:2]
            for part in range(n_dp):
                at = piece * n_dp + lax.rem(place_ref[0] + 1 + part, n_dp)
                taken = turned[pl.ds(pl.multiple_of(at * rows, rows), rows), :]
                if part < n_dp - 1:
                    send_ref[part * rows : (part + 1) * rows, :] = taken.astype(bf16)
                else:
                    keep_ref[...] = taken.astype(keep_ref.dtype)


def rotate_out(place, query_out, eigen_out, n_dp, ties):
    width = eigen_out.shape[1]
    rows = width // (PIECES * n_dp)
    shapes = []
    for kind in (f32, bf16):
        for _ in range(PIECES):
            shapes.append(jax.ShapeDtypeStruct(((n_dp - 1) * rows, TOKS), bf16))
            shapes.append(jax.ShapeDtypeStruct((rows, TOKS), kind))
    vmem = pl.BlockSpec(memory_space=pltpu.VMEM)
    return pl.pallas_call(
        functools.partial(rotate_out_kernel, n_dp, len(ties)),
        in_specs=[pl.BlockSpec(memory_space=pltpu.SMEM), vmem, vmem] + tied(ties),
        out_specs=[vmem] * len(shapes),
        out_shape=shapes,
        scratch_shapes=[pltpu.VMEM((width, TOKS), f32)],
        compiler_params=params(),
        name="rotate_out",
    )(place, query_out, eigen_out, *ties)


def rotate_in_kernel(place_ref, query_ref, eigen_ref, theirs_ref, mine_ref, product):
    product[...] = jnp.dot(query_ref[...], eigen_ref[...], preferred_element_type=f32)
    for out_ref, index in ((theirs_ref, 1 - place_ref[1]), (mine_ref, place_ref[1])):
        out_ref[...] = product[pl.ds(pl.multiple_of(index * TOKS, TOKS), TOKS), :]


def rotate_in(place, query_in, eigen_in):
    depth, cols = eigen_in.shape
    width = LANES if cols % LANES == 0 else cols
    out = jax.ShapeDtypeStruct((TOKS, cols), f32)
    return pl.pallas_call(
        rotate_in_kernel,
        grid_spec=pltpu.PrefetchScalarGridSpec(
            num_scalar_prefetch=1,
            grid=(cols // width,),
            in_specs=[
                pl.BlockSpec(query_in.shape, lambda at, _: (0, 0)),
                pl.BlockSpec((depth, width), lambda at, _: (0, at)),
            ],
            out_specs=[pl.BlockSpec((TOKS, width), lambda at, _: (0, at))] * 2,
            scratch_shapes=[pltpu.VMEM((CORES * TOKS, width), f32)],
        ),
        out_shape=[out, out],
        compiler_params=params(),
        cost_estimate=pl.CostEstimate(
            flops=2 * depth * cols * CORES * TOKS, bytes_accessed=2 * depth * cols, transcendentals=0
        ),
        name="rotate_in",
    )(place, query_in, eigen_in)


def side_by_side(place_ref, mine, theirs):
    return jnp.where(
        place_ref[1] == 0,
        jnp.concatenate([mine, theirs], axis=1),
        jnp.concatenate([theirs, mine], axis=1),
    )


def factor_kernel(n_ties, place_ref, eigen_ref, mine_ref, theirs_ref, *refs):
    send_ref, keep_ref, cols = refs[n_ties:]
    part, parts = pl.program_id(0), pl.num_programs(0)

    @pl.when(part == 0)
    def _():
        cols[...] = side_by_side(place_ref, mine_ref[...], theirs_ref[...])

    product = jnp.dot(eigen_ref[...], cols[...], preferred_element_type=f32)

    @pl.when(part < parts - 1)
    def _():
        send_ref[...] = product.astype(bf16)

    @pl.when(part == parts - 1)
    def _():
        keep_ref[...] = product


def factor_piece(place, eigen_in, mine, theirs, piece, n_dp, ties):
    rows, depth = eigen_in.shape
    rows = rows // (FACTOR_PIECES * n_dp)
    width = CORES * COLS
    fixed = pl.BlockSpec((depth, COLS), lambda part, _: (0, 0))

    def eigen_block(part, place_ref):
        return piece * n_dp + lax.rem(place_ref[0] + 1 + part, n_dp), 0

    return pl.pallas_call(
        functools.partial(factor_kernel, len(ties)),
        grid_spec=pltpu.PrefetchScalarGridSpec(
            num_scalar_prefetch=1,
            grid=(n_dp,),
            in_specs=[pl.BlockSpec((rows, depth), eigen_block), fixed, fixed] + tied(ties),
            out_specs=[
                pl.BlockSpec((rows, width), lambda part, _: (jnp.minimum(part, n_dp - 2), 0)),
                pl.BlockSpec((rows, width), lambda part, _: (0, 0)),
            ],
            scratch_shapes=[pltpu.VMEM((depth, width), bf16)],
        ),
        out_shape=[
            jax.ShapeDtypeStruct(((n_dp - 1) * rows, width), bf16),
            jax.ShapeDtypeStruct((rows, width), f32),
        ],
        compiler_params=params(),
        name="factor",
    )(place, eigen_in, mine, theirs, *ties)


def write_shares(place_ref, total, keep_ref, send_refs):
    rows = keep_ref.shape[0]
    for step in range(len(send_refs) + 1):
        other = place_ref[2] ^ step
        share = total[pl.ds(pl.multiple_of(other * rows, rows), rows), :]
        if step == 0:
            keep_ref[...] = share
        else:
            send_refs[step - 1][...] = share.astype(bf16)


def factor_out_kernel(n_ties, place_ref, eigen_ref, mine_ref, theirs_ref, *refs):
    keep_ref, *send_refs, total = refs[n_ties:]
    total[...] = jnp.dot(
        eigen_ref[...],
        side_by_side(place_ref, mine_ref[...], theirs_ref[...]),
        preferred_element_type=f32,
    )
    write_shares(place_ref, total, keep_ref, send_refs)


def shares(rows, width, n_width):
    shape = (rows // n_width, width)
    return [jax.ShapeDtypeStruct(shape, f32)] + [jax.ShapeDtypeStruct(shape, bf16)] * (n_width - 1)


def factor_out(place, eigen_out, mine, theirs, n_width, ties):
    rows = eigen_out.shape[0]
    width = CORES * COLS
    vmem = pl.BlockSpec(memory_space=pltpu.VMEM)
    return pl.pallas_call(
        functools.partial(factor_out_kernel, len(ties)),
        in_specs=[pl.BlockSpec(memory_space=pltpu.SMEM)] + [vmem] * 3 + tied(ties),
        out_specs=[vmem] * n_width,
        out_shape=shares(rows, width, n_width),
        scratch_shapes=[pltpu.VMEM((rows, width), f32)],
        compiler_params=params(),
        name="factor_out",
    )(place, eigen_out, mine, theirs, *ties)


def project_kernel(n_dp, n_parts, place_ref, hidden_ref, *refs):
    part_refs = refs[:n_parts]
    factor_ref, keep_ref, *send_refs, total = refs[n_parts:]
    rows = part_refs[0].shape[0]
    for at, ref in enumerate(part_refs):
        owner = lax.rem(place_ref[0] + 1 + at % n_dp, n_dp)
        begin = (at // n_dp * n_dp + owner) * rows
        factor_ref[pl.ds(pl.multiple_of(begin, 8), rows), :] = ref[...]
    total[...] = jnp.dot(hidden_ref[...], factor_ref[...], preferred_element_type=f32)
    write_shares(place_ref, total, keep_ref, send_refs)


def project(place, hidden, parts, n_dp, n_width):
    tokens, depth = hidden.shape
    width = parts[0].shape[1]
    vmem = pl.BlockSpec(memory_space=pltpu.VMEM)
    return pl.pallas_call(
        functools.partial(project_kernel, n_dp, len(parts)),
        in_specs=[pl.BlockSpec(memory_space=pltpu.SMEM)] + [vmem] * (1 + len(parts)),
        out_specs=[vmem] * (1 + n_width),
        out_shape=[jax.ShapeDtypeStruct((depth, width), bf16)] + shares(tokens, width, n_width),
        scratch_shapes=[pltpu.VMEM((tokens, width), f32)],
        compiler_params=params(),
        name="project",
    )(place, hidden, *parts)


def turn_kernel(n_dp, place_ref, inverse_ref, *refs):
    *image_refs, mine_ref, theirs_ref = refs
    rows = image_refs[0].shape[0]
    for at, ref in enumerate(image_refs):
        out_ref = mine_ref if at < PIECES * n_dp else theirs_ref
        owner = lax.rem(place_ref[0] + 1 + at % n_dp, n_dp)
        begin = (at // n_dp % PIECES * n_dp + owner) * rows
        out_ref[pl.ds(pl.multiple_of(begin, rows), rows), :] = lax.dot_general(
            ref[...].astype(f32),
            inverse_ref[...],
            (((1,), (1,)), ((), ())),
            precision=lax.Precision.HIGHEST,
            preferred_element_type=f32,
        ).astype(bf16)


def turn(place, inverse, images, n_dp):
    out = jax.ShapeDtypeStruct((PIECES * n_dp * images[0].shape[0], COLS), bf16)
    vmem = pl.BlockSpec(memory_space=pltpu.VMEM)
    return pl.pallas_call(
        functools.partial(turn_kernel, n_dp),
        in_specs=[pl.BlockSpec(memory_space=pltpu.SMEM)] + [vmem] * (1 + len(images)),
        out_specs=[vmem, vmem],
        out_shape=[out, out],
        compiler_params=params(),
        name="turn",
    )(place, inverse, *images)


def gram_kernel(*refs):
    gram = jnp.zeros((COLS, COLS), f32)
    for ref in refs[:-1]:
        image = ref[...]
        gram = gram + lax.dot_general(
            image, image, (((0,), (0,)), ((), ())), preferred_element_type=f32
        )
    refs[-1][...] = gram


def gram_of(images):
    return pl.pallas_call(
        gram_kernel,
        out_shape=jax.ShapeDtypeStruct((COLS, COLS), f32),
        compiler_params=params(),
        name="gram",
    )(*images)


def lower_inverse(gram):
    shape = (NG, RANK, COLS)
    row = lax.broadcasted_iota(jnp.int32, shape, 1)
    lane = lax.broadcasted_iota(jnp.int32, shape, 2)
    same = lane // RANK == lax.broadcasted_iota(jnp.int32, shape, 0)
    col = lane % RANK
    eye = same & (col == row)
    gram = jnp.where(same, gram.reshape(shape), 0.0)
    trace = jnp.sum(
        jnp.sum(jnp.where(eye, gram, 0.0), axis=2, keepdims=True), axis=1, keepdims=True
    )
    left = gram + jnp.where(eye, ridge_scale * (trace / RANK), 0.0)
    right = jnp.where(eye, 1.0, 0.0)
    for step in range(RANK):
        column = jnp.sum(jnp.where(col == step, left, 0.0), axis=2, keepdims=True)
        pivot = column[:, step : step + 1, :]
        factor = jnp.where(row[:, :, :1] > step, column / pivot, 0.0)
        right = right - factor * right[:, step : step + 1, :]
        left = left - factor * left[:, step : step + 1, :]
    diagonal = jnp.sum(jnp.where(eye, left, 0.0), axis=2, keepdims=True)
    return (right * lax.rsqrt(diagonal)).reshape(COLS, COLS)


def inverse_kernel(scale, gram_ref, gram_got_ref, *refs):
    refs[-1][...] = lower_inverse((gram_ref[...] + gram_got_ref[...]) * scale)


def inverse_of(gram, gram_got, scale, ties):
    vmem = pl.BlockSpec(memory_space=pltpu.VMEM)
    return pl.pallas_call(
        functools.partial(inverse_kernel, scale),
        in_specs=[vmem, vmem] + tied(ties),
        out_specs=vmem,
        out_shape=jax.ShapeDtypeStruct((COLS, COLS), f32),
        compiler_params=params(),
        name="inverse",
    )(gram, gram_got, *ties)


def normalize_kernel(total_ref, got_ref, inverse_ref, *refs):
    basis_ref = refs[-1]
    total = total_ref[...] + got_ref[...].astype(f32)
    basis_ref[...] = lax.dot_general(
        total,
        inverse_ref[...],
        (((0,), (1,)), ((), ())),
        precision=lax.Precision.HIGHEST,
        preferred_element_type=f32,
    ).astype(bf16)


def normalize(total, got, inverse, ties):
    vmem = pl.BlockSpec(memory_space=pltpu.VMEM)
    return pl.pallas_call(
        normalize_kernel,
        in_specs=[vmem] * 3 + tied(ties),
        out_specs=vmem,
        out_shape=jax.ShapeDtypeStruct((total.shape[1], COLS), bf16),
        compiler_params=params(),
        name="normalize",
    )(total, got, inverse, *ties)


def turned_by(count, step):
    return [(i, (i + step) % count) for i in range(count)]


def crossed(count, step):
    return [(i, i ^ step) for i in range(count)]


def swap_cores(part, n_width):
    return lax.ppermute(part, "width", crossed(n_width, 1))


def after(array, others):
    return lax.optimization_barrier((array, *others))[0] if others else array


def hop_kernel(n_got, n_ties, total_ref, *refs):
    total = total_ref[...].astype(f32)
    for ref in refs[:n_got]:
        total = total + ref[...].astype(f32)
    rounded_ref, *total_refs = refs[n_got + n_ties :]
    rounded_ref[...] = total.astype(bf16)
    for ref in total_refs:
        ref[...] = total


def hop_sum(total, got, others, last):
    vmem = pl.BlockSpec(memory_space=pltpu.VMEM)
    shapes = [jax.ShapeDtypeStruct(total.shape, bf16), jax.ShapeDtypeStruct(total.shape, f32)]
    shapes = shapes[:1] if last else shapes
    return pl.pallas_call(
        functools.partial(hop_kernel, len(got), len(others)),
        in_specs=[vmem] * (1 + len(got)) + tied(others),
        out_specs=[vmem] * len(shapes),
        out_shape=shapes,
        compiler_params=params(),
        name="hop",
    )(total, *got, *others)


class Reduction:
    def __init__(self, sends, n_grp, n_dp, even=False, keep=None):
        self.parts = self.own = None
        self.keep = keep
        self.steps = self.run(sends, n_grp, n_dp, even)
        next(self.steps)

    def advance(self, others):
        try:
            return self.steps.send(others)
        except StopIteration:
            return []

    def run(self, sends, n_grp, n_dp, even):
        rows = sends.shape[0] // (n_dp - 1)
        got = [
            lax.ppermute(sends[at * rows : (at + 1) * rows], "dp", turned_by(n_dp, at + 1))
            for at in range(n_dp - 1)
        ]
        others = yield []
        total, step, odd = self.keep, 1, lax.axis_index("grp") % 2
        while True:
            last = step >= n_grp
            if even and step == 2:
                total = after(total, others).astype(f32) + got[0].astype(f32)
                total = lax.dynamic_slice_in_dim(total, odd * (rows // 2), rows // 2, 0)
                own = sent = total = total.astype(bf16)
            else:
                sent, *totals = hop_sum(total, got, others, last or even)
                own, total = sent, totals[0] if totals else sent
            if last:
                break
            got = [lax.ppermute(sent, "grp", crossed(n_grp, step))]
            others = yield [sent]
            step *= 2
        if even and n_grp > 2:
            got = lax.ppermute(own, "grp", crossed(n_grp, 1))
            others = yield [own]
            got = after(got, others)
            own = jnp.where(
                odd == 0, jnp.concatenate([own, got]), jnp.concatenate([got, own])
            )
        self.own = own
        self.parts = [
            lax.ppermute(own, "dp", turned_by(n_dp, n_dp - 1 - at)) for at in range(n_dp - 1)
        ] + [own]
        yield [own]


class Steps:
    def __init__(self, steps):
        self.steps, self.count = steps, 0

    def advance(self, others):
        self.count += 1
        try:
            return self.steps.send(others if self.count > 1 else None)
        except StopIteration:
            return []


def boundary(others, reductions):
    ties = []
    for reduction in reversed(reductions):
        if reduction.parts is None and reduction.keep is not None:
            hop = reduction.advance(others)
            ties = hop + ties
            others = hop or others
    return ties


def sum_shares(keep, sends, n_width):
    total = keep
    for at, send in enumerate(sends):
        total = total + lax.ppermute(send, "width", crossed(n_width, at + 1)).astype(f32)
    return total


def sum_scatter(part, axes, count):
    pieces = lax.all_to_all(part.astype(bf16), axes, 0, 0, tiled=True)
    pieces = pieces.reshape((count, part.shape[0] // count) + part.shape[1:])
    return jnp.sum(pieces.astype(f32), axis=0)


def make_per_device(n_grp, n_dp, n_width):
    n_gd = n_grp * n_dp

    def per_device(
        query_out, query_in, eigen_out, eigen_in, eigvals, start, grads_out, gate_pre, up_pre
    ):
        dp = lax.axis_index("dp")
        along = lax.axis_index("width")
        core = along % CORES
        place = jnp.stack([dp, core, along]).astype(jnp.int32)
        scale = 1.0 / (eigen_out.shape[0] * n_gd)
        rows_out = eigvals.shape[0]

        def last_hop(total, sent=None):
            step = 2
            while True:
                sent = total.astype(bf16) if sent is None else sent
                got = lax.ppermute(sent, "width", crossed(n_width, step))
                step *= 2
                if step >= n_width:
                    return total, sent, got
                total, sent = total + got.astype(f32), None

        def output_side(summing, last):
            gram = gram_of([each.own for each in summing])
            got = [lax.ppermute(gram, "dp", turned_by(n_dp, at)) for at in range(1, n_dp)]
            for each in got:
                gram = gram + each
            step = 2
            while True:
                got = lax.ppermute(gram, "width", crossed(n_width, step))
                step *= 2
                if step >= n_width:
                    break
                gram = gram + got
            others = yield [gram]
            inverse = found["inverse"] = inverse_of(gram, got, scale, others)
            if not last:
                return
            images = [part for each in summing for part in each.parts]
            mine, theirs = turn(place, inverse, images, n_dp)
            theirs = swap_cores(theirs, n_width)
            others = yield [mine]
            keep, *sends = factor_out(place, eigen_out, mine, theirs, n_width, others)
            sends = [
                lax.ppermute(send, "width", crossed(n_width, at + 1))
                for at, send in enumerate(sends)
            ]
            others = yield [keep]
            share = after(keep, others)
            for send in sends:
                share = share + send.astype(f32)
            share = share.astype(bf16)
            piece_rows = share.shape[0]
            copies = jnp.broadcast_to(share[None], (n_gd,) + share.shape)
            gathered = lax.all_to_all(copies, GD, 0, 0, tiled=True)
            gathered = gathered.reshape(n_gd * piece_rows, -1)
            others = yield [copies]
            mixed = lax.all_to_all(after(gathered, others), "width", 0, 0, tiled=True)
            others = yield [gathered]
            out_factor = found["out_factor"] = (
                after(mixed, others)
                .reshape(n_width, n_gd // n_width, piece_rows, NQ * RANK)
                .transpose(1, 0, 2, 3)
                .reshape(rows_out, NQ * RANK)
            )
            proj_out = jnp.dot(grads_out, out_factor, preferred_element_type=f32)
            found["proj_out"] = sum_scatter(proj_out, "width", n_width)

        found = {}
        count = CORES * PIECES
        theirs_in, mine_in = rotate_in(place, query_in, eigen_in)
        pieces = list(rotate_out(place, query_out, eigen_out, n_dp, [mine_in]))
        own_pieces, their_pieces = pieces[: 2 * PIECES], pieces[2 * PIECES :]
        turning = [Reduction(own_pieces[0], n_grp, n_dp, keep=own_pieces[1])]
        theirs_in = swap_cores(theirs_in, n_width)
        their_pieces = [swap_cores(each, n_width) for each in their_pieces]
        hidden = (jax.nn.silu(gate_pre.astype(f32)) * up_pre.astype(f32)).astype(bf16)
        hops = boundary([mine_in], turning)
        total_in, sent_in, got_in = last_hop(mine_in + theirs_in)
        basis = lax.dynamic_slice_in_dim(start, core * COLS, COLS, 1)
        last = [sent_in, *hops]
        for at in range(1, count):
            sends, keep = (own_pieces + their_pieces)[2 * at : 2 * at + 2]
            turning.append(Reduction(after(sends, last), n_grp, n_dp, keep=keep))
            if turning[0].parts is None:
                last = boundary(last + [hidden, basis] if at == 2 else last, turning)[:1]
        rot_in = (total_in + got_in.astype(f32)).astype(bf16)
        eig_sent = after(eigvals, [rot_in, *turning[0].parts, *their_pieces])
        eig_theirs = swap_cores(eig_sent, n_width)
        calls = []
        for begin in range(0, count, PIECES):
            span = list(range(begin, begin + PIECES))
            calls += zip([None] + span, span + [None])
        rotated, ties = [None] * len(calls), []

        def parts_of(reductions, pieces):
            for piece in pieces:
                while piece is not None and reductions[piece].parts is None:
                    boundary([], reductions)
            keep, send = pieces
            return (
                [] if keep is None else reductions[keep].parts[-1:],
                [] if send is None else reductions[send].parts[:-1],
            )

        for iteration in range(ITERS):
            summing = []
            found.clear()
            for at, (keep, send) in enumerate(calls):
                n_keep, n_send = int(keep is not None), (n_dp - 1) * int(send is not None)
                if iteration == 0:
                    ours = (keep if send is None else send) < PIECES
                    rotated[at], *images = form_parts(
                        place,
                        *parts_of(turning, (keep, send)),
                        [0 if each is None else each % PIECES for each in (keep, send)],
                        rot_in,
                        eigvals if ours else eig_theirs,
                        basis,
                        n_dp,
                        ties,
                    )
                else:
                    images = image_parts(basis, rotated[at], n_keep, n_send, ties)
                if n_keep:
                    summing[keep].keep = images[0]
                ties = boundary(images[:1], summing + turning)
                if n_send:
                    summing.append(Reduction(images[-1], n_grp, n_dp))
            total = path = None
            for at, pieces in enumerate(calls):
                kept, sent = parts_of(summing, pieces)
                total, rounded = return_parts(kept + sent, rotated[at], total, ties)
                ties = boundary([rounded], summing)
                if path is None and all(each.own is not None for each in summing):
                    path = Steps(output_side(summing, iteration == ITERS - 1))
                if path is not None and path.count < 4:
                    ties = ties + path.advance([rounded])
            while "inverse" not in found:
                path.advance([])
            total, sent, got = last_hop(total, rounded)
            basis = normalize(total, got, found["inverse"], ties)
            ties = []

        their_basis = swap_cores(basis, n_width)
        factors, last = [], []
        for piece in range(FACTOR_PIECES):
            sends, keep = factor_piece(place, eigen_in, basis, their_basis, piece, n_dp, [])
            if piece:
                last = boundary([keep], factors)
            factors.append(Reduction(sends, n_grp, n_dp, True, keep))
        path.advance(last)
        while any(each.parts is None for each in factors):
            last = boundary(last, factors[::-1])[:1]
        parts = [part for each in factors for part in each.parts]
        in_factor, keep_in, *sends_in = project(place, hidden, parts, n_dp, n_width)
        while "proj_out" not in found:
            path.advance([])
        proj_in = sum_shares(keep_in, sends_in, n_width)
        scores = (found["proj_out"] * proj_in).reshape(proj_in.shape[0], NQ, RANK).sum(axis=2).T
        return (scores, found["out_factor"], in_factor)

    return per_device


def solution(mesh):
    return jax.shard_map(
        make_per_device(mesh.shape["grp"], mesh.shape["dp"], mesh.shape["width"]),
        mesh=mesh,
        in_specs=(
            P(None, GD),
            P(None, "width"),
            P(GD, "width"),
            P("width", GD),
            P("width", GD),
            P(GD, None),
            P(GD, "width"),
            P(GD, "width"),
            P(GD, "width"),
        ),
        out_specs=(P(None, GD + ("width",)), P("width", None), P("width", None)),
        check_vma=False,
    )
```
